32 devices in a mesh: dp: 8 (over z, core), mp: 4 (over y, x).
Axes of the slice: x: 2, y: 2, z: 4, core: 2. Of those that a mesh axis runs over, the one named last changes fastest.
Arguments:
- inputs: bfloat16 [4096, 2048], P(('dp', 'mp')), may hold values from -6 to 6
- cotangent: bfloat16 [4096, 2048], P(('dp', 'mp')), may hold values from -6 to 6
- segment_ids: int32 [8, 512], P('dp'), may hold values from 0 to 3, never falling along the last dimension, each value on 1 to 170 neighbouring positions
- norm_gain: bfloat16 [2048], replicated, may hold values from 0.099609375 to 1.8984375
- branch_weight: bfloat16 [2048, 2560], P(None, 'mp'), may hold values from -0.125 to 0.125
- stream_weight: bfloat16 [2048, 2560], P(None, 'mp'), may hold values from -0.125 to 0.125
- conv_weight: bfloat16 [4, 2560], P(None, 'mp'), may hold values from -3 to 3
- conv_bias: bfloat16 [2560], P('mp'), may hold values from -3 to 3
- recur_weight: float32 [16, 160, 160], P('mp'), may hold values from -0.5 to 0.5
- recur_bias: float32 [2560], P('mp'), may hold values from -4 to 4
- intake_weight: float32 [16, 160, 160], P('mp'), may hold values from -0.5 to 0.5
- intake_bias: float32 [2560], P('mp'), may hold values from -4 to 4
- decay_param: float32 [2560], P('mp'), may hold values from 2 to 7.5
- output_weight: bfloat16 [2560, 2048], P('mp'), may hold values from -0.3125 to 0.3125
- mlp_gain: bfloat16 [2048], replicated, may hold values from 0.099609375 to 1.8984375
- gate_weight: bfloat16 [2048, 6144], P(None, 'mp'), may hold values from -0.125 to 0.125
- up_weight: bfloat16 [2048, 6144], P(None, 'mp'), may hold values from -0.125 to 0.125
- down_weight: bfloat16 [6144, 2048], P('mp'), may hold values from -0.109375 to 0.109375
Outputs:
- block_out: bfloat16 [4096, 2048], P(('dp', 'mp'))
- inputs_grad: bfloat16 [4096, 2048], P(('dp', 'mp'))
- norm_gain_grad: float32 [2048], replicated
- branch_weight_grad: float32 [2048, 2560], P(None, 'mp')
- stream_weight_grad: float32 [2048, 2560], P(None, 'mp')
- conv_weight_grad: float32 [4, 2560], P(None, 'mp')
- conv_bias_grad: float32 [2560], P('mp')
- recur_weight_grad: float32 [16, 160, 160], P('mp')
- recur_bias_grad: float32 [2560], P('mp')
- intake_weight_grad: float32 [16, 160, 160], P('mp')
- intake_bias_grad: float32 [2560], P('mp')
- decay_param_grad: float32 [2560], P('mp')
- output_weight_grad: float32 [2560, 2048], P('mp')
- mlp_gain_grad: float32 [2048], replicated
- gate_weight_grad: float32 [2048, 6144], P(None, 'mp')
- up_weight_grad: float32 [2048, 6144], P(None, 'mp')
- down_weight_grad: float32 [6144, 2048], P('mp')
The draws below stay inside these ranges and needn't reach their ends.
Inputs may be any that keep to these rules, and one draw needn't show every extreme that they name: `segment_ids`: along each packed row the ids never fall; each id names 1 to 170 consecutive tokens and some segment has exactly that many.
All inputs are finite; a program needn't handle non-finite values.
Results may differ from the reference program's by a relative error of at most 0.019.
Values may be sent and summed in bfloat16 or wider, within the bound.
No kernel may reach another device: no remote copies, remote signals or barrier semaphores. Data moves between devices by JAX's collectives and lax.ppermute only.
A program may use at most 256 MiB of HBM per device.

```python
import math
import jax
import jax.numpy as jnp
import numpy as np
from jax import lax

D = 2048
RNN = 2560
HEADS = 16
FF = 6144
CONV = 4
HS = 160
LENGTH = 512
TOKENS = 4096
N_DP = 8


def steps_of(rng, extent, split, smallest, top_value):
    factor_of = 1.0
    for position, shards_of in split:
        draws = jax.random.uniform(jax.random.fold_in(jax.random.fold_in(rng, 6), position), (shards_of,), jnp.float32, smallest / len(split), top_value / len(split))
        factor_of = factor_of * jnp.repeat(jnp.exp(draws), extent[position] // shards_of).reshape((-1,) + (1,) * (len(extent) - 1 - position))
    return factor_of


def split_up(amount, total, bound, skew):
    weights = [(1 << 20) // math.isqrt(standing ** skew) + 1 for standing in range(2, amount + 1)]
    spare, given = total - bound - (amount - 1), [1] * (amount - 1)
    while spare > 0:
        free = [i for i in range(amount - 1) if given[i] < bound]
        whole, left = sum([weights[i] for i in free]), spare
        for i in free:
            addition = min(bound - given[i], max(1, left * weights[i] // whole), spare)
            given[i] = given[i] + addition
            spare = spare - addition
    return np.array([bound] + given)


def uneven(rng, number_of, total, most, skew):
    if number_of == 2:
        one = jax.random.randint(rng, (), max(1, total - most), min(most, total - 1) + 1)
        return jnp.stack([one, total - one])
    tallies = jnp.asarray(split_up(number_of, total, most, skew), jnp.int32)
    pairs = (number_of - 1) // 2
    source_of, receiver = tallies[1:1 + 2 * pairs:2], tallies[2:2 + 2 * pairs:2]
    slack = jnp.minimum(source_of - 1, most - receiver)
    passed = jax.random.randint(jax.random.fold_in(rng, 1), (pairs,), 0, 1 << 20) % (slack + 1)
    tallies = tallies.at[1:1 + 2 * pairs:2].set(source_of - passed).at[2:2 + 2 * pairs:2].set(receiver + passed)
    return tallies[jax.random.permutation(jax.random.fold_in(rng, 2), number_of)]


def normal_values(key, shape, scale, bound, split=(), kind=jnp.bfloat16):
    values = jax.random.normal(key, shape, jnp.float32) * scale
    if len(split) > 0:
        values = steps_of(key, shape, split, -0.22, 0.18) * values
    return jnp.clip(values, min=-bound, max=bound).astype(kind)


def setup_inputs(seed: int = 0) -> dict:
    streams_of = jax.random.split(jax.random.key(seed), 19)
    return {
        "inputs": normal_values(streams_of[0], (TOKENS, D), 1.0, 6.0, ((0, 32),)),
        "cotangent": normal_values(streams_of[1], (TOKENS, D), 1.0, 6.0, ((0, 32),)),
        "segment_ids": jax.vmap(lambda own: jnp.searchsorted(jnp.cumsum(uneven(own, max(LENGTH // 128, 4), LENGTH, LENGTH // 3, 2)), jnp.arange(LENGTH), side="right"))(jax.random.split(streams_of[2], N_DP)).reshape((N_DP, LENGTH)).astype(jnp.int32),
        "norm_gain": jnp.clip(1.0 + 0.18 * jax.random.normal(streams_of[3], (D,), jnp.float32), 0.099609375, 1.8984375).astype(jnp.bfloat16),
        "branch_weight": normal_values(streams_of[4], (D, RNN), D ** -0.5, 0.125, ((1, 4),)),
        "stream_weight": normal_values(streams_of[5], (D, RNN), D ** -0.5, 0.125, ((1, 4),)),
        "conv_weight": normal_values(streams_of[6], (CONV, RNN), CONV ** -0.5, 3.0, ((1, 4),)),
        "conv_bias": normal_values(streams_of[7], (RNN,), 0.5, 3.0, ((0, 4),)),
        "recur_weight": normal_values(streams_of[8], (HEADS, HS, HS), HS ** -0.5, 0.5, ((0, 4),), jnp.float32),
        "recur_bias": normal_values(streams_of[9], (RNN,), 1.0, 4.0, ((0, 4),), jnp.float32),
        "intake_weight": normal_values(streams_of[10], (HEADS, HS, HS), HS ** -0.5, 0.5, ((0, 4),), jnp.float32),
        "intake_bias": normal_values(streams_of[11], (RNN,), 1.0, 4.0, ((0, 4),), jnp.float32),
        "decay_param": jnp.clip(2.0 + 5.5 * jax.random.uniform(streams_of[12], (RNN,), jnp.float32) ** steps_of(streams_of[12], (RNN,), ((0, 4),), -0.2, 0.2), 2.0, 7.5),
        "output_weight": normal_values(streams_of[13], (RNN, D), (RNN // 8) ** -0.5, 0.3125, ((0, 4),)),
        "mlp_gain": jnp.clip(1.0 + 0.18 * jax.random.normal(streams_of[14], (D,), jnp.float32), 0.099609375, 1.8984375).astype(jnp.bfloat16),
        "gate_weight": normal_values(streams_of[15], (D, FF), D ** -0.5, 0.125, ((1, 4),)),
        "up_weight": normal_values(streams_of[16], (D, FF), D ** -0.5, 0.125, ((1, 4),)),
        "down_weight": normal_values(streams_of[17], (FF, D), (FF // 2) ** -0.5, 0.109375, ((0, 4),)),
    }


eps = 1e-06
decay_scale = 8.0

@jax.custom_vjp
def low(v):
    return lax.optimization_barrier(v.astype(jnp.bfloat16)).astype(jnp.float32)

@jax.custom_vjp
def low_back(v):
    return v

def low_keep(v):
    return (low(v), None)

def low_pass(kept, grad):
    return (grad,)

def back_keep(v):
    return (v, None)

def back_low(kept, grad):
    return (low(grad),)
low.defvjp(low_keep, low_pass)
low_back.defvjp(back_keep, back_low)

def matmul(left, right):
    return jnp.dot(left, right, precision=lax.Precision.HIGHEST, preferred_element_type=jnp.float32)

def rms_scale(values, gain):
    return values * lax.rsqrt(lax.optimization_barrier(jnp.mean(values * values, axis=-1, keepdims=True)) + eps) * gain

def combine(earlier, later):
    return (earlier[0] * later[0], later[0] * earlier[1] + later[1])

def recurrence(stream, seg_row, conv_weight, conv_bias, recur_weight, recur_bias, intake_weight, intake_bias, decay_param):
    length = stream.shape[0]
    channels = stream.shape[1]
    head_count = recur_weight.shape[0]
    head_size = recur_weight.shape[1]
    convolved = conv_bias[None, :] + conv_weight[0][None, :] * stream
    linked = jnp.zeros((length,), jnp.float32)
    for offset in range(1, conv_weight.shape[0]):
        earlier = jnp.concatenate([jnp.full((offset,), -1, jnp.int32), seg_row[:-offset].astype(jnp.int32)])
        joined = (seg_row.astype(jnp.int32) == earlier).astype(jnp.float32)
        if offset == 1:
            linked = joined
        shifted = jnp.concatenate([jnp.zeros((offset, channels), jnp.float32), stream[:-offset]], axis=0)
        convolved = convolved + conv_weight[offset][None, :] * shifted * joined[:, None]
    grouped = convolved.reshape(length, head_count, head_size)
    recur_gate = jax.nn.sigmoid(jnp.einsum('thi,hij->thj', grouped, recur_weight, precision=lax.Precision.HIGHEST).reshape(length, channels) + recur_bias[None, :])
    intake_gate = jax.nn.sigmoid(jnp.einsum('thi,hij->thj', grouped, intake_weight, precision=lax.Precision.HIGHEST).reshape(length, channels) + intake_bias[None, :])
    log_decay = -decay_scale * recur_gate * jax.nn.softplus(-decay_param)[None, :]
    link_col = linked[:, None]
    multiplier = link_col * jnp.sqrt(-jnp.expm1(2.0 * log_decay)) + (1.0 - link_col)
    carried = link_col * jnp.exp(log_decay)
    driven = multiplier * intake_gate * convolved
    products, state = lax.associative_scan(combine, (carried, driven), axis=0)
    return state

def gated_branch(branch_pre, stream_pre, seg_row, small_params):
    return jax.nn.gelu(branch_pre) * recurrence(stream_pre, seg_row, *small_params)

def gated_gelu(gate_pre, up_pre):
    return jax.nn.gelu(gate_pre) * up_pre

def block(resid, seg_row, params):
    norm_gain, branch_weight, stream_weight, conv_weight, conv_bias, recur_weight, recur_bias, intake_weight, intake_bias, decay_param, output_weight, mlp_gain, gate_weight, up_weight, down_weight = params
    normed = low(rms_scale(resid, norm_gain))
    branch_pre = low_back(matmul(normed, branch_weight))
    stream_pre = low_back(matmul(normed, stream_weight))
    small_params = (conv_weight, conv_bias, recur_weight, recur_bias, intake_weight, intake_bias, decay_param)
    gated = low(gated_branch(branch_pre, stream_pre, seg_row, small_params))
    hidden_resid = resid + low_back(matmul(gated, output_weight))
    normed_two = low(rms_scale(hidden_resid, mlp_gain))
    gate_pre = low_back(matmul(normed_two, gate_weight))
    up_pre = low_back(matmul(normed_two, up_weight))
    activ = low(gated_gelu(gate_pre, up_pre))
    return hidden_resid + low_back(matmul(activ, down_weight))

def reference(inputs, cotangent, segment_ids, norm_gain, branch_weight, stream_weight, conv_weight, conv_bias, recur_weight, recur_bias, intake_weight, intake_bias, decay_param, output_weight, mlp_gain, gate_weight, up_weight, down_weight):
    params = tuple((item.astype(jnp.float32) for item in (norm_gain, branch_weight, stream_weight, conv_weight, conv_bias, recur_weight, recur_bias, intake_weight, intake_bias, decay_param, output_weight, mlp_gain, gate_weight, up_weight, down_weight)))
    resid_rows = inputs.astype(jnp.float32).reshape(N_DP, LENGTH, D)
    cot_rows = cotangent.astype(jnp.float32).reshape(N_DP, LENGTH, D)

    def one_row(totals, items):
        resid, cot_row, seg_row = items
        result, back = jax.vjp(lambda values, weights: block(values, seg_row, weights), resid, params)
        resid_grad, param_grads = back(cot_row)
        totals = jax.tree.map(lambda first, second: first + second, totals, param_grads)
        return (totals, (result.astype(jnp.bfloat16), resid_grad.astype(jnp.bfloat16)))
    zeros = jax.tree.map(jnp.zeros_like, params)
    totals, (outputs, grads) = lax.scan(one_row, zeros, (resid_rows, cot_rows, segment_ids.astype(jnp.int32)))
    return (outputs.reshape(TOKENS, D), grads.reshape(TOKENS, D), totals[0], totals[1], totals[2], totals[3], totals[4], totals[5], totals[6], totals[7], totals[8], totals[9], totals[10], totals[11], totals[12], totals[13], totals[14])
```

```python
import functools

import jax
import jax.numpy as jnp
from jax import lax
from jax.experimental import pallas as pl
from jax.experimental.pallas import tpu as pltpu
from jax.sharding import Mesh
from jax.sharding import PartitionSpec as P

eps = 1e-06
decay_scale = 8.0
contract_rows = (((0,), (0,)), ((), ()))
contract_cols = (((1,), (1,)), ((), ()))
f32 = jnp.float32
bf16 = jnp.bfloat16
swap = [(0, 1), (1, 0)]
ALL = ("z", "core", "y", "x")
STEP = 16
root_two_over_pi = 0.7978845608028654


def gather_row(part, square):
    if not square:
        return lax.all_gather(part, ("y", "x"), axis=0, tiled=True)
    half = part.shape[0] // 2
    from_x = lax.ppermute(part, "x", swap)
    from_y = lax.ppermute(part, "y", swap)
    diag_a = lax.ppermute(from_x[:half], "y", swap)
    diag_b = lax.ppermute(from_y[half:], "x", swap)
    return jnp.concatenate([part, from_x, from_y, diag_a, diag_b], axis=0)


def scatter_row(partial, square):
    if not square:
        return lax.psum_scatter(partial, ("y", "x"), scatter_dimension=0, tiled=True).astype(f32)
    rows = partial.shape[0] // 4
    cut = partial.shape[1] // 2
    blocks = [partial[k * rows : (k + 1) * rows] for k in range(4)]
    got_x = lax.ppermute(
        jnp.concatenate([blocks[1][:, :cut], blocks[3][:, :cut]], axis=0), "x", swap
    )
    got_y = lax.ppermute(
        jnp.concatenate([blocks[2][:, cut:], blocks[3][:, cut:]], axis=0), "y", swap
    )
    send_y = (blocks[2][:, :cut].astype(f32) + got_x[rows:].astype(f32)).astype(bf16)
    send_x = (blocks[1][:, cut:].astype(f32) + got_y[rows:].astype(f32)).astype(bf16)
    last_y = lax.ppermute(send_y, "y", swap)
    last_x = lax.ppermute(send_x, "x", swap)
    left = blocks[0][:, :cut].astype(f32) + got_x[:rows].astype(f32) + last_y.astype(f32)
    right = blocks[0][:, cut:].astype(f32) + got_y[:rows].astype(f32) + last_x.astype(f32)
    return jnp.concatenate([left, right], axis=1)


def sibling(value):
    return lax.ppermute(value, "core", swap)


def half_of(value, which, axis):
    size = value.shape[axis] // 2
    return lax.dynamic_slice_in_dim(value, which * size, size, axis=axis)


def join(own, other, core, axis):
    first = jnp.where(core == 0, own, other)
    second = jnp.where(core == 0, other, own)
    return jnp.concatenate([first, second], axis=axis).astype(f32)


def line_sums(pieces, depth):
    if depth != 4:
        return [lax.psum(piece, "z") for piece in pieces]
    place = lax.axis_index("z")
    inner = (place == 1) | (place == 2)
    totals = []
    for piece in pieces:
        kind = piece.dtype
        inward = lax.ppermute(piece, "z", [(0, 1), (3, 2)])
        side = (piece.astype(f32) + inward.astype(f32)).astype(kind)
        across = lax.ppermute(side, "z", [(1, 2), (2, 1)])
        total = (side.astype(f32) + across.astype(f32)).astype(kind)
        outward = lax.ppermute(total, "z", [(1, 0), (2, 3)])
        totals.append(jnp.where(inner, total, outward))
    return totals


def tile_span(first, last, head, width):
    low = (first // head) * head // 128 * 128
    high = min(width, -(-(((last - 1) // head + 1) * head) // 128) * 128)
    return low, high


def tiles(width):
    return [(n, min(n + 256, width)) for n in range(0, width, 256)]


def sigmoid(x):
    return 1.0 / (1.0 + jnp.exp(-x))


def decay_terms(gate, soft, link):
    log_decay = gate * soft
    decay = jnp.exp(log_decay)
    square = decay * decay
    x = 2.0 * log_decay
    series = 1.0 + x * (1.0 / 6.0) * (1.0 + x * (1.0 / 7.0))
    series = 1.0 + x * (1.0 / 4.0) * (1.0 + x * (1.0 / 5.0) * series)
    series = -x * (1.0 + x * (1.0 / 2.0) * (1.0 + x * (1.0 / 3.0) * series))
    gap = jnp.where(x > -0.3, series, 1.0 - square)
    root = jnp.sqrt(gap)
    return link * decay, square, root, link * root + (1.0 - link)


def gelu_terms(x):
    inner = jnp.tanh(root_two_over_pi * (x + 0.044715 * x * x * x))
    value = 0.5 * x * (1.0 + inner)
    slope = 0.5 * (1.0 + inner) + 0.5 * x * (1.0 - inner * inner) * root_two_over_pi * (
        1.0 + 3.0 * 0.044715 * x * x
    )
    return value, slope


def widen(mask, width):
    return jnp.concatenate([mask] * (-(-width // 128)), axis=1)[:, :width]


def forward_kernel(
    spot_ref,
    branch_ref,
    stream_ref,
    joined_ref,
    taps_ref,
    bias_ref,
    high_ref,
    low_ref,
    gate_bias_ref,
    soft_ref,
    gated_ref,
    conv_ref,
    recur_ref,
    intake_ref,
    state_ref,
    part_high,
    part_low,
    *,
    head,
):
    length, width = branch_ref.shape
    block = length // 4
    per_block = block // STEP
    steps = length // STEP
    spot = spot_ref[0]

    def offset(step):
        turn = lax.bitwise_xor(step // per_block, spot)
        return pl.multiple_of(turn * block + lax.rem(step, per_block) * STEP, STEP)

    def convolve(step, before):
        at = offset(step)
        here = pl.multiple_of(step * STEP, STEP)
        now = stream_ref[pl.ds(at, STEP), :]
        both = jnp.concatenate([before, now], axis=0)
        total = bias_ref[0:1, :] + taps_ref[0:1, :] * now
        for k in range(1, 4):
            mask = widen(joined_ref[k - 1, pl.ds(here, STEP), :], width)
            total = total + taps_ref[k : k + 1, :] * both[8 - k : 8 - k + STEP] * mask
        conv_ref[pl.ds(at, STEP), :] = total
        high = total.astype(bf16)
        part_high[pl.ds(here, STEP), :] = high
        part_low[pl.ds(here, STEP), :] = (total - high.astype(f32)).astype(bf16)
        return now[STEP - 8 :]

    lax.fori_loop(0, steps, convolve, jnp.zeros((8, width), f32))

    for which, out_ref in ((0, recur_ref), (1, intake_ref)):
        for first, last in tiles(width):
            low, high = tile_span(first, last, head, width)
            span, cols = slice(low, high), slice(first, last)
            high_part, low_part = high_ref[which, span, cols], low_ref[which, span, cols]
            pre = (
                jnp.dot(part_high[:, span], high_part, preferred_element_type=f32)
                + jnp.dot(part_low[:, span], high_part, preferred_element_type=f32)
                + jnp.dot(part_high[:, span], low_part, preferred_element_type=f32)
            )
            out_ref[:, cols] = pre + gate_bias_ref[which : which + 1, cols]

    rows = lax.broadcasted_iota(jnp.int32, (8, width), 0)
    soft = soft_ref[0:1, :]

    def advance(step, last_state):
        at = offset(step)
        here = pl.multiple_of(step * STEP, STEP)
        link = widen(joined_ref[0, pl.ds(here, STEP), :], width)
        conv = conv_ref[pl.ds(at, STEP), :]
        recur = sigmoid(recur_ref[pl.ds(here, STEP), :])
        intake = sigmoid(intake_ref[pl.ds(here, STEP), :])
        recur_ref[pl.ds(here, STEP), :] = recur
        intake_ref[pl.ds(here, STEP), :] = intake
        carried, square, root, multiplier = decay_terms(recur, soft, link)
        driven = multiplier * intake * conv
        found = []
        for part in range(STEP // 8):
            a = carried[8 * part : 8 * part + 8]
            b = driven[8 * part : 8 * part + 8]
            for shift in (1, 2, 4):
                a_before = jnp.where(rows >= shift, pltpu.roll(a, shift, 0), 1.0)
                b_before = jnp.where(rows >= shift, pltpu.roll(b, shift, 0), 0.0)
                b = b + a * b_before
                a = a * a_before
            state = b + a * last_state
            last_state = state[7:8]
            found.append(state)
        state = jnp.concatenate(found, axis=0)
        state_ref[pl.ds(at, STEP), :] = state
        value, slope = gelu_terms(branch_ref[pl.ds(at, STEP), :])
        gated_ref[pl.ds(at, STEP), :] = (value * state).astype(bf16)
        return last_state

    lax.fori_loop(0, steps, advance, jnp.zeros((1, width), f32))


def backward_kernel(
    spot_ref,
    grad_ref,
    stream_ref,
    joined_ref,
    conv_ref,
    recur_ref,
    intake_ref,
    state_ref,
    taps_ref,
    back_ref,
    soft_ref,
    stream_grad_ref,
    gates_ref,
    sums_ref,
    pre_ref,
    conv_low,
    conv_grad,
    *,
    head,
):
    length, width = grad_ref.shape
    block = length // 4
    per_block = block // STEP
    steps = length // STEP
    spot = spot_ref[0]

    def offset(step):
        turn = lax.bitwise_xor(step // per_block, spot)
        return pl.multiple_of(turn * block + lax.rem(step, per_block) * STEP, STEP)

    rows = lax.broadcasted_iota(jnp.int32, (8, width), 0)
    soft = soft_ref[0:1, :]
    count = STEP // 8

    def fold(value):
        total = value[0:8]
        for part in range(1, count):
            total = total + value[8 * part : 8 * part + 8]
        return total

    def retreat(turn, kept):
        after_carried, after_adjoint, decay_sum, recur_sum, intake_sum = kept
        step = steps - 1 - turn
        at = offset(step)
        at_before = offset(jnp.maximum(step - 1, 0))
        here = pl.multiple_of(step * STEP, STEP)
        link = widen(joined_ref[0, pl.ds(here, STEP), :], width)
        conv = conv_ref[pl.ds(at, STEP), :]
        recur = recur_ref[pl.ds(here, STEP), :]
        intake = intake_ref[pl.ds(here, STEP), :]
        carried, square, root, multiplier = decay_terms(recur, soft, link)
        grad = grad_ref[pl.ds(at, STEP), :]
        found = []
        for part in reversed(range(count)):
            own = carried[8 * part : 8 * part + 8]
            a = jnp.where(rows < 7, pltpu.roll(own, 7, 0), after_carried)
            b = grad[8 * part : 8 * part + 8]
            for shift in (1, 2, 4):
                a_after = jnp.where(rows < 8 - shift, pltpu.roll(a, 8 - shift, 0), 1.0)
                b_after = jnp.where(rows < 8 - shift, pltpu.roll(b, 8 - shift, 0), 0.0)
                b = b + a * b_after
                a = a * a_after
            adjoint = b + a * after_adjoint
            after_adjoint = adjoint[0:1]
            after_carried = own[0:1]
            found.append(adjoint)
        adjoint = jnp.concatenate(found[::-1], axis=0)
        state = state_ref[pl.ds(at, STEP), :]
        tail = state_ref[pl.ds(at_before + (STEP - 8), 8), :]
        earlier = jnp.concatenate([tail, state], axis=0)[7 : 7 + STEP]
        driven_part = adjoint * intake
        log_grad = adjoint * earlier * carried - driven_part * conv * link * square / root
        recur_grad = log_grad * soft * recur * (1.0 - recur)
        spread = driven_part * multiplier
        intake_grad = spread * conv * (1.0 - intake)
        pre_ref[0, pl.ds(here, STEP), :] = recur_grad.astype(bf16)
        pre_ref[1, pl.ds(here, STEP), :] = intake_grad.astype(bf16)
        conv_low[pl.ds(here, STEP), :] = conv.astype(bf16)
        conv_grad[pl.ds(here, STEP), :] = spread
        return (
            after_carried,
            after_adjoint,
            decay_sum + fold(log_grad * recur),
            recur_sum + fold(recur_grad),
            intake_sum + fold(intake_grad),
        )

    line = jnp.zeros((1, width), f32)
    eight = jnp.zeros((8, width), f32)
    kept = lax.fori_loop(0, steps, retreat, (line, line, eight, eight, eight))
    sums_ref[5:6, :] = jnp.sum(kept[3], axis=0, keepdims=True)
    sums_ref[6:7, :] = jnp.sum(kept[4], axis=0, keepdims=True)
    sums_ref[7:8, :] = jnp.sum(kept[2], axis=0, keepdims=True)

    conv_grad[length : length + 8, :] = eight
    for first, last in tiles(width):
        low, high = tile_span(first, last, head, width)
        span, cols = slice(low, high), slice(first, last)
        total = conv_grad[0:length, cols]
        for which in range(2):
            total = total + jnp.dot(
                pre_ref[which, :, span], back_ref[which, span, cols], preferred_element_type=f32
            )
            gates_ref[which, span, cols] = lax.dot_general(
                conv_low[:, span], pre_ref[which, :, cols], contract_rows, preferred_element_type=f32
            )
        conv_grad[0:length, cols] = total

    def unwind(step, kept):
        at = offset(step)
        here = pl.multiple_of(step * STEP, STEP)
        ahead = conv_grad[pl.ds(here, STEP + 8), :]
        now = stream_ref[pl.ds(at, STEP), :]
        total = taps_ref[0:1, :] * ahead[0:STEP]
        sums = [kept[0] + fold(ahead[0:STEP] * now)]
        for k in range(1, 4):
            mask = widen(joined_ref[k - 1, pl.ds(here, STEP + 8), :], width)
            moved = (ahead * mask)[k : k + STEP]
            total = total + taps_ref[k : k + 1, :] * moved
            sums.append(kept[k] + fold(moved * now))
        stream_grad_ref[pl.ds(at, STEP), :] = total.astype(bf16)
        return (*sums, kept[4] + fold(ahead[0:STEP]))

    kept = lax.fori_loop(0, steps, unwind, (eight,) * 5)
    for k in range(5):
        sums_ref[k : k + 1, :] = jnp.sum(kept[k], axis=0, keepdims=True)


def call(body, outs, scratch, args):
    vmem = pl.BlockSpec(memory_space=pltpu.VMEM)
    return pl.pallas_call(
        body,
        out_shape=outs,
        in_specs=[pl.BlockSpec(memory_space=pltpu.SMEM)] + [vmem] * (len(args) - 1),
        out_specs=[vmem] * len(outs),
        scratch_shapes=scratch,
        compiler_params=pltpu.CompilerParams(vmem_limit_bytes=48 * 1024 * 1024),
    )(*args)


def spread_heads(weight):
    count, size = weight.shape[0], weight.shape[1]
    rows = []
    for h in range(count):
        rows.append(jnp.pad(weight[h], ((0, 0), (h * size, (count - 1 - h) * size))))
    return jnp.concatenate(rows, axis=0)


def take_heads(wide, count, size):
    return jnp.stack([wide[h * size : (h + 1) * size, h * size : (h + 1) * size] for h in range(count)])


def local(
    inputs,
    cotangent,
    segment_ids,
    norm_gain,
    branch_weight,
    stream_weight,
    conv_weight,
    conv_bias,
    recur_weight,
    recur_bias,
    intake_weight,
    intake_bias,
    decay_param,
    output_weight,
    mlp_gain,
    gate_weight,
    up_weight,
    down_weight,
    *,
    depth,
    square,
):
    core = lax.axis_index("core")
    spot = jnp.zeros((1,), jnp.int32)
    if square:
        spot = spot + (2 * lax.axis_index("y") + lax.axis_index("x")).astype(jnp.int32)
    heads, head = recur_weight.shape[0], recur_weight.shape[1]
    width = heads * head
    length = segment_ids.shape[1]

    seg_row = segment_ids[0]
    masks = []
    for k in range(1, 4):
        earlier = jnp.concatenate([jnp.full((k,), -1, jnp.int32), seg_row[:-k]])
        masks.append((seg_row == earlier).astype(f32))
    joined = jnp.pad(jnp.stack(masks), ((0, 0), (0, 8)))
    joined = jnp.broadcast_to(joined[:, :, None], (3, length + 8, 128))
    wide = jnp.stack([spread_heads(recur_weight), spread_heads(intake_weight)])
    wide_high = wide.astype(bf16)
    wide_low = (wide - wide_high.astype(f32)).astype(bf16)
    wide_back = jnp.swapaxes(wide_high, 1, 2)
    gate_bias = jnp.stack([recur_bias, intake_bias])
    soft = (-decay_scale * jax.nn.softplus(-decay_param))[None, :]
    taps = conv_weight.astype(f32)

    resid = inputs.astype(f32)
    scale_one = lax.rsqrt(jnp.mean(resid * resid, axis=-1, keepdims=True) + eps)
    gain_one = norm_gain.astype(f32)[None, :]
    normed = gather_row((resid * scale_one * gain_one).astype(bf16), square)
    cot_all = lax.all_gather(cotangent, ALL, axis=0, tiled=True)

    branch_pre = jnp.dot(normed, branch_weight, preferred_element_type=f32)
    stream_pre = jnp.dot(normed, stream_weight, preferred_element_type=f32)
    token = jax.ShapeDtypeStruct((length, width), f32)
    gated, convolved, recur_gate, intake_gate, state = call(
        functools.partial(forward_kernel, head=head),
        [jax.ShapeDtypeStruct((length, width), bf16), token, token, token, token],
        [pltpu.VMEM((length, width), bf16), pltpu.VMEM((length, width), bf16)],
        (
            spot,
            branch_pre,
            stream_pre,
            joined,
            taps,
            conv_bias.astype(f32)[None, :],
            wide_high,
            wide_low,
            gate_bias,
            soft,
        ),
    )
    mixer = scatter_row(jnp.dot(gated, output_weight, preferred_element_type=f32).astype(bf16), square)

    hidden = resid + mixer
    scale_two = lax.rsqrt(jnp.mean(hidden * hidden, axis=-1, keepdims=True) + eps)
    gain_two = mlp_gain.astype(f32)[None, :]
    hat_two = hidden * scale_two
    normed_two = (hat_two * gain_two).astype(bf16)
    mlp_in = gather_row(normed_two, square)
    mlp_all = lax.all_gather(normed_two, ALL, axis=0, tiled=True)
    cot_row = gather_row(cotangent, square)

    def mlp_grads(tokens, cots, gate, up, down):
        gate_pre = jnp.dot(tokens, gate, preferred_element_type=f32)
        up_pre = jnp.dot(tokens, up, preferred_element_type=f32)
        activ_grad = lax.dot_general(cots, down, contract_cols, preferred_element_type=f32)
        value, slope = gelu_terms(gate_pre)
        return (
            (value * up_pre).astype(bf16),
            (activ_grad * up_pre * slope).astype(bf16),
            (activ_grad * value).astype(bf16),
        )

    activ, gate_low, up_low = mlp_grads(mlp_in, cot_row, gate_weight, up_weight, down_weight)
    two_grad = scatter_row(
        (
            lax.dot_general(gate_low, gate_weight, contract_cols, preferred_element_type=f32)
            + lax.dot_general(up_low, up_weight, contract_cols, preferred_element_type=f32)
        ).astype(bf16),
        square,
    )
    mlp_out = scatter_row(jnp.dot(activ, down_weight, preferred_element_type=f32).astype(bf16), square)
    block_out = (hidden + mlp_out).astype(bf16)

    mlp_gain_part = jnp.sum(two_grad * hat_two, axis=0)
    scaled = two_grad * gain_two
    resid_grad = cotangent.astype(f32) + scale_two * (
        scaled - hat_two * jnp.mean(scaled * hat_two, axis=-1, keepdims=True)
    )
    branch_cot = gather_row(resid_grad.astype(bf16), square)

    gated_grad = lax.dot_general(branch_cot, output_weight, contract_cols, preferred_element_type=f32)
    value, slope = gelu_terms(branch_pre)
    state_grad = gated_grad * value
    branch_low = (gated_grad * state * slope).astype(bf16)
    stream_low, wide_grad, sums = call(
        functools.partial(backward_kernel, head=head),
        [
            jax.ShapeDtypeStruct((length, width), bf16),
            jax.ShapeDtypeStruct((2, width, width), f32),
            jax.ShapeDtypeStruct((8, width), f32),
        ],
        [
            pltpu.VMEM((2, length, width), bf16),
            pltpu.VMEM((length, width), bf16),
            pltpu.VMEM((length + 8, width), f32),
        ],
        (
            spot,
            state_grad,
            stream_pre,
            joined,
            convolved,
            recur_gate,
            intake_gate,
            state,
            taps,
            wide_back,
            soft,
        ),
    )
    one_grad = scatter_row(
        (
            lax.dot_general(branch_low, branch_weight, contract_cols, preferred_element_type=f32)
            + lax.dot_general(stream_low, stream_weight, contract_cols, preferred_element_type=f32)
        ).astype(bf16),
        square,
    )
    hat_one = resid * scale_one
    norm_gain_part = jnp.sum(one_grad * hat_one, axis=0)
    scaled = one_grad * gain_one
    inputs_grad = (
        resid_grad
        + scale_one * (scaled - hat_one * jnp.mean(scaled * hat_one, axis=-1, keepdims=True))
    ).astype(bf16)

    def both(value):
        return jnp.concatenate([value, sibling(value)], axis=0)

    def both_halves(value):
        return jnp.concatenate(
            [half_of(value, core, 1), sibling(half_of(value, 1 - core, 1))], axis=0
        )

    normed_half = both_halves(normed)
    output_half = lax.dot_general(
        both(gated), both_halves(branch_cot), contract_rows, preferred_element_type=f32
    ).astype(bf16)
    branch_half = lax.dot_general(
        normed_half, both(branch_low), contract_rows, preferred_element_type=f32
    ).astype(bf16)
    stream_half = lax.dot_general(
        normed_half, both(stream_low), contract_rows, preferred_element_type=f32
    ).astype(bf16)
    recur_part = take_heads(wide_grad[0], heads, head).astype(bf16)
    intake_part = take_heads(wide_grad[1], heads, head).astype(bf16)
    gate_half = (
        jnp.where(core == 0, recur_part, intake_part).astype(f32)
        + sibling(jnp.where(core == 0, intake_part, recur_part)).astype(f32)
    ).astype(bf16)
    gains = jnp.concatenate([norm_gain_part, mlp_gain_part])
    if square:
        gains = gains + lax.ppermute(gains, "x", swap)
        gains = gains + lax.ppermute(gains, "y", swap)
    else:
        gains = lax.psum(gains, ("y", "x"))
    small = jnp.concatenate([sums.reshape(-1), gains]).reshape(-1, 128)
    small = small + sibling(small)
    output_sum, branch_sum, stream_sum, gate_sum, small_sum = line_sums(
        [output_half, branch_half, stream_half, gate_half, small], depth
    )

    gate_part = half_of(gate_weight, core, 1)
    up_part = half_of(up_weight, core, 1)
    down_part = half_of(down_weight, core, 0)
    activ_all, gate_all, up_all = mlp_grads(mlp_all, cot_all, gate_part, up_part, down_part)
    down_half = lax.dot_general(activ_all, cot_all, contract_rows, preferred_element_type=f32).astype(bf16)
    gate_w_half = lax.dot_general(mlp_all, gate_all, contract_rows, preferred_element_type=f32).astype(bf16)
    up_w_half = lax.dot_general(mlp_all, up_all, contract_rows, preferred_element_type=f32).astype(bf16)

    def whole(own, axis):
        return join(own, sibling(own), core, axis)

    gate_other = sibling(gate_sum)
    small_flat = small_sum.reshape(-1)
    sums = small_flat[: 8 * width].reshape(8, width)
    gains = small_flat[8 * width :].reshape(2, -1)
    return (
        block_out,
        inputs_grad,
        gains[0],
        whole(branch_sum, 0),
        whole(stream_sum, 0),
        sums[0:4],
        sums[4],
        jnp.where(core == 0, gate_sum, gate_other).astype(f32),
        sums[5],
        jnp.where(core == 0, gate_other, gate_sum).astype(f32),
        sums[6],
        sums[7] * decay_scale * jax.nn.sigmoid(-decay_param),
        whole(output_sum, 1),
        gains[1],
        whole(gate_w_half, 1),
        whole(up_w_half, 1),
        whole(down_half, 0),
    )


def solution(mesh):
    depth = mesh.shape["dp"] // 2
    across = mesh.shape["mp"] // 2
    fine = Mesh(mesh.devices.reshape(depth, 2, 2, across), ALL)
    dp, mp = ("z", "core"), ("y", "x")
    cols, vec, blocks, rows = P(None, mp), P(mp), P(mp, None, None), P(mp, None)
    tokens = P(ALL, None)
    return jax.shard_map(
        functools.partial(local, depth=depth, square=across == 2),
        mesh=fine,
        in_specs=(
            tokens,
            tokens,
            P(dp, None),
            P(),
            cols,
            cols,
            cols,
            vec,
            blocks,
            vec,
            blocks,
            vec,
            vec,
            rows,
            P(),
            cols,
            cols,
            rows,
        ),
        out_specs=(
            tokens,
            tokens,
            P(),
            cols,
            cols,
            cols,
            vec,
            blocks,
            vec,
            blocks,
            vec,
            vec,
            rows,
            P(),
            cols,
            cols,
            rows,
        ),
        check_vma=False,
    )
```

```python
import functools

import jax
import jax.numpy as jnp
from jax import lax
from jax.experimental import pallas as pl
from jax.experimental.pallas import tpu as pltpu
from jax.sharding import Mesh
from jax.sharding import PartitionSpec as P

eps = 1e-06
decay_scale = 8.0
contract_rows = (((0,), (0,)), ((), ()))
contract_cols = (((1,), (1,)), ((), ()))
f32 = jnp.float32
bf16 = jnp.bfloat16
swap = [(0, 1), (1, 0)]
brief = pl.CostEstimate(flops=1, bytes_accessed=1, transcendentals=0)
large = pltpu.CompilerParams(vmem_limit_bytes=48 * 1024 * 1024)
ALL = ("z", "core", "y", "x")
STEP = 16
root_two_over_pi = 0.7978845608028654


def pass_kernel(*refs):
    pass


def held(values, after):
    values, after = list(values), list(after)
    anywhere = pl.BlockSpec(memory_space=pl.ANY)
    return pl.pallas_call(
        pass_kernel,
        in_specs=[anywhere] * (len(values) + len(after)),
        out_specs=[anywhere] * len(values),
        out_shape=[jax.ShapeDtypeStruct(value.shape, value.dtype) for value in values],
        input_output_aliases={n: n for n in range(len(values))},
        cost_estimate=brief,
    )(*values, *after)


def gather_row(halves, square, beside=()):
    if not square:
        return [lax.all_gather(jnp.concatenate(halves, axis=0), ("y", "x"), axis=0, tiled=True)]
    one, two = halves
    one_x = lax.ppermute(one, "x", swap)
    two_y = lax.ppermute(two, "y", swap)
    two_x = lax.ppermute(two, "x", swap)
    one_y = lax.ppermute(one, "y", swap)
    if beside:
        one_x, two_y = held((one_x, two_y), beside)
    one_d = lax.ppermute(one_x, "y", swap)
    two_d = lax.ppermute(two_y, "x", swap)
    return [one, one_x, one_y, one_d, two, two_x, two_y, two_d]


def scatter_row(sends, square, beside=()):
    if not square:
        return [lax.psum_scatter(sends[0], ("y", "x"), scatter_dimension=0, tiled=True)]
    to_x, to_y, keep_x, keep_y, own = sends
    got_x = lax.ppermute(to_x, "x", swap)
    got_y = lax.ppermute(to_y, "y", swap)
    if beside:
        got_x, got_y = held((got_x, got_y), beside)
    send_y, send_x = pl.pallas_call(
        middle_kernel,
        out_shape=[jax.ShapeDtypeStruct(keep_x.shape, bf16)] * 2,
        cost_estimate=brief,
    )(got_x, got_y, keep_x, keep_y)
    last_y = lax.ppermute(send_y, "y", swap)
    last_x = lax.ppermute(send_x, "x", swap)
    return [own, got_x, got_y, last_y, last_x]


def sibling(value):
    return lax.ppermute(value, "core", swap)


def half_of(value, which, axis):
    size = value.shape[axis] // 2
    return lax.dynamic_slice_in_dim(value, which * size, size, axis=axis)


def join(own, other, core, axis):
    first = jnp.where(core == 0, own, other)
    second = jnp.where(core == 0, other, own)
    return jnp.concatenate([first, second], axis=axis).astype(f32)


def line_sums(groups, beside):
    place = lax.axis_index("z")
    inner = (place == 1) | (place == 2)
    pairs = [[(0, 1), (3, 2)], [(1, 2), (2, 1)], [(1, 0), (2, 3)]]
    groups = [list(group) for group in groups]
    for step in range(len(groups) + 2):
        moves = [(step - stage, stage) for stage in range(3) if 0 <= step - stage < len(groups)]
        got = [lax.ppermute(piece, "z", pairs[stage]) for n, stage in moves for piece in groups[n]]
        if beside[step]:
            got = held(got, beside[step])
        got = list(got)
        for n, stage in moves:
            for k, piece in enumerate(groups[n]):
                other = got.pop(0)
                if stage < 2:
                    groups[n][k] = (piece.astype(f32) + other.astype(f32)).astype(piece.dtype)
                else:
                    groups[n][k] = jnp.where(inner, piece, other)
    return groups


def assemble(pieces, out_ref):
    at = 0
    for piece in pieces:
        out_ref[at : at + piece.shape[0], :] = piece[...]
        at += piece.shape[0]


def send_shapes(length, width, plain):
    if plain:
        return [jax.ShapeDtypeStruct((length, width), bf16)]
    block, cut = length // 4, width // 2
    return (
        [jax.ShapeDtypeStruct((2 * block, cut), bf16)] * 2
        + [jax.ShapeDtypeStruct((block, cut), bf16)] * 2
        + [jax.ShapeDtypeStruct((block, width), f32)]
    )


def emit(value, first, width, sends, plain):
    last = first + value.shape[1]
    if plain:
        sends[0][:, first:last] = value.astype(bf16)
        return
    to_x, to_y, keep_x, keep_y, own = sends
    cut = width // 2
    half = value.shape[0] // 8

    def put(ref, at, block, cols, kind):
        for n in range(2):
            rows = slice(n * 4 * half + block * half, n * 4 * half + (block + 1) * half)
            ref[at + n * half : at + (n + 1) * half, cols] = value[rows].astype(kind)

    put(own, 0, 0, slice(first, last), f32)
    if last <= cut:
        cols = slice(first, last)
        put(to_x, 0, 1, cols, bf16)
        put(to_x, 2 * half, 3, cols, bf16)
        put(keep_y, 0, 2, cols, bf16)
    else:
        cols = slice(first - cut, last - cut)
        put(to_y, 0, 2, cols, bf16)
        put(to_y, 2 * half, 3, cols, bf16)
        put(keep_x, 0, 1, cols, bf16)


def middle_kernel(got_x, got_y, keep_x, keep_y, send_y, send_x):
    block = keep_x.shape[0]
    send_y[...] = (keep_y[...].astype(f32) + got_x[block:].astype(f32)).astype(bf16)
    send_x[...] = (keep_x[...].astype(f32) + got_y[block:].astype(f32)).astype(bf16)


def finish(refs):
    if len(refs) == 1:
        return refs[0][...].astype(f32)
    own, got_x, got_y, last_y, last_x = refs
    block, cut = last_y.shape
    left = own[:, :cut] + got_x[:block].astype(f32) + last_y[...].astype(f32)
    right = own[:, cut:] + got_y[:block].astype(f32) + last_x[...].astype(f32)
    return jnp.concatenate([left, right], axis=1)


def mean_of(x):
    return jnp.mean(x, axis=-1, keepdims=True)


def norm_kernel(input_ref, gain_ref, one_ref, two_ref):
    values = input_ref[...].astype(f32)
    normed = (values * lax.rsqrt(mean_of(values * values) + eps) * gain_ref[...]).astype(bf16)
    half = normed.shape[0] // 2
    one_ref[...] = normed[:half]
    two_ref[...] = normed[half:]


def second_norm_kernel(input_ref, gain_ref, *refs, cuts):
    hidden_ref, one_ref, two_ref, *parts = refs[-3 - len(cuts) + 1 :]
    addends = refs[: -3 - len(cuts) + 1]
    hidden = input_ref[...].astype(f32) + finish(addends)
    hidden_ref[...] = hidden
    normed = (hidden * lax.rsqrt(mean_of(hidden * hidden) + eps) * gain_ref[...]).astype(bf16)
    half = normed.shape[0] // 2
    one_ref[...] = normed[:half]
    two_ref[...] = normed[half:]
    for ref, first, last in zip(parts, cuts[:-1], cuts[1:], strict=True):
        ref[...] = normed[first:last]


def norm_back_kernel(value_ref, before_ref, gain_ref, *refs, final):
    outs = 2 if final else 4
    addends, outs = refs[:-outs], refs[-outs:]
    values = value_ref[...].astype(f32)
    scale = lax.rsqrt(mean_of(values * values) + eps)
    hat = values * scale
    grad = finish(addends)
    outs[0][...] = jnp.sum(grad * hat, axis=0, keepdims=True)
    scaled = grad * gain_ref[...]
    total = before_ref[...].astype(f32) + scale * (scaled - hat * mean_of(scaled * hat))
    if final:
        outs[1][...] = total.astype(bf16)
        return
    outs[1][...] = total
    low = total.astype(bf16)
    half = low.shape[0] // 2
    outs[2][...] = low[:half]
    outs[3][...] = low[half:]


def add_kernel(value_ref, *refs):
    refs[-1][...] = (value_ref[...] + finish(refs[:-1])).astype(bf16)


def mlp_kernel(*refs, count, plain, keep):
    pieces, (grad_ref, gate_w, up_w), refs = refs[:count], refs[count : count + 3], refs[count + 3 :]
    *outs, token_ref, total_ref = refs
    token_out, activ_ref, *outs = outs
    step = pl.program_id(0)

    @pl.when(step == 0)
    def _():
        assemble(pieces, token_ref)
        token_out[...] = token_ref[...]

    tokens = token_ref[...]
    gate_pre = jnp.dot(tokens, gate_w[...], preferred_element_type=f32)
    up_pre = jnp.dot(tokens, up_w[...], preferred_element_type=f32)
    activ_grad = grad_ref[...]
    value, slope = gelu_terms(gate_pre)
    activ_ref[...] = (value * up_pre).astype(bf16)
    gate_low = (activ_grad * up_pre * slope).astype(bf16)
    up_low = (activ_grad * value).astype(bf16)
    if keep:
        outs[0][...] = gate_low
        outs[1][...] = up_low
        outs = outs[2:]
    width = total_ref.shape[1]
    last = step == pl.num_programs(0) - 1
    for first in range(0, width, 512):
        cols = slice(first, first + 512)
        part = lax.dot_general(
            gate_low, gate_w[cols, :], contract_cols, preferred_element_type=f32
        ) + lax.dot_general(up_low, up_w[cols, :], contract_cols, preferred_element_type=f32)

        @pl.when(step == 0)
        def _(part=part, cols=cols):
            total_ref[:, cols] = part

        @pl.when(step > 0)
        def _(part=part, cols=cols):
            total_ref[:, cols] += part

    @pl.when(last)
    def _():
        for first in range(0, width, 512):
            emit(total_ref[:, first : first + 512], first, width, outs, plain)


def down_kernel(activ_ref, weight_ref, *sends, plain):
    width = weight_ref.shape[1]
    for first in range(0, width, 512):
        cols = slice(first, first + 512)
        value = jnp.dot(activ_ref[...], weight_ref[:, cols], preferred_element_type=f32)
        emit(value, first, width, sends, plain)


def tile_span(first, last, head, width):
    low = (first // head) * head // 128 * 128
    high = min(width, -(-(((last - 1) // head + 1) * head) // 128) * 128)
    return low, high


def tiles(width):
    return [(n, min(n + 256, width)) for n in range(0, width, 256)]


def sigmoid(x):
    return 1.0 / (1.0 + jnp.exp(-x))


def decay_terms(gate, soft, link):
    log_decay = gate * soft
    decay = jnp.exp(log_decay)
    square = decay * decay
    x = 2.0 * log_decay
    series = 1.0 + x * (1.0 / 6.0) * (1.0 + x * (1.0 / 7.0))
    series = 1.0 + x * (1.0 / 4.0) * (1.0 + x * (1.0 / 5.0) * series)
    series = -x * (1.0 + x * (1.0 / 2.0) * (1.0 + x * (1.0 / 3.0) * series))
    gap = jnp.where(x > -0.3, series, 1.0 - square)
    root = jnp.sqrt(gap)
    return link * decay, square, root, link * root + (1.0 - link)


def gelu_terms(x):
    inner = jnp.tanh(root_two_over_pi * (x + 0.044715 * x * x * x))
    value = 0.5 * x * (1.0 + inner)
    slope = 0.5 * (1.0 + inner) + 0.5 * x * (1.0 - inner * inner) * root_two_over_pi * (
        1.0 + 3.0 * 0.044715 * x * x
    )
    return value, slope


def widen(mask, width):
    return jnp.concatenate([mask] * (-(-width // 128)), axis=1)[:, :width]


def token_place(length, spot, plain):
    block, half = length // 4, length // 8
    per_block = block // STEP
    per_half = half // STEP

    def offset(step):
        if plain:
            return pl.multiple_of(step * STEP, STEP)
        turn = lax.bitwise_xor(step // per_block, spot)
        inside = lax.rem(step, per_block)
        at = (inside // per_half) * (length // 2) + turn * half + lax.rem(inside, per_half) * STEP
        return pl.multiple_of(at, STEP)

    return offset


def prep_kernel(recur_ref, intake_ref, high_ref, low_ref):
    count, size, _ = recur_ref.shape
    for which, ref in ((0, recur_ref), (1, intake_ref)):
        for h in range(count):
            parts = [ref[h]]
            if h:
                parts.insert(0, jnp.zeros((size, h * size), f32))
            if h < count - 1:
                parts.append(jnp.zeros((size, (count - 1 - h) * size), f32))
            row = jnp.concatenate(parts, axis=1)
            high = row.astype(bf16)
            rows = slice(h * size, (h + 1) * size)
            high_ref[which, rows, :] = high
            low_ref[which, rows, :] = (row - high.astype(f32)).astype(bf16)


def forward_kernel(spot_ref, *refs, count, head, plain):
    pieces, refs = refs[:count], refs[count:]
    (branch_w, stream_w, output_w, joined_ref, taps_ref, bias_ref, high_ref, low_ref, gate_bias_ref, soft_ref), refs = (
        refs[:10],
        refs[10:],
    )
    (normed_ref, branch_ref, stream_ref, gated_ref, conv_ref, recur_ref, intake_ref, state_ref), refs = (
        refs[:8],
        refs[8:],
    )
    *sends, part_high, part_low = refs
    assemble(pieces, normed_ref)
    for first, last in tiles(branch_ref.shape[1]):
        cols = slice(first, last)
        branch_ref[:, cols] = jnp.dot(normed_ref[...], branch_w[:, cols], preferred_element_type=f32)
        stream_ref[:, cols] = jnp.dot(normed_ref[...], stream_w[:, cols], preferred_element_type=f32)
    length, width = branch_ref.shape
    steps = length // STEP
    offset = token_place(length, spot_ref[0], plain)

    def convolve(step, before):
        at = offset(step)
        here = pl.multiple_of(step * STEP, STEP)
        now = stream_ref[pl.ds(at, STEP), :]
        both = jnp.concatenate([before, now], axis=0)
        total = bias_ref[0:1, :] + taps_ref[0:1, :] * now
        for k in range(1, 4):
            mask = widen(joined_ref[k - 1, pl.ds(here, STEP), :], width)
            total = total + taps_ref[k : k + 1, :] * both[8 - k : 8 - k + STEP] * mask
        conv_ref[pl.ds(at, STEP), :] = total
        high = total.astype(bf16)
        part_high[pl.ds(here, STEP), :] = high
        part_low[pl.ds(here, STEP), :] = (total - high.astype(f32)).astype(bf16)
        return now[STEP - 8 :]

    lax.fori_loop(0, steps, convolve, jnp.zeros((8, width), f32))

    for which, out_ref in ((0, recur_ref), (1, intake_ref)):
        for first, last in tiles(width):
            low, high = tile_span(first, last, head, width)
            span, cols = slice(low, high), slice(first, last)
            high_part, low_part = high_ref[which, span, cols], low_ref[which, span, cols]
            pre = (
                jnp.dot(part_high[:, span], high_part, preferred_element_type=f32)
                + jnp.dot(part_low[:, span], high_part, preferred_element_type=f32)
                + jnp.dot(part_high[:, span], low_part, preferred_element_type=f32)
            )
            out_ref[:, cols] = pre + gate_bias_ref[which : which + 1, cols]

    rows = lax.broadcasted_iota(jnp.int32, (8, width), 0)
    soft = soft_ref[0:1, :]

    def advance(step, last_state):
        at = offset(step)
        here = pl.multiple_of(step * STEP, STEP)
        link = widen(joined_ref[0, pl.ds(here, STEP), :], width)
        conv = conv_ref[pl.ds(at, STEP), :]
        recur = sigmoid(recur_ref[pl.ds(here, STEP), :])
        intake = sigmoid(intake_ref[pl.ds(here, STEP), :])
        recur_ref[pl.ds(here, STEP), :] = recur
        intake_ref[pl.ds(here, STEP), :] = intake
        carried, square, root, multiplier = decay_terms(recur, soft, link)
        driven = multiplier * intake * conv
        found = []
        for part in range(STEP // 8):
            a = carried[8 * part : 8 * part + 8]
            b = driven[8 * part : 8 * part + 8]
            for shift in (1, 2, 4):
                a_before = jnp.where(rows >= shift, pltpu.roll(a, shift, 0), 1.0)
                b_before = jnp.where(rows >= shift, pltpu.roll(b, shift, 0), 0.0)
                b = b + a * b_before
                a = a * a_before
            state = b + a * last_state
            last_state = state[7:8]
            found.append(state)
        state = jnp.concatenate(found, axis=0)
        state_ref[pl.ds(at, STEP), :] = state
        value, slope = gelu_terms(branch_ref[pl.ds(at, STEP), :])
        gated_ref[pl.ds(at, STEP), :] = (value * state).astype(bf16)
        return last_state

    lax.fori_loop(0, steps, advance, jnp.zeros((1, width), f32))
    step_cols = 512
    for first in range(0, output_w.shape[1], step_cols):
        cols = slice(first, first + step_cols)
        value = jnp.dot(gated_ref[...], output_w[:, cols], preferred_element_type=f32)
        emit(value, first, output_w.shape[1], sends, plain)


def backward_kernel(spot_ref, *refs, count, head, plain):
    pieces, refs = refs[:count], refs[count:]
    (
        output_w,
        branch_w,
        stream_w,
        branch_ref,
        stream_ref,
        joined_ref,
        conv_ref,
        recur_ref,
        intake_ref,
        state_ref,
        taps_ref,
        high_ref,
        soft_ref,
    ), refs = refs[:13], refs[13:]
    (cot_ref, branch_grad_ref, stream_grad_ref, gates_ref, sums_ref), refs = refs[:5], refs[5:]
    *sends, grad_ref, pre_ref, conv_low, conv_grad = refs
    assemble(pieces, cot_ref)
    for first, last in tiles(branch_ref.shape[1]):
        cols = slice(first, last)
        grad_ref[:, cols] = lax.dot_general(
            cot_ref[...], output_w[cols, :], contract_cols, preferred_element_type=f32
        )
    length, width = grad_ref.shape
    steps = length // STEP
    offset = token_place(length, spot_ref[0], plain)

    rows = lax.broadcasted_iota(jnp.int32, (8, width), 0)
    soft = soft_ref[0:1, :]
    count = STEP // 8

    def fold(value):
        total = value[0:8]
        for part in range(1, count):
            total = total + value[8 * part : 8 * part + 8]
        return total

    def retreat(turn, kept):
        after_carried, after_adjoint, decay_sum, recur_sum, intake_sum = kept
        step = steps - 1 - turn
        at = offset(step)
        at_before = offset(jnp.maximum(step - 1, 0))
        here = pl.multiple_of(step * STEP, STEP)
        link = widen(joined_ref[0, pl.ds(here, STEP), :], width)
        conv = conv_ref[pl.ds(at, STEP), :]
        recur = recur_ref[pl.ds(here, STEP), :]
        intake = intake_ref[pl.ds(here, STEP), :]
        carried, square, root, multiplier = decay_terms(recur, soft, link)
        value, slope = gelu_terms(branch_ref[pl.ds(at, STEP), :])
        gated_grad = grad_ref[pl.ds(at, STEP), :]
        grad = gated_grad * value
        found = []
        for part in reversed(range(count)):
            own = carried[8 * part : 8 * part + 8]
            a = jnp.where(rows < 7, pltpu.roll(own, 7, 0), after_carried)
            b = grad[8 * part : 8 * part + 8]
            for shift in (1, 2, 4):
                a_after = jnp.where(rows < 8 - shift, pltpu.roll(a, 8 - shift, 0), 1.0)
                b_after = jnp.where(rows < 8 - shift, pltpu.roll(b, 8 - shift, 0), 0.0)
                b = b + a * b_after
                a = a * a_after
            adjoint = b + a * after_adjoint
            after_adjoint = adjoint[0:1]
            after_carried = own[0:1]
            found.append(adjoint)
        adjoint = jnp.concatenate(found[::-1], axis=0)
        state = state_ref[pl.ds(at, STEP), :]
        branch_grad_ref[pl.ds(at, STEP), :] = (gated_grad * state * slope).astype(bf16)
        tail = state_ref[pl.ds(at_before + (STEP - 8), 8), :]
        earlier = jnp.concatenate([tail, state], axis=0)[7 : 7 + STEP]
        driven_part = adjoint * intake
        log_grad = adjoint * earlier * carried - driven_part * conv * link * square / root
        recur_grad = log_grad * soft * recur * (1.0 - recur)
        spread = driven_part * multiplier
        intake_grad = spread * conv * (1.0 - intake)
        pre_ref[0, pl.ds(here, STEP), :] = recur_grad.astype(bf16)
        pre_ref[1, pl.ds(here, STEP), :] = intake_grad.astype(bf16)
        conv_low[pl.ds(here, STEP), :] = conv.astype(bf16)
        conv_grad[pl.ds(here, STEP), :] = spread
        return (
            after_carried,
            after_adjoint,
            decay_sum + fold(log_grad * recur),
            recur_sum + fold(recur_grad),
            intake_sum + fold(intake_grad),
        )

    line = jnp.zeros((1, width), f32)
    eight = jnp.zeros((8, width), f32)
    kept = lax.fori_loop(0, steps, retreat, (line, line, eight, eight, eight))
    sums_ref[5:6, :] = jnp.sum(kept[3], axis=0, keepdims=True)
    sums_ref[6:7, :] = jnp.sum(kept[4], axis=0, keepdims=True)
    sums_ref[7:8, :] = jnp.sum(kept[2], axis=0, keepdims=True)

    conv_grad[length : length + 8, :] = eight
    for first, last in tiles(width):
        low, high = tile_span(first, last, head, width)
        span, cols = slice(low, high), slice(first, last)
        total = conv_grad[0:length, cols]
        for which in range(2):
            total = total + lax.dot_general(
                pre_ref[which, :, span], high_ref[which, cols, span], contract_cols, preferred_element_type=f32
            )
            gates_ref[which, span, cols] = lax.dot_general(
                conv_low[:, span], pre_ref[which, :, cols], contract_rows, preferred_element_type=f32
            )
        conv_grad[0:length, cols] = total

    def unwind(step, kept):
        at = offset(step)
        here = pl.multiple_of(step * STEP, STEP)
        ahead = conv_grad[pl.ds(here, STEP + 8), :]
        now = stream_ref[pl.ds(at, STEP), :]
        total = taps_ref[0:1, :] * ahead[0:STEP]
        sums = [kept[0] + fold(ahead[0:STEP] * now)]
        for k in range(1, 4):
            mask = widen(joined_ref[k - 1, pl.ds(here, STEP + 8), :], width)
            moved = (ahead * mask)[k : k + STEP]
            total = total + taps_ref[k : k + 1, :] * moved
            sums.append(kept[k] + fold(moved * now))
        stream_grad_ref[pl.ds(at, STEP), :] = total.astype(bf16)
        return (*sums, kept[4] + fold(ahead[0:STEP]))

    kept = lax.fori_loop(0, steps, unwind, (eight,) * 5)
    for k in range(5):
        sums_ref[k : k + 1, :] = jnp.sum(kept[k], axis=0, keepdims=True)
    step_cols = 512
    for first in range(0, branch_w.shape[0], step_cols):
        cols = slice(first, first + step_cols)
        value = lax.dot_general(
            branch_grad_ref[...], branch_w[cols, :], contract_cols, preferred_element_type=f32
        ) + lax.dot_general(
            stream_grad_ref[...], stream_w[cols, :], contract_cols, preferred_element_type=f32
        )
        emit(value, first, branch_w.shape[0], sends, plain)


def rows_kernel(core_ref, token_ref, cot_ref, gate_ref, up_ref, down_ref, *rest):
    activ_ref, gate_out, up_out = rest[-3:]
    tokens, cots = token_ref[...], cot_ref[...]
    hidden = gate_ref.shape[0]
    part = hidden // 3
    for n in range(3):
        rows = slice(n * part, (n + 1) * part)
        gate_pre = lax.dot_general(gate_ref[rows], tokens, contract_cols, preferred_element_type=f32)
        up_pre = lax.dot_general(up_ref[rows], tokens, contract_cols, preferred_element_type=f32)
        activ_grad = lax.dot_general(down_ref[rows], cots, contract_cols, preferred_element_type=f32)
        value, slope = gelu_terms(gate_pre)
        activ_ref[rows] = (value * up_pre).astype(bf16)
        gate_out[rows] = (activ_grad * up_pre * slope).astype(bf16)
        up_out[rows] = (activ_grad * value).astype(bf16)


def mlp_rows(core, tokens, cots, gate, up, down, after):
    count, width = tokens.shape
    hidden = gate.shape[0]
    tile = 256
    rows = pl.BlockSpec((tile, width), lambda i, core: (i, 0))
    tall = pl.BlockSpec((hidden, tile), lambda i, core: (0, i))
    weight = pl.BlockSpec((hidden, width), lambda i, core: (0, 0))
    return pl.pallas_call(
        rows_kernel,
        grid_spec=pltpu.PrefetchScalarGridSpec(
            num_scalar_prefetch=1,
            grid=(count // tile,),
            in_specs=[rows, rows, weight, weight]
            + [pl.BlockSpec((hidden, width), lambda i, core: (core[0], 0))]
            + [pl.BlockSpec(memory_space=pl.ANY)] * len(after),
            out_specs=[tall, tall, tall],
        ),
        out_shape=[jax.ShapeDtypeStruct((hidden, count), bf16)] * 3,
        cost_estimate=brief,
        compiler_params=large,
    )(core, tokens, cots, gate, up, down, *after)


def product(left, right, added=(), after=()):
    rows, depth = left.shape
    cols = right.shape[1]
    kind = bf16 if added else f32

    def body(left_ref, right_ref, *rest):
        total = jnp.dot(left_ref[...], right_ref[...], preferred_element_type=f32)
        if added:
            total = total + rest[0][...]
        rest[-1][...] = total.astype(kind)

    column = pl.BlockSpec((rows, 256), lambda n: (0, n))
    return pl.pallas_call(
        body,
        grid=(cols // 256,),
        in_specs=[
            pl.BlockSpec((rows, depth), lambda n: (0, 0)),
            pl.BlockSpec((depth, 256), lambda n: (0, n)),
        ]
        + [column] * len(added)
        + [pl.BlockSpec(memory_space=pl.ANY)] * len(after),
        out_specs=column,
        out_shape=jax.ShapeDtypeStruct((rows, cols), kind),
        cost_estimate=brief,
        compiler_params=pltpu.CompilerParams(vmem_limit_bytes=48 * 1024 * 1024),
    )(left, right, *added, *after)


def flip_kernel(core_ref, one_ref, two_ref, *rest):
    rest[-2][...] = one_ref[...].astype(f32).T.astype(bf16)
    rest[-1][...] = two_ref[...].astype(f32).T.astype(bf16)


def flipped(one, two, core, after):
    width, hidden = one.shape[0], one.shape[1] // 2
    tile = 256
    source = pl.BlockSpec((tile, hidden), lambda n, core: (n, core[0]))
    result = pl.BlockSpec((hidden, tile), lambda n, core: (0, n))
    return pl.pallas_call(
        flip_kernel,
        grid_spec=pltpu.PrefetchScalarGridSpec(
            num_scalar_prefetch=1,
            grid=(width // tile,),
            in_specs=[source, source] + [pl.BlockSpec(memory_space=pl.ANY)] * len(after),
            out_specs=[result, result],
        ),
        out_shape=[jax.ShapeDtypeStruct((hidden, width), bf16)] * 2,
        cost_estimate=brief,
    )(core.astype(jnp.int32).reshape((1,)), one, two, *after)


def turn_kernel(core_ref, own_ref, other_ref, out_ref):
    mine = pl.program_id(0) == core_ref[0]

    @pl.when(mine)
    def _():
        out_ref[...] = own_ref[...].astype(f32).T

    @pl.when(jnp.logical_not(mine))
    def _():
        out_ref[...] = other_ref[...].astype(f32).T


def turned(own, other, core):
    hidden, width = own.shape
    tile = 256

    def chosen(h, n, core):
        return (0, jnp.where(h == core[0], n, 0))

    def unchosen(h, n, core):
        return (0, jnp.where(h == core[0], 0, n))

    return pl.pallas_call(
        turn_kernel,
        grid_spec=pltpu.PrefetchScalarGridSpec(
            num_scalar_prefetch=1,
            grid=(2, width // tile),
            in_specs=[pl.BlockSpec((hidden, tile), chosen), pl.BlockSpec((hidden, tile), unchosen)],
            out_specs=pl.BlockSpec((tile, hidden), lambda h, n, core: (n, h)),
        ),
        out_shape=jax.ShapeDtypeStruct((width, 2 * hidden), f32),
        cost_estimate=brief,
        compiler_params=pltpu.CompilerParams(vmem_limit_bytes=48 * 1024 * 1024),
    )(core.astype(jnp.int32).reshape((1,)), own, other)


def run(body, outs, args, scratch=(), after=(), scalar=False):
    vmem = pl.BlockSpec(memory_space=pltpu.VMEM)
    specs = [vmem] * len(args)
    if scalar:
        specs[0] = pl.BlockSpec(memory_space=pltpu.SMEM)
    count = len(args)

    def whole(*refs):
        body(*refs[:count], *refs[count + len(after) :])

    return pl.pallas_call(
        whole,
        out_shape=outs,
        in_specs=specs + [pl.BlockSpec(memory_space=pl.ANY)] * len(after),
        out_specs=[vmem] * len(outs),
        scratch_shapes=scratch,
        cost_estimate=brief,
        compiler_params=large,
    )(*args, *after)


def take_heads(wide, count, size):
    return jnp.stack([wide[h * size : (h + 1) * size, h * size : (h + 1) * size] for h in range(count)])


def local(
    inputs,
    cotangent,
    segment_ids,
    norm_gain,
    branch_weight,
    stream_weight,
    conv_weight,
    conv_bias,
    recur_weight,
    recur_bias,
    intake_weight,
    intake_bias,
    decay_param,
    output_weight,
    mlp_gain,
    gate_weight,
    up_weight,
    down_weight,
    *,
    depth,
    square,
):
    line = square and depth == 4
    plain = not square
    core = lax.axis_index("core")
    core_id = core.astype(jnp.int32).reshape((1,))
    spot = jnp.zeros((1,), jnp.int32)
    if square:
        spot = spot + (2 * lax.axis_index("y") + lax.axis_index("x")).astype(jnp.int32)
    heads, head = recur_weight.shape[0], recur_weight.shape[1]
    width = heads * head
    length = segment_ids.shape[1]
    block, features = inputs.shape
    hidden_units = gate_weight.shape[1]
    shape = jax.ShapeDtypeStruct
    halves = [shape((block // 2, features), bf16)] * 2

    gain_one = norm_gain.astype(f32)[None, :]
    gain_two = mlp_gain.astype(f32)[None, :]
    normed_own = run(norm_kernel, halves, (inputs, gain_one))

    seg_row = segment_ids[0]
    masks = []
    for k in range(1, 4):
        earlier = jnp.concatenate([jnp.full((k,), -1, jnp.int32), seg_row[:-k]])
        masks.append((seg_row == earlier).astype(f32))
    joined = jnp.pad(jnp.stack(masks), ((0, 0), (0, 8)))
    joined = jnp.broadcast_to(joined[:, :, None], (3, length + 8, 128))
    square_low = shape((2, width, width), bf16)
    wide_high, wide_low = pl.pallas_call(
        prep_kernel, out_shape=[square_low, square_low], cost_estimate=brief
    )(recur_weight, intake_weight)
    gate_bias = jnp.stack([recur_bias, intake_bias])
    soft = (-decay_scale * jax.nn.softplus(-decay_param))[None, :]
    taps = conv_weight.astype(f32)

    cuts = (0, block * 3 // 4, block)
    spans = list(zip(cuts[:-1], cuts[1:], strict=True))
    if line:
        cots = [lax.all_gather(cotangent[a:b], ALL, axis=0, tiled=True) for a, b in spans]

    normed_pieces = gather_row(normed_own, square, (wide_high,) if square else ())
    token = shape((length, width), f32)
    token_low = shape((length, width), bf16)
    row_low = shape((length, features), bf16)
    row_sends = send_shapes(length, features, plain)
    normed, branch_pre, stream_pre, gated, convolved, recur_gate, intake_gate, state, *sends = run(
        functools.partial(forward_kernel, count=len(normed_pieces), head=head, plain=plain),
        [row_low, token, token, token_low, token, token, token, token, *row_sends],
        (
            spot,
            *normed_pieces,
            branch_weight,
            stream_weight,
            output_weight,
            joined,
            taps,
            conv_bias.astype(f32)[None, :],
            wide_high,
            wide_low,
            gate_bias,
            soft,
        ),
        [pltpu.VMEM((length, width), bf16)] * 2,
        scalar=True,
    )
    cot_own = (cotangent[: block // 2], cotangent[block // 2 :])
    if square:
        cot_own = held(cot_own, (normed_pieces[-1],))
    cot_row = jnp.concatenate(gather_row(cot_own, square), axis=0)
    activ_grad = lax.dot_general(cot_row, down_weight, contract_cols, preferred_element_type=f32)
    addends = scatter_row(sends, square)

    parts = [shape((b - a, features), bf16) for a, b in spans]
    hidden, one, two, *token_parts = run(
        functools.partial(second_norm_kernel, cuts=cuts),
        [shape((block, features), f32), *halves, *parts],
        (inputs, gain_two, *addends),
    )
    if line:
        tokens = [lax.all_gather(part, ALL, axis=0, tiled=True) for part in token_parts]
        gate_turned, up_turned = flipped(gate_weight, up_weight, core, (gated,))
    mlp_pieces = gather_row((one, two), square, (gate_turned,) if line else ())
    tile = min(512, hidden_units)
    fixed = [pl.BlockSpec(piece.shape, lambda i: (0, 0)) for piece in mlp_pieces]
    column = pl.BlockSpec((length, tile), lambda i: (0, i))
    weight_column = pl.BlockSpec((features, tile), lambda i: (0, i))
    low_units = shape((length, hidden_units), bf16)
    kept = [] if line else [low_units, low_units]
    mlp_in, activ, *sends = pl.pallas_call(
        functools.partial(mlp_kernel, count=len(mlp_pieces), plain=plain, keep=not line),
        grid=(hidden_units // tile,),
        in_specs=[*fixed, column, weight_column, weight_column],
        out_specs=[pl.BlockSpec(row_low.shape, lambda i: (0, 0)), column]
        + [column] * len(kept)
        + [pl.BlockSpec(send.shape, lambda i: (0, 0)) for send in row_sends],
        out_shape=[row_low, low_units, *kept, *row_sends],
        scratch_shapes=[pltpu.VMEM((length, features), bf16), pltpu.VMEM((length, features), f32)],
        cost_estimate=brief,
        compiler_params=pltpu.CompilerParams(vmem_limit_bytes=56 * 1024 * 1024),
    )(*mlp_pieces, activ_grad, gate_weight, up_weight)
    kept, sends = sends[: len(kept)], sends[len(kept) :]
    out_sends = run(functools.partial(down_kernel, plain=plain), row_sends, (activ, down_weight))
    addends = scatter_row(sends, square, (out_sends[0],) if square else ())

    mlp_gain_part, resid_grad, one, two = run(
        functools.partial(norm_back_kernel, final=False),
        [shape((1, features), f32), shape((block, features), f32), *halves],
        (hidden, cotangent, gain_two, *addends),
    )
    if line:
        kept_a = mlp_rows(core_id, tokens[0], cots[0], gate_turned, up_turned, down_weight, (one,))
    cot_pieces = gather_row((one, two), square)

    branch_cot, branch_low, stream_low, wide_grad, sums, *sends = run(
        functools.partial(backward_kernel, count=len(cot_pieces), head=head, plain=plain),
        [row_low, token_low, token_low, shape((2, width, width), f32), shape((8, width), f32), *row_sends],
        (
            spot,
            *cot_pieces,
            output_weight,
            branch_weight,
            stream_weight,
            branch_pre,
            stream_pre,
            joined,
            convolved,
            recur_gate,
            intake_gate,
            state,
            taps,
            wide_high,
            soft,
        ),
        [
            pltpu.VMEM((length, width), f32),
            pltpu.VMEM((2, length, width), bf16),
            pltpu.VMEM((length, width), bf16),
            pltpu.VMEM((length + 8, width), f32),
        ],
        scalar=True,
    )
    addends = scatter_row(sends, square)
    norm_gain_part, inputs_grad = run(
        functools.partial(norm_back_kernel, final=True),
        [shape((1, features), f32), shape((block, features), bf16)],
        (inputs, resid_grad, gain_one, *addends),
    )
    if square:
        out_sends = held(out_sends, (inputs_grad,))
    addends = scatter_row(out_sends, square)
    (block_out,) = run(add_kernel, [shape((block, features), bf16)], (hidden, *addends))

    def both(value):
        return jnp.concatenate([value, sibling(value)], axis=0)

    def both_halves(value):
        return jnp.concatenate(
            [half_of(value, core, 1), sibling(half_of(value, 1 - core, 1))], axis=0
        )

    normed_half = both_halves(normed)
    output_half = lax.dot_general(
        both(gated), both_halves(branch_cot), contract_rows, preferred_element_type=f32
    ).astype(bf16)
    branch_half = lax.dot_general(
        normed_half, both(branch_low), contract_rows, preferred_element_type=f32
    ).astype(bf16)
    stream_half = lax.dot_general(
        normed_half, both(stream_low), contract_rows, preferred_element_type=f32
    ).astype(bf16)
    recur_part = take_heads(wide_grad[0], heads, head).astype(bf16)
    intake_part = take_heads(wide_grad[1], heads, head).astype(bf16)
    gate_half = (
        jnp.where(core == 0, recur_part, intake_part).astype(f32)
        + sibling(jnp.where(core == 0, intake_part, recur_part)).astype(f32)
    ).astype(bf16)
    gains = jnp.concatenate([norm_gain_part, mlp_gain_part], axis=1)
    if square:
        gains = gains + lax.ppermute(gains, "x", swap)
        gains = gains + lax.ppermute(gains, "y", swap)
    else:
        gains = lax.psum(gains, ("y", "x"))
    small = jnp.concatenate([sums.reshape(-1), gains.reshape(-1)]).reshape(-1, 128)
    small = small + sibling(small)

    if line:
        first = [product(part, right, (), (stream_half,)) for part, right in zip(kept_a, (cots[0], tokens[0], tokens[0]), strict=True)]
        kept_b = mlp_rows(
            core_id, tokens[1], cots[1], gate_turned, up_turned, down_weight, (stream_half, *first)
        )
        down_half, gate_half_w, up_half_w = (
            product(part, right, (before,))
            for part, right, before in zip(kept_b, (cots[1], tokens[1], tokens[1]), first, strict=True)
        )
        groups = line_sums(
            [(output_half,), (branch_half,), (stream_half,), (gate_half, small)],
            ((first[0],), (first[2],), (kept_b[0],), (down_half,), (up_half_w,), ()),
        )
        (output_sum,), (branch_sum,), (stream_sum,), (gate_sum, small_sum) = groups
        down_w_grad = join(down_half, sibling(down_half), core, 0)
        gate_w_grad = turned(gate_half_w, sibling(gate_half_w), core)
        up_w_grad = turned(up_half_w, sibling(up_half_w), core)
    else:
        output_sum, branch_sum, stream_sum, gate_sum, small_sum = (
            lax.psum(part, "z") for part in (output_half, branch_half, stream_half, gate_half, small)
        )

        def over_rows(left, right):
            part = lax.dot_general(left, right, contract_rows, preferred_element_type=f32)
            return lax.psum(part.astype(bf16), ("z", "core")).astype(f32)

        gate_w_grad = over_rows(mlp_in, kept[0])
        up_w_grad = over_rows(mlp_in, kept[1])
        down_w_grad = over_rows(activ, cot_row)

    def whole(own, axis):
        return join(own, sibling(own), core, axis)

    gate_other = sibling(gate_sum)
    small_flat = small_sum.reshape(-1)
    sums = small_flat[: 8 * width].reshape(8, width)
    gains = small_flat[8 * width :].reshape(2, -1)
    return (
        block_out,
        inputs_grad,
        gains[0],
        whole(branch_sum, 0),
        whole(stream_sum, 0),
        sums[0:4],
        sums[4],
        jnp.where(core == 0, gate_sum, gate_other).astype(f32),
        sums[5],
        jnp.where(core == 0, gate_other, gate_sum).astype(f32),
        sums[6],
        sums[7] * decay_scale * jax.nn.sigmoid(-decay_param),
        whole(output_sum, 1),
        gains[1],
        gate_w_grad,
        up_w_grad,
        down_w_grad,
    )


def solution(mesh):
    depth = mesh.shape["dp"] // 2
    across = mesh.shape["mp"] // 2
    fine = Mesh(mesh.devices.reshape(depth, 2, 2, across), ALL)
    dp, mp = ("z", "core"), ("y", "x")
    cols, vec, blocks, rows = P(None, mp), P(mp), P(mp, None, None), P(mp, None)
    tokens = P(ALL, None)
    return jax.shard_map(
        functools.partial(local, depth=depth, square=across == 2),
        mesh=fine,
        in_specs=(
            tokens,
            tokens,
            P(dp, None),
            P(),
            cols,
            cols,
            cols,
            vec,
            blocks,
            vec,
            blocks,
            vec,
            vec,
            rows,
            P(),
            cols,
            cols,
            rows,
        ),
        out_specs=(
            tokens,
            tokens,
            P(),
            cols,
            cols,
            cols,
            vec,
            blocks,
            vec,
            blocks,
            vec,
            vec,
            rows,
            P(),
            cols,
            cols,
            rows,
        ),
        check_vma=False,
    )
```

```python
import functools

import jax
import jax.numpy as jnp
from jax import lax
from jax.experimental import pallas as pl
from jax.experimental.pallas import tpu as pltpu
from jax.sharding import Mesh
from jax.sharding import PartitionSpec as P

eps = 1e-06
decay_scale = 8.0
contract_rows = (((0,), (0,)), ((), ()))
contract_cols = (((1,), (1,)), ((), ()))
f32 = jnp.float32
bf16 = jnp.bfloat16
swap = [(0, 1), (1, 0)]


def cost(micros):
    return pl.CostEstimate(flops=0, bytes_accessed=int(micros * 3e6), transcendentals=0)


brief = cost(1)
large = pltpu.CompilerParams(vmem_limit_bytes=48 * 1024 * 1024)
ALL = ("z", "core", "y", "x")
STEP = 16
root_two_over_pi = 0.7978845608028654


def pass_kernel(*refs):
    pass


def held(values, after):
    values, after = list(values), list(after)
    anywhere = pl.BlockSpec(memory_space=pl.ANY)
    return pl.pallas_call(
        pass_kernel,
        in_specs=[anywhere] * (len(values) + len(after)),
        out_specs=[anywhere] * len(values),
        out_shape=[jax.ShapeDtypeStruct(value.shape, value.dtype) for value in values],
        input_output_aliases={n: n for n in range(len(values))},
        cost_estimate=cost(0.1),
    )(*values, *after)


def gather_row(halves, square, beside=()):
    if not square:
        return [lax.all_gather(jnp.concatenate(halves, axis=0), ("y", "x"), axis=0, tiled=True)]
    one, two = halves
    one_x = lax.ppermute(one, "x", swap)
    two_y = lax.ppermute(two, "y", swap)
    two_x = lax.ppermute(two, "x", swap)
    one_y = lax.ppermute(one, "y", swap)
    if beside:
        one_x, two_y = held((one_x, two_y), beside)
    one_d = lax.ppermute(one_x, "y", swap)
    two_d = lax.ppermute(two_y, "x", swap)
    return [one, one_x, one_y, one_d, two, two_x, two_y, two_d]


def gather_blocks(block, square):
    if not square:
        return gather_row((block,), square)
    return [
        block,
        lax.ppermute(block, "x", swap),
        lax.ppermute(block, "y", swap),
        lax.ppermute(block, ("y", "x"), [(0, 3), (3, 0), (1, 2), (2, 1)]),
    ]


def scatter_row(sends, square, beside=()):
    if not square:
        return [lax.psum_scatter(sends[0], ("y", "x"), scatter_dimension=0, tiled=True)]
    to_x, to_y, keep_x, keep_y, own = sends
    got_x = lax.ppermute(to_x, "x", swap)
    got_y = lax.ppermute(to_y, "y", swap)
    if beside:
        got_x, got_y = held((got_x, got_y), beside)
    send_y, send_x = pl.pallas_call(
        middle_kernel,
        out_shape=[jax.ShapeDtypeStruct(keep_x.shape, bf16)] * 2,
        cost_estimate=brief,
    )(got_x, got_y, keep_x, keep_y)
    last_y = lax.ppermute(send_y, "y", swap)
    last_x = lax.ppermute(send_x, "x", swap)
    return [own, got_x, got_y, last_y, last_x]


def sibling(value):
    return lax.ppermute(value, "core", swap)


def line_move(pieces):
    pairs = [[(0, 1), (3, 2)], [(1, 2), (2, 1)], [(1, 0), (2, 3)]]
    return [(piece, stage, lax.ppermute(piece, "z", pairs[stage])) for piece, stage in pieces]


def settle_kernel(inner_ref, *refs, stages):
    count = len(stages)
    for n, stage in enumerate(stages):
        piece, other, out = refs[n], refs[count + n], refs[2 * count + n]
        if stage < 2:
            out[...] = (piece[...].astype(f32) + other[...].astype(f32)).astype(out.dtype)
        else:
            out[...] = jnp.where(inner_ref[0] == 1, piece[...], other[...])


def line_settle(moved, after):
    place = lax.axis_index("z")
    inner = ((place == 1) | (place == 2)).astype(jnp.int32).reshape((1,))
    pieces, stages, others = zip(*moved, strict=True)
    return run(
        functools.partial(settle_kernel, stages=stages),
        [jax.ShapeDtypeStruct(piece.shape, piece.dtype) for piece in pieces],
        (inner, *pieces, *others),
        after=after,
        scalar=True,
    )


def assemble(pieces, out_ref):
    at = 0
    for piece in pieces:
        out_ref[at : at + piece.shape[0], :] = piece[...]
        at += piece.shape[0]


def split(whole_ref, core, mine_ref, theirs_ref):
    size = mine_ref.shape[1]
    for ref, which in ((mine_ref, core), (theirs_ref, 1 - core)):
        ref[...] = whole_ref[:, pl.ds(pl.multiple_of(which * size, 128), size)]


def pairs_kernel(*refs):
    count = len(refs) // 5
    for n in range(count):
        own_left, other_left, own_right, other_right = refs[4 * n : 4 * n + 4]
        out_ref = refs[4 * count + n]
        cols = out_ref.shape[1]
        for first in range(0, cols, 512):
            span = slice(first, min(first + 512, cols))
            out_ref[:, span] = (
                lax.dot_general(
                    own_left[...], own_right[:, span], contract_rows, preferred_element_type=f32
                )
                + lax.dot_general(
                    other_left[...], other_right[:, span], contract_rows, preferred_element_type=f32
                )
            ).astype(bf16)


def sum_kernel(one_ref, two_ref, *refs):
    out_ref, count = refs[-1], one_ref.shape[0]
    total = one_ref[...] + two_ref[...]
    if len(refs) > 1:
        gains = refs[0][...] + refs[1][...]
        rest = jnp.zeros((gains.shape[0], total.shape[1] - gains.shape[1]), f32)
        total = jnp.concatenate([total, jnp.concatenate([gains, rest], axis=1)], axis=0)
    out_ref[...] = total.astype(out_ref.dtype)


def add_one_kernel(one_ref, two_ref, out_ref):
    out_ref[...] = one_ref[...] + two_ref[...]


def send_shapes(length, width, plain):
    if plain:
        return [jax.ShapeDtypeStruct((length, width), bf16)]
    block, cut = length // 4, width // 2
    return (
        [jax.ShapeDtypeStruct((2 * block, cut), bf16)] * 2
        + [jax.ShapeDtypeStruct((block, cut), bf16)] * 2
        + [jax.ShapeDtypeStruct((block, width), f32)]
    )


def emit(value, first, width, sends, plain, spot=None):
    last = first + value.shape[1]
    if spot is not None:
        half = value.shape[0] // 8
        for n in range(2):
            for k in range(4):
                start = pl.multiple_of((lax.bitwise_xor(k, spot) * 2 + n) * half, half)
                block = value[(n * 4 + k) * half : (n * 4 + k + 1) * half]
                sends[0][pl.ds(start, half), first:last] = block.astype(bf16)
        return
    if plain:
        sends[0][:, first:last] = value.astype(bf16)
        return
    to_x, to_y, keep_x, keep_y, own = sends
    cut = width // 2
    half = value.shape[0] // 8

    def put(ref, at, block, cols, kind):
        for n in range(2):
            rows = slice(n * 4 * half + block * half, n * 4 * half + (block + 1) * half)
            ref[at + n * half : at + (n + 1) * half, cols] = value[rows].astype(kind)

    put(own, 0, 0, slice(first, last), f32)
    if last <= cut:
        cols = slice(first, last)
        put(to_x, 0, 1, cols, bf16)
        put(to_x, 2 * half, 3, cols, bf16)
        put(keep_y, 0, 2, cols, bf16)
    else:
        cols = slice(first - cut, last - cut)
        put(to_y, 0, 2, cols, bf16)
        put(to_y, 2 * half, 3, cols, bf16)
        put(keep_x, 0, 1, cols, bf16)


def middle_kernel(got_x, got_y, keep_x, keep_y, send_y, send_x):
    block = keep_x.shape[0]
    send_y[...] = (keep_y[...].astype(f32) + got_x[block:].astype(f32)).astype(bf16)
    send_x[...] = (keep_x[...].astype(f32) + got_y[block:].astype(f32)).astype(bf16)


def finish(refs):
    if len(refs) == 1:
        return refs[0][...].astype(f32)
    own, got_x, got_y, last_y, last_x = refs
    block, cut = last_y.shape
    left = own[:, :cut] + got_x[:block].astype(f32) + last_y[...].astype(f32)
    right = own[:, cut:] + got_y[:block].astype(f32) + last_x[...].astype(f32)
    return jnp.concatenate([left, right], axis=1)


def mean_of(x):
    return jnp.mean(x, axis=-1, keepdims=True)


def norm_kernel(input_ref, gain_ref, one_ref, two_ref):
    values = input_ref[...].astype(f32)
    normed = (values * lax.rsqrt(mean_of(values * values) + eps) * gain_ref[...]).astype(bf16)
    half = normed.shape[0] // 2
    one_ref[...] = normed[:half]
    two_ref[...] = normed[half:]


def second_norm_kernel(input_ref, gain_ref, *refs):
    addends, (hidden_ref, one_ref, two_ref, all_ref) = refs[:-4], refs[-4:]
    hidden = input_ref[...].astype(f32) + finish(addends)
    hidden_ref[...] = hidden
    normed = (hidden * lax.rsqrt(mean_of(hidden * hidden) + eps) * gain_ref[...]).astype(bf16)
    half = normed.shape[0] // 2
    one_ref[...] = normed[:half]
    two_ref[...] = normed[half:]
    all_ref[...] = normed


def norm_back_kernel(value_ref, before_ref, gain_ref, *refs, final):
    outs = 1 if final else 4
    addends, outs = refs[:-outs], refs[-outs:]
    values = value_ref[...].astype(f32)
    scale = lax.rsqrt(mean_of(values * values) + eps)
    hat = values * scale
    grad = finish(addends)
    scaled = grad * gain_ref[...]
    total = before_ref[...].astype(f32) + scale * (scaled - hat * mean_of(scaled * hat))
    if final:
        outs[0][...] = total.astype(bf16)
        return
    outs[0][...] = jnp.sum(grad * hat, axis=0, keepdims=True)
    outs[1][...] = total
    low = total.astype(bf16)
    half = low.shape[0] // 2
    outs[2][...] = low[:half]
    outs[3][...] = low[half:]


def add_kernel(value_ref, *refs):
    refs[-1][...] = (value_ref[...] + finish(refs[:-1])).astype(bf16)


def mlp_kernel(*refs, count, plain, keep):
    pieces, (grad_ref, gate_w, up_w), refs = refs[:count], refs[count : count + 3], refs[count + 3 :]
    *outs, token_ref, total_ref = refs
    token_out, activ_ref, *outs = outs
    step = pl.program_id(0)

    @pl.when(step == 0)
    def _():
        assemble(pieces, token_ref)
        token_out[...] = token_ref[...]

    tokens = token_ref[...]
    gate_pre = jnp.dot(tokens, gate_w[...], preferred_element_type=f32)
    up_pre = jnp.dot(tokens, up_w[...], preferred_element_type=f32)
    activ_grad = grad_ref[...]
    value, slope = gelu_terms(gate_pre)
    activ_ref[...] = (value * up_pre).astype(bf16)
    gate_low = (activ_grad * up_pre * slope).astype(bf16)
    up_low = (activ_grad * value).astype(bf16)
    if keep:
        outs[0][...] = gate_low
        outs[1][...] = up_low
        outs = outs[2:]
    width = total_ref.shape[1]
    last = step == pl.num_programs(0) - 1
    for first in range(0, width, 512):
        cols = slice(first, first + 512)
        part = lax.dot_general(
            gate_low, gate_w[cols, :], contract_cols, preferred_element_type=f32
        ) + lax.dot_general(up_low, up_w[cols, :], contract_cols, preferred_element_type=f32)

        @pl.when(step == 0)
        def _(part=part, cols=cols):
            total_ref[:, cols] = part

        @pl.when(step > 0)
        def _(part=part, cols=cols):
            total_ref[:, cols] += part

    @pl.when(last)
    def _():
        for first in range(0, width, 512):
            emit(total_ref[:, first : first + 512], first, width, outs, plain)


def down_kernel(spot_ref, activ_ref, weight_ref, *sends, plain):
    spot = None if plain else spot_ref[0]
    width = weight_ref.shape[1]
    for first in range(0, width, 512):
        cols = slice(first, first + 512)
        value = jnp.dot(activ_ref[...], weight_ref[:, cols], preferred_element_type=f32)
        emit(value, first, width, sends, plain, spot)


def tile_span(first, last, head, width):
    low = (first // head) * head // 128 * 128
    high = min(width, -(-(((last - 1) // head + 1) * head) // 128) * 128)
    return low, high


def tiles(width):
    return [(n, min(n + 256, width)) for n in range(0, width, 256)]


def sigmoid(x):
    return 1.0 / (1.0 + jnp.exp(-x))


def decay_terms(gate, soft, link):
    log_decay = gate * soft
    decay = jnp.exp(log_decay)
    square = decay * decay
    x = 2.0 * log_decay
    series = 1.0 + x * (1.0 / 6.0) * (1.0 + x * (1.0 / 7.0))
    series = 1.0 + x * (1.0 / 4.0) * (1.0 + x * (1.0 / 5.0) * series)
    series = -x * (1.0 + x * (1.0 / 2.0) * (1.0 + x * (1.0 / 3.0) * series))
    gap = jnp.where(x > -0.3, series, 1.0 - square)
    root = jnp.sqrt(gap)
    return link * decay, square, root, link * root + (1.0 - link)


def gelu_terms(x):
    inner = jnp.tanh(root_two_over_pi * (x + 0.044715 * x * x * x))
    value = 0.5 * x * (1.0 + inner)
    slope = 0.5 * (1.0 + inner) + 0.5 * x * (1.0 - inner * inner) * root_two_over_pi * (
        1.0 + 3.0 * 0.044715 * x * x
    )
    return value, slope


def widen(mask, width):
    return jnp.concatenate([mask] * (-(-width // 128)), axis=1)[:, :width]


def token_place(length, spot, plain):
    block, half = length // 4, length // 8
    per_block = block // STEP
    per_half = half // STEP

    def offset(step):
        if plain:
            return pl.multiple_of(step * STEP, STEP)
        turn = lax.bitwise_xor(step // per_block, spot)
        inside = lax.rem(step, per_block)
        at = (inside // per_half) * (length // 2) + turn * half + lax.rem(inside, per_half) * STEP
        return pl.multiple_of(at, STEP)

    return offset


def prep_kernel(recur_ref, intake_ref, high_ref, low_ref):
    count, size, _ = recur_ref.shape
    for which, ref in ((0, recur_ref), (1, intake_ref)):
        for h in range(count):
            parts = [ref[h]]
            if h:
                parts.insert(0, jnp.zeros((size, h * size), f32))
            if h < count - 1:
                parts.append(jnp.zeros((size, (count - 1 - h) * size), f32))
            row = jnp.concatenate(parts, axis=1)
            high = row.astype(bf16)
            rows = slice(h * size, (h + 1) * size)
            high_ref[which, rows, :] = high
            low_ref[which, rows, :] = (row - high.astype(f32)).astype(bf16)


def forward_kernel(spot_ref, *refs, count, head, plain):
    pieces, refs = refs[:count], refs[count:]
    (branch_w, stream_w, output_w, joined_ref, taps_ref, bias_ref, high_ref, low_ref, gate_bias_ref, soft_ref), refs = (
        refs[:10],
        refs[10:],
    )
    (mine_ref, theirs_ref, branch_ref, stream_ref, gated_ref, conv_ref, recur_ref, intake_ref, state_ref), refs = (
        refs[:9],
        refs[9:],
    )
    *sends, part_high, part_low, normed_ref = refs
    assemble(pieces, normed_ref)
    split(normed_ref, spot_ref[1], mine_ref, theirs_ref)
    for first, last in tiles(branch_ref.shape[1]):
        cols = slice(first, last)
        branch_ref[:, cols] = jnp.dot(normed_ref[...], branch_w[:, cols], preferred_element_type=f32)
        stream_ref[:, cols] = jnp.dot(normed_ref[...], stream_w[:, cols], preferred_element_type=f32)
    length, width = branch_ref.shape
    steps = length // STEP
    offset = token_place(length, spot_ref[0], plain)

    def convolve(step, before):
        at = offset(step)
        here = pl.multiple_of(step * STEP, STEP)
        now = stream_ref[pl.ds(at, STEP), :]
        both = jnp.concatenate([before, now], axis=0)
        total = bias_ref[0:1, :] + taps_ref[0:1, :] * now
        for k in range(1, 4):
            mask = widen(joined_ref[k - 1, pl.ds(here, STEP), :], width)
            total = total + taps_ref[k : k + 1, :] * both[8 - k : 8 - k + STEP] * mask
        conv_ref[pl.ds(at, STEP), :] = total
        high = total.astype(bf16)
        part_high[pl.ds(here, STEP), :] = high
        part_low[pl.ds(here, STEP), :] = (total - high.astype(f32)).astype(bf16)
        return now[STEP - 8 :]

    lax.fori_loop(0, steps, convolve, jnp.zeros((8, width), f32))

    for which, out_ref in ((0, recur_ref), (1, intake_ref)):
        for first, last in tiles(width):
            low, high = tile_span(first, last, head, width)
            span, cols = slice(low, high), slice(first, last)
            high_part, low_part = high_ref[which, span, cols], low_ref[which, span, cols]
            pre = (
                jnp.dot(part_high[:, span], high_part, preferred_element_type=f32)
                + jnp.dot(part_low[:, span], high_part, preferred_element_type=f32)
                + jnp.dot(part_high[:, span], low_part, preferred_element_type=f32)
            )
            out_ref[:, cols] = pre + gate_bias_ref[which : which + 1, cols]

    rows = lax.broadcasted_iota(jnp.int32, (8, width), 0)
    soft = soft_ref[0:1, :]

    def advance(step, last_state):
        at = offset(step)
        here = pl.multiple_of(step * STEP, STEP)
        link = widen(joined_ref[0, pl.ds(here, STEP), :], width)
        conv = conv_ref[pl.ds(at, STEP), :]
        recur = sigmoid(recur_ref[pl.ds(here, STEP), :])
        intake = sigmoid(intake_ref[pl.ds(here, STEP), :])
        recur_ref[pl.ds(here, STEP), :] = recur
        intake_ref[pl.ds(here, STEP), :] = intake
        carried, square, root, multiplier = decay_terms(recur, soft, link)
        driven = multiplier * intake * conv
        found = []
        for part in range(STEP // 8):
            a = carried[8 * part : 8 * part + 8]
            b = driven[8 * part : 8 * part + 8]
            for shift in (1, 2, 4):
                a_before = jnp.where(rows >= shift, pltpu.roll(a, shift, 0), 1.0)
                b_before = jnp.where(rows >= shift, pltpu.roll(b, shift, 0), 0.0)
                b = b + a * b_before
                a = a * a_before
            state = b + a * last_state
            last_state = state[7:8]
            found.append(state)
        state = jnp.concatenate(found, axis=0)
        state_ref[pl.ds(at, STEP), :] = state
        value, slope = gelu_terms(branch_ref[pl.ds(at, STEP), :])
        gated_ref[pl.ds(at, STEP), :] = (value * state).astype(bf16)
        return last_state

    lax.fori_loop(0, steps, advance, jnp.zeros((1, width), f32))
    step_cols = 512
    for first in range(0, output_w.shape[1], step_cols):
        cols = slice(first, first + step_cols)
        value = jnp.dot(gated_ref[...], output_w[:, cols], preferred_element_type=f32)
        emit(value, first, output_w.shape[1], sends, plain)


def branch_back_kernel(spot_ref, *refs, count):
    pieces, (output_w, branch_ref, state_ref), refs = refs[:count], refs[count : count + 3], refs[count + 3 :]
    mine_ref, theirs_ref, branch_grad_ref, grad_ref, cot_ref = refs
    assemble(pieces, cot_ref)
    split(cot_ref, spot_ref[1], mine_ref, theirs_ref)
    length, width = branch_ref.shape
    for first, last in tiles(width):
        cols = slice(first, last)
        grad_ref[:, cols] = lax.dot_general(
            cot_ref[...], output_w[cols, :], contract_cols, preferred_element_type=f32
        )

    def rows(step, _):
        at = pl.ds(pl.multiple_of(step * STEP, STEP), STEP)
        value, slope = gelu_terms(branch_ref[at, :])
        grad = grad_ref[at, :]
        branch_grad_ref[at, :] = (grad * state_ref[at, :] * slope).astype(bf16)
        grad_ref[at, :] = grad * value
        return _

    lax.fori_loop(0, length // STEP, rows, 0)


def backward_kernel(
    spot_ref,
    grad_ref,
    branch_grad_ref,
    branch_w,
    stream_w,
    stream_ref,
    joined_ref,
    conv_ref,
    recur_ref,
    intake_ref,
    state_ref,
    taps_ref,
    high_ref,
    soft_ref,
    normed_mine,
    normed_theirs,
    gain_ref,
    stream_grad_ref,
    mine_ref,
    theirs_ref,
    gains_ref,
    *refs,
    head,
    plain,
):
    *sends, gates_ref, sums_ref, pre_ref, conv_low, conv_grad = refs
    length, width = grad_ref.shape
    steps = length // STEP
    offset = token_place(length, spot_ref[0], plain)

    rows = lax.broadcasted_iota(jnp.int32, (8, width), 0)
    soft = soft_ref[0:1, :]
    count = STEP // 8

    def fold(value):
        total = value[0:8]
        for part in range(1, count):
            total = total + value[8 * part : 8 * part + 8]
        return total

    def retreat(turn, kept):
        after_carried, after_adjoint, decay_sum, recur_sum, intake_sum = kept
        step = steps - 1 - turn
        at = offset(step)
        at_before = offset(jnp.maximum(step - 1, 0))
        here = pl.multiple_of(step * STEP, STEP)
        link = widen(joined_ref[0, pl.ds(here, STEP), :], width)
        conv = conv_ref[pl.ds(at, STEP), :]
        recur = recur_ref[pl.ds(here, STEP), :]
        intake = intake_ref[pl.ds(here, STEP), :]
        carried, square, root, multiplier = decay_terms(recur, soft, link)
        grad = grad_ref[pl.ds(at, STEP), :]
        found = []
        for part in reversed(range(count)):
            own = carried[8 * part : 8 * part + 8]
            a = jnp.where(rows < 7, pltpu.roll(own, 7, 0), after_carried)
            b = grad[8 * part : 8 * part + 8]
            for shift in (1, 2, 4):
                a_after = jnp.where(rows < 8 - shift, pltpu.roll(a, 8 - shift, 0), 1.0)
                b_after = jnp.where(rows < 8 - shift, pltpu.roll(b, 8 - shift, 0), 0.0)
                b = b + a * b_after
                a = a * a_after
            adjoint = b + a * after_adjoint
            after_adjoint = adjoint[0:1]
            after_carried = own[0:1]
            found.append(adjoint)
        adjoint = jnp.concatenate(found[::-1], axis=0)
        state = state_ref[pl.ds(at, STEP), :]
        tail = state_ref[pl.ds(at_before + (STEP - 8), 8), :]
        earlier = jnp.concatenate([tail, state], axis=0)[7 : 7 + STEP]
        driven_part = adjoint * intake
        log_grad = adjoint * earlier * carried - driven_part * conv * link * square / root
        recur_grad = log_grad * soft * recur * (1.0 - recur)
        spread = driven_part * multiplier
        intake_grad = spread * conv * (1.0 - intake)
        pre_ref[0, pl.ds(here, STEP), :] = recur_grad.astype(bf16)
        pre_ref[1, pl.ds(here, STEP), :] = intake_grad.astype(bf16)
        conv_low[pl.ds(here, STEP), :] = conv.astype(bf16)
        conv_grad[pl.ds(here, STEP), :] = spread
        return (
            after_carried,
            after_adjoint,
            decay_sum + fold(log_grad * recur),
            recur_sum + fold(recur_grad),
            intake_sum + fold(intake_grad),
        )

    line = jnp.zeros((1, width), f32)
    eight = jnp.zeros((8, width), f32)
    kept = lax.fori_loop(0, steps, retreat, (line, line, eight, eight, eight))
    sums_ref[5:6, :] = jnp.sum(kept[3], axis=0, keepdims=True)
    sums_ref[6:7, :] = jnp.sum(kept[4], axis=0, keepdims=True)
    sums_ref[7:8, :] = jnp.sum(kept[2], axis=0, keepdims=True)

    conv_grad[length : length + 8, :] = eight
    for first, last in tiles(width):
        low, high = tile_span(first, last, head, width)
        span, cols = slice(low, high), slice(first, last)
        total = conv_grad[0:length, cols]
        for which in range(2):
            total = total + lax.dot_general(
                pre_ref[which, :, span], high_ref[which, cols, span], contract_cols, preferred_element_type=f32
            )
            gates_ref[which, span, cols] = lax.dot_general(
                conv_low[:, span], pre_ref[which, :, cols], contract_rows, preferred_element_type=f32
            )
        conv_grad[0:length, cols] = total

    def unwind(step, kept):
        at = offset(step)
        here = pl.multiple_of(step * STEP, STEP)
        ahead = conv_grad[pl.ds(here, STEP + 8), :]
        now = stream_ref[pl.ds(at, STEP), :]
        total = taps_ref[0:1, :] * ahead[0:STEP]
        sums = [kept[0] + fold(ahead[0:STEP] * now)]
        for k in range(1, 4):
            mask = widen(joined_ref[k - 1, pl.ds(here, STEP + 8), :], width)
            moved = (ahead * mask)[k : k + STEP]
            total = total + taps_ref[k : k + 1, :] * moved
            sums.append(kept[k] + fold(moved * now))
        stream_grad_ref[pl.ds(at, STEP), :] = total.astype(bf16)
        return (*sums, kept[4] + fold(ahead[0:STEP]))

    kept = lax.fori_loop(0, steps, unwind, (eight,) * 5)
    for k in range(5):
        sums_ref[k : k + 1, :] = jnp.sum(kept[k], axis=0, keepdims=True)
    count = width // head
    lanes = lax.broadcasted_iota(jnp.int32, (head, width), 1)
    for out_ref, which in ((mine_ref, spot_ref[1]), (theirs_ref, 1 - spot_ref[1])):
        blocks = gates_ref[which, 0:head, :]
        for h in range(1, count):
            blocks = jnp.where(lanes >= h * head, gates_ref[which, h * head : (h + 1) * head, :], blocks)
        out_ref[0:head, :] = blocks
        out_ref[head : head + 8, :] = sums_ref[...]

    step_cols = 512
    for first in range(0, branch_w.shape[0], step_cols):
        cols = slice(first, first + step_cols)
        value = lax.dot_general(
            branch_grad_ref[...], branch_w[cols, :], contract_cols, preferred_element_type=f32
        ) + lax.dot_general(
            stream_grad_ref[...], stream_w[cols, :], contract_cols, preferred_element_type=f32
        )
        half = normed_mine.shape[1]
        inside = slice(first % half, first % half + step_cols)
        mine = spot_ref[1] == first // half
        normed = jnp.where(mine, normed_mine[:, inside], normed_theirs[:, inside]).astype(f32)
        gains_ref[:, cols] = jnp.sum(value * normed, axis=0, keepdims=True) / gain_ref[:, cols]
        emit(value, first, branch_w.shape[0], sends, plain, None if plain else spot_ref[0])


def rows_kernel(token_ref, grad_ref, gate_ref, up_ref, *rest):
    activ_ref, gate_out, up_out = rest[-3:]
    tokens = token_ref[...]
    hidden = gate_ref.shape[0]
    part = hidden // 3
    for n in range(3):
        rows = slice(n * part, (n + 1) * part)
        gate_pre = lax.dot_general(gate_ref[rows], tokens, contract_cols, preferred_element_type=f32)
        up_pre = lax.dot_general(up_ref[rows], tokens, contract_cols, preferred_element_type=f32)
        activ_grad = grad_ref[rows]
        value, slope = gelu_terms(gate_pre)
        activ_ref[rows] = (value * up_pre).astype(bf16)
        gate_out[rows] = (activ_grad * up_pre * slope).astype(bf16)
        up_out[rows] = (activ_grad * value).astype(bf16)


def mlp_rows(tokens, grads, gate, up, part, kept, after):
    count, width = tokens.shape
    hidden = gate.shape[0]
    tile = 512
    steps = count // tile // 2
    tall = pl.BlockSpec((hidden, tile), lambda i: (0, i + part * steps))
    weight = pl.BlockSpec((hidden, width), lambda i: (0, 0))
    return pl.pallas_call(
        rows_kernel,
        grid=(steps,),
        in_specs=[pl.BlockSpec((tile, width), lambda i: (i + part * steps, 0)), tall, weight, weight]
        + [pl.BlockSpec(memory_space=pl.ANY)] * (len(kept) + len(after)),
        out_specs=[tall, tall, tall],
        out_shape=[jax.ShapeDtypeStruct((hidden, count), bf16)] * 3,
        input_output_aliases={4 + n: n for n in range(len(kept))},
        cost_estimate=cost(20),
        compiler_params=large,
    )(tokens, grads, gate, up, *kept, *after)


def row_back_kernel(*refs, count):
    pieces, (weight_ref, out_ref, rows_ref) = refs[:count], refs[count:]

    @pl.when(pl.program_id(0) == 0)
    def _():
        half = pieces[0].shape[0] // 2
        at = 0
        for n in range(2):
            for piece in pieces:
                rows_ref[at : at + half, :] = piece[n * half : (n + 1) * half, :]
                at += half

    out_ref[...] = lax.dot_general(
        rows_ref[...], weight_ref[...], contract_cols, preferred_element_type=f32
    )


def row_back(pieces, down):
    hidden, width = down.shape
    length = sum(piece.shape[0] for piece in pieces)
    tile = min(512, hidden)
    return pl.pallas_call(
        functools.partial(row_back_kernel, count=len(pieces)),
        grid=(hidden // tile,),
        in_specs=[pl.BlockSpec(piece.shape, lambda i: (0, 0)) for piece in pieces]
        + [pl.BlockSpec((tile, width), lambda i: (i, 0))],
        out_specs=pl.BlockSpec((length, tile), lambda i: (0, i)),
        out_shape=jax.ShapeDtypeStruct((length, hidden), f32),
        scratch_shapes=[pltpu.VMEM((length, width), bf16)],
        cost_estimate=cost(6),
        compiler_params=large,
    )(*pieces, down)


def product(left, right, core, turn, after=()):
    rows, depth = left.shape
    cols = right.shape[1]
    tile = 256

    def body(core_ref, left_ref, right_ref, *rest):
        low_ref, whole_ref = rest[-2:]
        low = jnp.dot(left_ref[...], right_ref[...], preferred_element_type=f32).astype(bf16)
        low_ref[...] = low
        wide = low.astype(f32)
        whole_ref[...] = wide.T if turn else wide

    if turn:
        place = pl.BlockSpec((tile, rows), lambda n, core: (n, core[0]))
        shape = (cols, 2 * rows)
    else:
        place = pl.BlockSpec((rows, tile), lambda n, core: (core[0], n))
        shape = (2 * rows, cols)
    return pl.pallas_call(
        body,
        grid_spec=pltpu.PrefetchScalarGridSpec(
            num_scalar_prefetch=1,
            grid=(cols // tile,),
            in_specs=[
                pl.BlockSpec((rows, depth), lambda n, core: (0, 0)),
                pl.BlockSpec((depth, tile), lambda n, core: (0, n)),
            ]
            + [pl.BlockSpec(memory_space=pl.ANY)] * len(after),
            out_specs=[pl.BlockSpec((rows, tile), lambda n, core: (0, n)), place],
        ),
        out_shape=[jax.ShapeDtypeStruct((rows, cols), bf16), jax.ShapeDtypeStruct(shape, f32)],
        cost_estimate=cost(20),
        compiler_params=large,
    )(core, left, right, *after)


def filled(whole, other, core, turn, after=()):
    rows, cols = other.shape
    tile = cols // 2

    def body(core_ref, other_ref, *rest):
        wide = other_ref[...].astype(f32)
        rest[-1][...] = wide.T if turn else wide

    if turn:
        place = pl.BlockSpec((tile, rows), lambda n, core: (n, 1 - core[0]))
    else:
        place = pl.BlockSpec((rows, tile), lambda n, core: (1 - core[0], n))
    return pl.pallas_call(
        body,
        grid_spec=pltpu.PrefetchScalarGridSpec(
            num_scalar_prefetch=1,
            grid=(2,),
            in_specs=[
                pl.BlockSpec((rows, tile), lambda n, core: (0, n)),
            ]
            + [pl.BlockSpec(memory_space=pl.ANY)] * (1 + len(after)),
            out_specs=place,
        ),
        out_shape=jax.ShapeDtypeStruct(whole.shape, f32),
        input_output_aliases={2: 0},
        cost_estimate=cost(4.5),
        compiler_params=large,
    )(core, other, whole, *after)


def join_kernel(core_ref, own_ref, other_ref, *rest):
    mine = pl.program_id(0) == core_ref[0]
    rest[-1][...] = jnp.where(mine, own_ref[...], other_ref[...]).astype(f32)


def joined_halves(own, other, core, axis, after):
    rows, cols = own.shape
    part = pl.BlockSpec((rows, cols), lambda h, core: (0, 0))
    place = pl.BlockSpec((rows, cols), (lambda h, core: (h, 0)) if axis == 0 else (lambda h, core: (0, h)))
    shape = (2 * rows, cols) if axis == 0 else (rows, 2 * cols)
    return pl.pallas_call(
        join_kernel,
        grid_spec=pltpu.PrefetchScalarGridSpec(
            num_scalar_prefetch=1,
            grid=(2,),
            in_specs=[part, part] + [pl.BlockSpec(memory_space=pl.ANY)] * len(after),
            out_specs=place,
        ),
        out_shape=jax.ShapeDtypeStruct(shape, f32),
        cost_estimate=cost(4),
        compiler_params=large,
    )(core, own, other, *after)


def back_kernel(core_ref, weight_ref, cot_ref, *rest):
    rest[-1][...] = lax.dot_general(
        weight_ref[...], cot_ref[...], contract_cols, preferred_element_type=f32
    )


def down_back(core, cots, down, after):
    count, width = cots.shape
    hidden = down.shape[0] // 2
    tile = 512
    return pl.pallas_call(
        back_kernel,
        grid_spec=pltpu.PrefetchScalarGridSpec(
            num_scalar_prefetch=1,
            grid=(count // tile,),
            in_specs=[
                pl.BlockSpec((hidden, width), lambda i, core: (core[0], 0)),
                pl.BlockSpec((tile, width), lambda i, core: (i, 0)),
            ]
            + [pl.BlockSpec(memory_space=pl.ANY)] * len(after),
            out_specs=pl.BlockSpec((hidden, tile), lambda i, core: (0, i)),
        ),
        out_shape=jax.ShapeDtypeStruct((hidden, count), f32),
        cost_estimate=cost(20),
        compiler_params=large,
    )(core, down, cots, *after)


def flip_kernel(core_ref, one_ref, two_ref, *rest):
    rest[-2][...] = one_ref[...].astype(f32).T.astype(bf16)
    rest[-1][...] = two_ref[...].astype(f32).T.astype(bf16)


def flipped(one, two, core, after):
    width, hidden = one.shape[0], one.shape[1] // 2
    tile = 256
    source = pl.BlockSpec((tile, hidden), lambda n, core: (n, core[0]))
    result = pl.BlockSpec((hidden, tile), lambda n, core: (0, n))
    return pl.pallas_call(
        flip_kernel,
        grid_spec=pltpu.PrefetchScalarGridSpec(
            num_scalar_prefetch=1,
            grid=(width // tile,),
            in_specs=[source, source] + [pl.BlockSpec(memory_space=pl.ANY)] * len(after),
            out_specs=[result, result],
        ),
        out_shape=[jax.ShapeDtypeStruct((hidden, width), bf16)] * 2,
        cost_estimate=cost(8),
    )(core.astype(jnp.int32).reshape((1,)), one, two, *after)


def run(body, outs, args, scratch=(), after=(), scalar=False, micros=1):
    vmem = pl.BlockSpec(memory_space=pltpu.VMEM)
    specs = [vmem] * len(args)
    if scalar:
        specs[0] = pl.BlockSpec(memory_space=pltpu.SMEM)
    count = len(args)

    def whole(*refs):
        body(*refs[:count], *refs[count + len(after) :])

    return pl.pallas_call(
        whole,
        out_shape=outs,
        in_specs=specs + [pl.BlockSpec(memory_space=pl.ANY)] * len(after),
        out_specs=[vmem] * len(outs),
        scratch_shapes=scratch,
        cost_estimate=cost(micros),
        compiler_params=large,
    )(*args, *after)


def local(
    inputs,
    cotangent,
    segment_ids,
    norm_gain,
    branch_weight,
    stream_weight,
    conv_weight,
    conv_bias,
    recur_weight,
    recur_bias,
    intake_weight,
    intake_bias,
    decay_param,
    output_weight,
    mlp_gain,
    gate_weight,
    up_weight,
    down_weight,
    *,
    depth,
    square,
):
    line = square and depth == 4
    plain = not square
    core = lax.axis_index("core")
    core_id = core.astype(jnp.int32).reshape((1,))
    spot = jnp.zeros((1,), jnp.int32)
    if square:
        spot = spot + (2 * lax.axis_index("y") + lax.axis_index("x")).astype(jnp.int32)
    where = jnp.concatenate([spot, core_id])
    heads, head = recur_weight.shape[0], recur_weight.shape[1]
    width = heads * head
    length = segment_ids.shape[1]
    block, features = inputs.shape
    hidden_units = gate_weight.shape[1]
    shape = jax.ShapeDtypeStruct
    halves = [shape((block // 2, features), bf16)] * 2

    gain_one = norm_gain.astype(f32)[None, :]
    gain_two = mlp_gain.astype(f32)[None, :]
    normed_own = run(norm_kernel, halves, (inputs, gain_one))

    seg_row = segment_ids[0]
    masks = []
    for k in range(1, 4):
        earlier = jnp.concatenate([jnp.full((k,), -1, jnp.int32), seg_row[:-k]])
        masks.append((seg_row == earlier).astype(f32))
    joined = jnp.pad(jnp.stack(masks), ((0, 0), (0, 8)))
    joined = jnp.broadcast_to(joined[:, :, None], (3, length + 8, 128))
    square_low = shape((2, width, width), bf16)
    wide_high, wide_low = pl.pallas_call(
        prep_kernel, out_shape=[square_low, square_low], cost_estimate=brief
    )(recur_weight, intake_weight)
    gate_bias = jnp.stack([recur_bias, intake_bias])
    soft = (-decay_scale * jax.nn.softplus(-decay_param))[None, :]
    taps = conv_weight.astype(f32)

    if line:
        cots = lax.all_gather(cotangent, ALL, axis=0, tiled=True)

    normed_pieces = gather_row(normed_own, square, (wide_high,) if square else ())
    token = shape((length, width), f32)
    token_low = shape((length, width), bf16)
    row_low = shape((length, features), bf16)
    row_sends = send_shapes(length, features, plain)
    half_row = shape((length, features // 2), bf16)
    normed_mine, normed_theirs, branch_pre, stream_pre, gated, convolved, recur_gate, intake_gate, state, *sends = run(
        functools.partial(forward_kernel, count=len(normed_pieces), head=head, plain=plain),
        [half_row, half_row, token, token, token_low, token, token, token, token, *row_sends],
        (
            where,
            *normed_pieces,
            branch_weight,
            stream_weight,
            output_weight,
            joined,
            taps,
            conv_bias.astype(f32)[None, :],
            wide_high,
            wide_low,
            gate_bias,
            soft,
        ),
        [pltpu.VMEM((length, width), bf16)] * 2 + [pltpu.VMEM((length, features), bf16)],
        scalar=True,
        micros=20,
    )
    own_cots = cotangent
    if square:
        (own_cots,) = held((cotangent,), normed_pieces)
    own_cots = gather_blocks(own_cots, square)
    activ_grad = row_back(own_cots, down_weight)
    if square:
        sends[:2] = held(sends[:2], own_cots[1:])
    addends = scatter_row(sends, square, (activ_grad,) if square else ())

    hidden, one, two, normed_two = run(
        second_norm_kernel,
        [shape((block, features), f32), *halves, shape((block, features), bf16)],
        (inputs, gain_two, *addends),
    )
    if line:
        tokens = lax.all_gather(normed_two, ALL, axis=0, tiled=True)
        gate_turned, up_turned = flipped(gate_weight, up_weight, core, (gated,))
    mlp_pieces = gather_row((one, two), square, (gate_turned,) if line else ())
    tile = min(512, hidden_units)
    fixed = [pl.BlockSpec(piece.shape, lambda i: (0, 0)) for piece in mlp_pieces]
    column = pl.BlockSpec((length, tile), lambda i: (0, i))
    weight_column = pl.BlockSpec((features, tile), lambda i: (0, i))
    low_units = shape((length, hidden_units), bf16)
    kept = [] if line else [low_units, low_units]
    mlp_in, activ, *sends = pl.pallas_call(
        functools.partial(mlp_kernel, count=len(mlp_pieces), plain=plain, keep=not line),
        grid=(hidden_units // tile,),
        in_specs=[*fixed, column, weight_column, weight_column],
        out_specs=[pl.BlockSpec(row_low.shape, lambda i: (0, 0)), column]
        + [column] * len(kept)
        + [pl.BlockSpec(send.shape, lambda i: (0, 0)) for send in row_sends],
        out_shape=[row_low, low_units, *kept, *row_sends],
        scratch_shapes=[pltpu.VMEM((length, features), bf16), pltpu.VMEM((length, features), f32)],
        cost_estimate=cost(23),
        compiler_params=pltpu.CompilerParams(vmem_limit_bytes=56 * 1024 * 1024),
    )(*mlp_pieces, activ_grad, gate_weight, up_weight)
    kept, sends = sends[: len(kept)], sends[len(kept) :]
    beside = ()
    if line:
        grads = down_back(core_id, cots, down_weight, (sends[0],))
        beside = (grads,)
    addends = scatter_row(sends, square, beside)

    mlp_gain_part, resid_grad, one, two = run(
        functools.partial(norm_back_kernel, final=False),
        [shape((1, features), f32), shape((block, features), f32), *halves],
        (hidden, cotangent, gain_two, *addends),
    )
    (out_part,) = run(
        functools.partial(down_kernel, plain=plain), [row_low], (spot, activ, down_weight), after=(one,), scalar=True, micros=6
    )
    mlp_out = lax.psum_scatter(out_part, ("y", "x"), scatter_dimension=0, tiled=True)
    cot_pieces = gather_row((one, two), square, (out_part,) if square else ())

    cot_mine, cot_theirs, branch_low, state_grad = run(
        functools.partial(branch_back_kernel, count=len(cot_pieces)),
        [half_row, half_row, token_low, token],
        (where, *cot_pieces, output_weight, branch_pre, state),
        [pltpu.VMEM((length, features), bf16)],
        scalar=True,
        micros=6,
    )
    normed_other = sibling(normed_theirs)
    output_half, branch_half = run(
        pairs_kernel,
        [shape((width, features // 2), bf16), shape((features // 2, width), bf16)],
        (
            gated,
            sibling(gated),
            cot_mine,
            sibling(cot_theirs),
            normed_mine,
            normed_other,
            branch_low,
            sibling(branch_low),
        ),
    )
    packed = shape((head + 8, width), f32)
    stream_low, flat_mine, flat_theirs, norm_gain_part, one_part = run(
        functools.partial(backward_kernel, head=head, plain=plain),
        [token_low, packed, packed, shape((1, features), f32), row_low],
        (
            where,
            state_grad,
            branch_low,
            branch_weight,
            stream_weight,
            stream_pre,
            joined,
            convolved,
            recur_gate,
            intake_gate,
            state,
            taps,
            wide_high,
            soft,
            normed_mine,
            normed_theirs,
            gain_one,
        ),
        [
            pltpu.VMEM((2, width, width), f32),
            pltpu.VMEM((8, width), f32),
            pltpu.VMEM((2, length, width), bf16),
            pltpu.VMEM((length, width), bf16),
            pltpu.VMEM((length + 8, width), f32),
        ],
        after=(output_half, branch_half),
        scalar=True,
        micros=18,
    )
    gains = jnp.concatenate([norm_gain_part, mlp_gain_part], axis=1).reshape(8, -1)
    if line:
        moved = line_move([(output_half, 0)])
        (output_sum,) = line_settle(moved, (stream_low,))
        branch_half, stream_low, flat_mine, flat_theirs, one_part, gains = held(
            (branch_half, stream_low, flat_mine, flat_theirs, one_part, gains), (output_sum,)
        )
        moved = line_move([(output_sum, 1), (branch_half, 0)])
        gains_other = lax.ppermute(gains, "x", swap)
    (stream_half,) = run(
        pairs_kernel,
        [shape((features // 2, width), bf16)],
        (normed_mine, normed_other, stream_low, sibling(stream_low)),
        micros=3,
    )
    one_grad = lax.psum_scatter(one_part, ("y", "x"), scatter_dimension=0, tiled=True)

    gate_low = ()
    if line:
        small = [shape(gains.shape, f32)]
        (gains,) = run(add_one_kernel, small, (gains, gains_other))
        gains_other = lax.ppermute(gains, "y", swap)
        (gains,) = run(add_one_kernel, small, (gains, gains_other), after=(stream_half,))
        flat_other, gains_other = sibling(flat_theirs), sibling(gains)
        rows_a = mlp_rows(tokens, grads, gate_turned, up_turned, 0, (), (stream_half, gains))
        output_sum, branch_sum = line_settle(moved, rows_a[:1])
        (flat,) = run(
            sum_kernel,
            [shape((packed.shape[0] + 8, width), bf16)],
            (flat_mine, flat_other, gains, gains_other),
            after=rows_a[:1],
        )
        moved = line_move([(output_sum, 2), (branch_sum, 1), (stream_half, 0), (flat, 0)])
        activ_all, gate_all, up_all = mlp_rows(
            tokens, grads, gate_turned, up_turned, 1, rows_a, (branch_sum, flat)
        )
        gate_low, gate_w_grad = product(gate_all, tokens, core_id, True)
        output_sum, branch_sum, stream_sum, flat_sum = line_settle(moved, (gate_low,))
        moved = line_move([(branch_sum, 2), (stream_sum, 1), (flat_sum, 1)])
        (gate_sent,) = held((gate_low,), (stream_sum,))
        up_low, up_w_grad = product(up_all, tokens, core_id, True, (branch_sum, stream_sum))
        gate_low = (up_low,)
    else:
        (flat,) = run(sum_kernel, [packed], (flat_mine, sibling(flat_theirs)))

    (inputs_grad,) = run(
        functools.partial(norm_back_kernel, final=True),
        [shape((block, features), bf16)],
        (inputs, resid_grad, gain_one, one_grad),
        after=gate_low,
    )
    (block_out,) = run(
        add_kernel, [shape((block, features), bf16)], (hidden, mlp_out), after=gate_low
    )

    def whole(own, axis, after=()):
        return joined_halves(own, sibling(own), core_id, axis, after)

    if line:
        gate_w_grad = filled(gate_w_grad, sibling(gate_sent), core_id, True, (inputs_grad, block_out))
        branch_sum, stream_sum, flat_sum = line_settle(moved, (gate_w_grad,))
        moved = line_move([(stream_sum, 2), (flat_sum, 2)])
        (up_sent,) = held((up_low,), (stream_sum,))
        down_low, down_w_grad = product(activ_all, cots, core_id, False, (stream_sum, flat_sum))
        up_w_grad = filled(up_w_grad, sibling(up_sent), core_id, True, (down_low,))
        output_w_grad = whole(output_sum, 1, (up_w_grad,))
        branch_w_grad = whole(branch_sum, 0, (output_w_grad,))
        stream_sum, flat_sum = line_settle(moved, (branch_w_grad,))
        (down_sent,) = held((down_low,), (stream_sum,))
        stream_w_grad = whole(stream_sum, 0)
        down_w_grad = filled(down_w_grad, sibling(down_sent), core_id, False, (flat_sum,))
        gains = flat_sum[packed.shape[0] :, : features // 4].astype(f32)
    else:
        gains = lax.psum(gains, ALL)
        output_sum, branch_sum, stream_sum, flat_sum = (
            lax.psum(part, "z") for part in (output_half, branch_half, stream_half, flat)
        )
        output_w_grad, branch_w_grad, stream_w_grad = (
            whole(output_sum, 1),
            whole(branch_sum, 0),
            whole(stream_sum, 0),
        )

        def over_rows(left, right):
            part = lax.dot_general(left, right, contract_rows, preferred_element_type=f32)
            return lax.psum(part.astype(bf16), ("z", "core")).astype(f32)

        gate_w_grad = over_rows(mlp_in, kept[0])
        up_w_grad = over_rows(mlp_in, kept[1])
        down_w_grad = over_rows(activ, jnp.concatenate(own_cots, axis=0))

    sums = flat_sum[head : head + 8].astype(f32)
    gates = flat_sum[:head]
    gates_other = sibling(gates)

    def heads_of(blocks):
        return blocks.reshape(head, heads, head).transpose(1, 0, 2).astype(f32)

    gains = gains.reshape(2, -1)
    return (
        block_out,
        inputs_grad,
        gains[0],
        branch_w_grad,
        stream_w_grad,
        sums[0:4],
        sums[4],
        heads_of(jnp.where(core == 0, gates, gates_other)),
        sums[5],
        heads_of(jnp.where(core == 0, gates_other, gates)),
        sums[6],
        sums[7] * decay_scale * jax.nn.sigmoid(-decay_param),
        output_w_grad,
        gains[1],
        gate_w_grad,
        up_w_grad,
        down_w_grad,
    )


def solution(mesh):
    depth = mesh.shape["dp"] // 2
    across = mesh.shape["mp"] // 2
    fine = Mesh(mesh.devices.reshape(depth, 2, 2, across), ALL)
    dp, mp = ("z", "core"), ("y", "x")
    cols, vec, blocks, rows = P(None, mp), P(mp), P(mp, None, None), P(mp, None)
    tokens = P(ALL, None)
    return jax.shard_map(
        functools.partial(local, depth=depth, square=across == 2),
        mesh=fine,
        in_specs=(
            tokens,
            tokens,
            P(dp, None),
            P(),
            cols,
            cols,
            cols,
            vec,
            blocks,
            vec,
            blocks,
            vec,
            vec,
            rows,
            P(),
            cols,
            cols,
            rows,
        ),
        out_specs=(
            tokens,
            tokens,
            P(),
            cols,
            cols,
            cols,
            vec,
            blocks,
            vec,
            blocks,
            vec,
            vec,
            rows,
            P(),
            cols,
            cols,
            rows,
        ),
        check_vma=False,
    )
```

```python
import functools

import jax
import jax.numpy as jnp
from jax import lax
from jax.experimental import pallas as pl
from jax.experimental.pallas import tpu as pltpu
from jax.sharding import Mesh
from jax.sharding import PartitionSpec as P

eps = 1e-06
decay_scale = 8.0
contract_rows = (((0,), (0,)), ((), ()))
contract_cols = (((1,), (1,)), ((), ()))
f32 = jnp.float32
bf16 = jnp.bfloat16
swap = [(0, 1), (1, 0)]


def cost(micros):
    return pl.CostEstimate(flops=0, bytes_accessed=int(micros * 3e6), transcendentals=0)


brief = cost(1)
large = pltpu.CompilerParams(vmem_limit_bytes=48 * 1024 * 1024)
middle = pltpu.CompilerParams(vmem_limit_bytes=32 * 1024 * 1024)
ALL = ("z", "core", "y", "x")
STEP = 16
root_two_over_pi = 0.7978845608028654


def pass_kernel(*refs):
    pass


def held(values, after):
    values, after = list(values), list(after)
    anywhere = pl.BlockSpec(memory_space=pl.ANY)
    return pl.pallas_call(
        pass_kernel,
        in_specs=[anywhere] * (len(values) + len(after)),
        out_specs=[anywhere] * len(values),
        out_shape=[jax.ShapeDtypeStruct(value.shape, value.dtype) for value in values],
        input_output_aliases={n: n for n in range(len(values))},
        cost_estimate=cost(0.1),
    )(*values, *after)


def gather_row(halves, square, beside=()):
    if not square:
        return [lax.all_gather(jnp.concatenate(halves, axis=0), ("y", "x"), axis=0, tiled=True)]
    one, two = halves
    one_x = lax.ppermute(one, "x", swap)
    two_y = lax.ppermute(two, "y", swap)
    two_x = lax.ppermute(two, "x", swap)
    one_y = lax.ppermute(one, "y", swap)
    if beside:
        one_x, two_y = held((one_x, two_y), beside)
    one_d = lax.ppermute(one_x, "y", swap)
    two_d = lax.ppermute(two_y, "x", swap)
    return [one, one_x, one_y, one_d, two, two_x, two_y, two_d]


def gather_blocks(block, square):
    if not square:
        return gather_row((block,), square)
    return [
        block,
        lax.ppermute(block, "x", swap),
        lax.ppermute(block, "y", swap),
        lax.ppermute(block, ("y", "x"), [(0, 3), (3, 0), (1, 2), (2, 1)]),
    ]


def scatter_row(sends, square, beside=()):
    if not square:
        return [lax.psum_scatter(sends[0], ("y", "x"), scatter_dimension=0, tiled=True)]
    to_x, to_y, keep_x, keep_y, own = sends
    got_x = lax.ppermute(to_x, "x", swap)
    got_y = lax.ppermute(to_y, "y", swap)
    if beside:
        got_x, got_y = held((got_x, got_y), beside)
    send_y, send_x = run(
        middle_kernel,
        [jax.ShapeDtypeStruct(keep_x.shape, bf16)] * 2,
        (got_x, got_y, keep_x, keep_y),
    )
    last_y = lax.ppermute(send_y, "y", swap)
    last_x = lax.ppermute(send_x, "x", swap)
    return [own, got_x, got_y, last_y, last_x]


def sibling(value):
    return lax.ppermute(value, "core", swap)


def line_move(pieces):
    pairs = [[(0, 1), (3, 2)], [(1, 2), (2, 1)], [(1, 0), (2, 3)]]
    return [(piece, stage, lax.ppermute(piece, "z", pairs[stage])) for piece, stage in pieces]


def settle_kernel(inner_ref, *refs, stages):
    count = len(stages)
    for n, stage in enumerate(stages):
        piece, other, out = refs[n], refs[count + n], refs[2 * count + n]
        if stage < 2:
            out[...] = (piece[...].astype(f32) + other[...].astype(f32)).astype(out.dtype)
        else:
            out[...] = jnp.where(inner_ref[0] == 1, piece[...], other[...])


def line_settle(moved, after):
    place = lax.axis_index("z")
    inner = ((place == 1) | (place == 2)).astype(jnp.int32).reshape((1,))
    pieces, stages, others = zip(*moved, strict=True)
    blocks = [
        pl.BlockSpec((piece.shape[0] // 4, piece.shape[1]), lambda n, inner: (n, 0)) for piece in pieces
    ]

    def body(inner_ref, *refs):
        settle_kernel(inner_ref, *refs[: 2 * len(pieces)], *refs[-len(pieces) :], stages=stages)

    return pl.pallas_call(
        body,
        grid_spec=pltpu.PrefetchScalarGridSpec(
            num_scalar_prefetch=1,
            grid=(4,),
            in_specs=[*blocks, *blocks] + [pl.BlockSpec(memory_space=pl.ANY)] * len(after),
            out_specs=blocks,
        ),
        out_shape=[jax.ShapeDtypeStruct(piece.shape, piece.dtype) for piece in pieces],
        cost_estimate=brief,
        compiler_params=large,
    )(inner, *pieces, *others, *after)


def assemble(pieces, out_ref):
    at = 0
    for piece in pieces:
        out_ref[at : at + piece.shape[0], :] = piece[...]
        at += piece.shape[0]


def split(whole_ref, core, mine_ref, theirs_ref):
    size = mine_ref.shape[1]
    for ref, which in ((mine_ref, core), (theirs_ref, 1 - core)):
        ref[...] = whole_ref[:, pl.ds(pl.multiple_of(which * size, 128), size)]


def pairs_kernel(*refs):
    count = len(refs) // 5
    for n in range(count):
        own_left, other_left, own_right, other_right = refs[4 * n : 4 * n + 4]
        out_ref = refs[4 * count + n]
        cols = out_ref.shape[1]
        for first in range(0, cols, 512):
            span = slice(first, min(first + 512, cols))
            out_ref[:, span] = (
                lax.dot_general(
                    own_left[...], own_right[:, span], contract_rows, preferred_element_type=f32
                )
                + lax.dot_general(
                    other_left[...], other_right[:, span], contract_rows, preferred_element_type=f32
                )
            ).astype(bf16)


def sum_kernel(one_ref, two_ref, out_ref):
    out_ref[...] = (one_ref[...] + two_ref[...]).astype(out_ref.dtype)


def below_kernel(top_ref, one_ref, two_ref, out_ref):
    rows = top_ref.shape[0]
    out_ref[:rows, :] = top_ref[...]
    out_ref[rows:, :] = (one_ref[...] + two_ref[...]).astype(out_ref.dtype)


def send_shapes(length, width, plain):
    if plain:
        return [jax.ShapeDtypeStruct((length, width), bf16)]
    block, cut = length // 4, width // 2
    return (
        [jax.ShapeDtypeStruct((2 * block, cut), bf16)] * 2
        + [jax.ShapeDtypeStruct((block, cut), bf16)] * 2
        + [jax.ShapeDtypeStruct((block, width), f32)]
    )


def emit(value, first, width, sends, plain, spot=None):
    last = first + value.shape[1]
    if spot is not None:
        half = value.shape[0] // 8
        for n in range(2):
            for k in range(4):
                start = pl.multiple_of((lax.bitwise_xor(k, spot) * 2 + n) * half, half)
                block = value[(n * 4 + k) * half : (n * 4 + k + 1) * half]
                sends[0][pl.ds(start, half), first:last] = block.astype(bf16)
        return
    if plain:
        sends[0][:, first:last] = value.astype(bf16)
        return
    to_x, to_y, keep_x, keep_y, own = sends
    cut = width // 2
    half = value.shape[0] // 8

    def put(ref, at, block, cols, kind):
        for n in range(2):
            rows = slice(n * 4 * half + block * half, n * 4 * half + (block + 1) * half)
            ref[at + n * half : at + (n + 1) * half, cols] = value[rows].astype(kind)

    put(own, 0, 0, slice(first, last), f32)
    if last <= cut:
        cols = slice(first, last)
        put(to_x, 0, 1, cols, bf16)
        put(to_x, 2 * half, 3, cols, bf16)
        put(keep_y, 0, 2, cols, bf16)
    else:
        cols = slice(first - cut, last - cut)
        put(to_y, 0, 2, cols, bf16)
        put(to_y, 2 * half, 3, cols, bf16)
        put(keep_x, 0, 1, cols, bf16)


def middle_kernel(got_x, got_y, keep_x, keep_y, send_y, send_x):
    block = keep_x.shape[0]
    send_y[...] = (keep_y[...].astype(f32) + got_x[block:].astype(f32)).astype(bf16)
    send_x[...] = (keep_x[...].astype(f32) + got_y[block:].astype(f32)).astype(bf16)


def finish(refs):
    if len(refs) == 1:
        return refs[0][...].astype(f32)
    own, got_x, got_y, last_y, last_x = refs
    block, cut = last_y.shape
    left = own[:, :cut] + got_x[:block].astype(f32) + last_y[...].astype(f32)
    right = own[:, cut:] + got_y[:block].astype(f32) + last_x[...].astype(f32)
    return jnp.concatenate([left, right], axis=1)


def mean_of(x):
    return jnp.mean(x, axis=-1, keepdims=True)


def norm_kernel(input_ref, gain_ref, one_ref, two_ref):
    values = input_ref[...].astype(f32)
    normed = (values * lax.rsqrt(mean_of(values * values) + eps) * gain_ref[...]).astype(bf16)
    half = normed.shape[0] // 2
    one_ref[...] = normed[:half]
    two_ref[...] = normed[half:]


def second_norm_kernel(input_ref, gain_ref, *refs):
    addends, (hidden_ref, one_ref, two_ref, all_ref) = refs[:-4], refs[-4:]
    hidden = input_ref[...].astype(f32) + finish(addends)
    hidden_ref[...] = hidden
    normed = (hidden * lax.rsqrt(mean_of(hidden * hidden) + eps) * gain_ref[...]).astype(bf16)
    half = normed.shape[0] // 2
    one_ref[...] = normed[:half]
    two_ref[...] = normed[half:]
    all_ref[...] = normed


def norm_back_kernel(value_ref, before_ref, gain_ref, *refs, final):
    outs = 1 if final else 4
    addends, outs = refs[:-outs], refs[-outs:]
    values = value_ref[...].astype(f32)
    scale = lax.rsqrt(mean_of(values * values) + eps)
    hat = values * scale
    grad = finish(addends)
    scaled = grad * gain_ref[...]
    total = before_ref[...].astype(f32) + scale * (scaled - hat * mean_of(scaled * hat))
    if final:
        outs[0][...] = total.astype(bf16)
        return
    outs[0][...] = jnp.sum(grad * hat, axis=0, keepdims=True)
    outs[1][...] = total
    low = total.astype(bf16)
    half = low.shape[0] // 2
    outs[2][...] = low[:half]
    outs[3][...] = low[half:]


def add_kernel(value_ref, *refs):
    refs[-1][...] = (value_ref[...] + finish(refs[:-1])).astype(bf16)


def mlp_kernel(*refs, count, plain, keep):
    pieces, (grad_ref, gate_w, up_w), refs = refs[:count], refs[count : count + 3], refs[count + 3 :]
    *outs, token_ref, total_ref = refs
    token_out, activ_ref, *outs = outs
    step = pl.program_id(0)

    @pl.when(step == 0)
    def _():
        assemble(pieces, token_ref)
        token_out[...] = token_ref[...]

    tokens = token_ref[...]
    gate_pre = jnp.dot(tokens, gate_w[...], preferred_element_type=f32)
    up_pre = jnp.dot(tokens, up_w[...], preferred_element_type=f32)
    activ_grad = grad_ref[...]
    value, slope = gelu_terms(gate_pre)
    activ_ref[...] = (value * up_pre).astype(bf16)
    gate_low = (activ_grad * up_pre * slope).astype(bf16)
    up_low = (activ_grad * value).astype(bf16)
    if keep:
        outs[0][...] = gate_low
        outs[1][...] = up_low
        outs = outs[2:]
    width = total_ref.shape[1]
    last = step == pl.num_programs(0) - 1
    for first in range(0, width, 512):
        cols = slice(first, first + 512)
        part = lax.dot_general(
            gate_low, gate_w[cols, :], contract_cols, preferred_element_type=f32
        ) + lax.dot_general(up_low, up_w[cols, :], contract_cols, preferred_element_type=f32)

        @pl.when(step == 0)
        def _(part=part, cols=cols):
            total_ref[:, cols] = part

        @pl.when(step > 0)
        def _(part=part, cols=cols):
            total_ref[:, cols] += part

    @pl.when(last)
    def _():
        for first in range(0, width, 512):
            emit(total_ref[:, first : first + 512], first, width, outs, plain)


def down_kernel(spot_ref, activ_ref, weight_ref, *sends, plain):
    spot = None if plain else spot_ref[0]
    width = weight_ref.shape[1]
    for first in range(0, width, 512):
        cols = slice(first, first + 512)
        value = jnp.dot(activ_ref[...], weight_ref[:, cols], preferred_element_type=f32)
        emit(value, first, width, sends, plain, spot)


def tile_span(first, last, head, width):
    low = (first // head) * head // 128 * 128
    high = min(width, -(-(((last - 1) // head + 1) * head) // 128) * 128)
    return low, high


def tiles(width):
    return [(n, min(n + 256, width)) for n in range(0, width, 256)]


def sigmoid(x):
    return 1.0 / (1.0 + jnp.exp(-x))


def decay_terms(gate, soft, link):
    log_decay = gate * soft
    decay = jnp.exp(log_decay)
    square = decay * decay
    x = 2.0 * log_decay
    series = 1.0 + x * (1.0 / 6.0) * (1.0 + x * (1.0 / 7.0))
    series = 1.0 + x * (1.0 / 4.0) * (1.0 + x * (1.0 / 5.0) * series)
    series = -x * (1.0 + x * (1.0 / 2.0) * (1.0 + x * (1.0 / 3.0) * series))
    gap = jnp.where(x > -0.3, series, 1.0 - square)
    root = jnp.sqrt(gap)
    return link * decay, square, root, link * root + (1.0 - link)


def gelu_terms(x):
    inner = jnp.tanh(root_two_over_pi * (x + 0.044715 * x * x * x))
    value = 0.5 * x * (1.0 + inner)
    slope = 0.5 * (1.0 + inner) + 0.5 * x * (1.0 - inner * inner) * root_two_over_pi * (
        1.0 + 3.0 * 0.044715 * x * x
    )
    return value, slope


def widen(mask, width):
    return jnp.concatenate([mask] * (-(-width // 128)), axis=1)[:, :width]


def token_place(length, spot, plain):
    block, half = length // 4, length // 8
    per_block = block // STEP
    per_half = half // STEP

    def offset(step):
        if plain:
            return pl.multiple_of(step * STEP, STEP)
        turn = lax.bitwise_xor(step // per_block, spot)
        inside = lax.rem(step, per_block)
        at = (inside // per_half) * (length // 2) + turn * half + lax.rem(inside, per_half) * STEP
        return pl.multiple_of(at, STEP)

    return offset


def prep_kernel(recur_ref, intake_ref, high_ref, low_ref):
    count, size, _ = recur_ref.shape
    for which, ref in ((0, recur_ref), (1, intake_ref)):
        for h in range(count):
            parts = [ref[h]]
            if h:
                parts.insert(0, jnp.zeros((size, h * size), f32))
            if h < count - 1:
                parts.append(jnp.zeros((size, (count - 1 - h) * size), f32))
            row = jnp.concatenate(parts, axis=1)
            high = row.astype(bf16)
            rows = slice(h * size, (h + 1) * size)
            high_ref[which, rows, :] = high
            low_ref[which, rows, :] = (row - high.astype(f32)).astype(bf16)


def forward_kernel(spot_ref, *refs, count, head, plain):
    pieces, refs = refs[:count], refs[count:]
    (branch_w, stream_w, output_w, joined_ref, taps_ref, bias_ref, high_ref, low_ref, gate_bias_ref, soft_ref), refs = (
        refs[:10],
        refs[10:],
    )
    (mine_ref, theirs_ref, branch_ref, stream_ref, gated_ref, conv_ref, recur_ref, intake_ref, state_ref), refs = (
        refs[:9],
        refs[9:],
    )
    *sends, part_high, part_low, normed_ref = refs
    assemble(pieces, normed_ref)
    split(normed_ref, spot_ref[1], mine_ref, theirs_ref)
    for first, last in tiles(branch_ref.shape[1]):
        cols = slice(first, last)
        branch_ref[:, cols] = jnp.dot(normed_ref[...], branch_w[:, cols], preferred_element_type=f32)
        stream_ref[:, cols] = jnp.dot(normed_ref[...], stream_w[:, cols], preferred_element_type=f32)
    length, width = branch_ref.shape
    steps = length // STEP
    offset = token_place(length, spot_ref[0], plain)

    def convolve(step, before):
        at = offset(step)
        here = pl.multiple_of(step * STEP, STEP)
        now = stream_ref[pl.ds(at, STEP), :]
        both = jnp.concatenate([before, now], axis=0)
        total = bias_ref[0:1, :] + taps_ref[0:1, :] * now
        for k in range(1, 4):
            mask = widen(joined_ref[k - 1, pl.ds(here, STEP), :], width)
            total = total + taps_ref[k : k + 1, :] * both[8 - k : 8 - k + STEP] * mask
        conv_ref[pl.ds(at, STEP), :] = total
        high = total.astype(bf16)
        part_high[pl.ds(here, STEP), :] = high
        part_low[pl.ds(here, STEP), :] = (total - high.astype(f32)).astype(bf16)
        return now[STEP - 8 :]

    lax.fori_loop(0, steps, convolve, jnp.zeros((8, width), f32), unroll=2)

    for which, out_ref in ((0, recur_ref), (1, intake_ref)):
        for first, last in tiles(width):
            low, high = tile_span(first, last, head, width)
            span, cols = slice(low, high), slice(first, last)
            high_part, low_part = high_ref[which, span, cols], low_ref[which, span, cols]
            pre = (
                jnp.dot(part_high[:, span], high_part, preferred_element_type=f32)
                + jnp.dot(part_low[:, span], high_part, preferred_element_type=f32)
                + jnp.dot(part_high[:, span], low_part, preferred_element_type=f32)
            )
            out_ref[:, cols] = pre + gate_bias_ref[which : which + 1, cols]

    rows = lax.broadcasted_iota(jnp.int32, (8, width), 0)
    soft = soft_ref[0:1, :]

    def advance(step, last_state):
        at = offset(step)
        here = pl.multiple_of(step * STEP, STEP)
        link = widen(joined_ref[0, pl.ds(here, STEP), :], width)
        conv = conv_ref[pl.ds(at, STEP), :]
        recur = sigmoid(recur_ref[pl.ds(here, STEP), :])
        intake = sigmoid(intake_ref[pl.ds(here, STEP), :])
        recur_ref[pl.ds(here, STEP), :] = recur
        intake_ref[pl.ds(here, STEP), :] = intake
        carried, square, root, multiplier = decay_terms(recur, soft, link)
        driven = multiplier * intake * conv
        found = []
        for part in range(STEP // 8):
            a = carried[8 * part : 8 * part + 8]
            b = driven[8 * part : 8 * part + 8]
            for shift in (1, 2, 4):
                a_before = jnp.where(rows >= shift, pltpu.roll(a, shift, 0), 1.0)
                b_before = jnp.where(rows >= shift, pltpu.roll(b, shift, 0), 0.0)
                b = b + a * b_before
                a = a * a_before
            state = b + a * last_state
            last_state = state[7:8]
            found.append(state)
        state = jnp.concatenate(found, axis=0)
        state_ref[pl.ds(at, STEP), :] = state
        value, slope = gelu_terms(branch_ref[pl.ds(at, STEP), :])
        gated_ref[pl.ds(at, STEP), :] = (value * state).astype(bf16)
        return last_state

    lax.fori_loop(0, steps, advance, jnp.zeros((1, width), f32), unroll=2)
    step_cols = 512
    for first in range(0, output_w.shape[1], step_cols):
        cols = slice(first, first + step_cols)
        value = jnp.dot(gated_ref[...], output_w[:, cols], preferred_element_type=f32)
        emit(value, first, output_w.shape[1], sends, plain)


def branch_back_kernel(spot_ref, *refs, count):
    pieces, (output_w, branch_ref, state_ref), refs = refs[:count], refs[count : count + 3], refs[count + 3 :]
    mine_ref, theirs_ref, branch_grad_ref, grad_ref, cot_ref = refs
    assemble(pieces, cot_ref)
    split(cot_ref, spot_ref[1], mine_ref, theirs_ref)
    length, width = branch_ref.shape
    for first, last in tiles(width):
        cols = slice(first, last)
        grad_ref[:, cols] = lax.dot_general(
            cot_ref[...], output_w[cols, :], contract_cols, preferred_element_type=f32
        )

    def rows(step, _):
        at = pl.ds(pl.multiple_of(step * STEP, STEP), STEP)
        value, slope = gelu_terms(branch_ref[at, :])
        grad = grad_ref[at, :]
        branch_grad_ref[at, :] = (grad * state_ref[at, :] * slope).astype(bf16)
        grad_ref[at, :] = grad * value
        return _

    lax.fori_loop(0, length // STEP, rows, 0)


def backward_kernel(
    spot_ref,
    grad_ref,
    branch_grad_ref,
    branch_w,
    stream_w,
    stream_ref,
    joined_ref,
    conv_ref,
    recur_ref,
    intake_ref,
    state_ref,
    taps_ref,
    high_ref,
    soft_ref,
    normed_mine,
    normed_theirs,
    gain_ref,
    other_gains,
    stream_grad_ref,
    mine_ref,
    theirs_ref,
    *refs,
    head,
    plain,
):
    *sends, gates_ref, sums_ref, pre_ref, conv_low, conv_grad = refs
    length, width = grad_ref.shape
    steps = length // STEP
    offset = token_place(length, spot_ref[0], plain)

    rows = lax.broadcasted_iota(jnp.int32, (8, width), 0)
    soft = soft_ref[0:1, :]
    count = STEP // 8

    def fold(value):
        total = value[0:8]
        for part in range(1, count):
            total = total + value[8 * part : 8 * part + 8]
        return total

    def retreat(turn, kept):
        after_carried, after_adjoint, decay_sum, recur_sum, intake_sum = kept
        step = steps - 1 - turn
        at = offset(step)
        at_before = offset(jnp.maximum(step - 1, 0))
        here = pl.multiple_of(step * STEP, STEP)
        link = widen(joined_ref[0, pl.ds(here, STEP), :], width)
        conv = conv_ref[pl.ds(at, STEP), :]
        recur = recur_ref[pl.ds(here, STEP), :]
        intake = intake_ref[pl.ds(here, STEP), :]
        carried, square, root, multiplier = decay_terms(recur, soft, link)
        grad = grad_ref[pl.ds(at, STEP), :]
        found = []
        for part in reversed(range(count)):
            own = carried[8 * part : 8 * part + 8]
            a = jnp.where(rows < 7, pltpu.roll(own, 7, 0), after_carried)
            b = grad[8 * part : 8 * part + 8]
            for shift in (1, 2, 4):
                a_after = jnp.where(rows < 8 - shift, pltpu.roll(a, 8 - shift, 0), 1.0)
                b_after = jnp.where(rows < 8 - shift, pltpu.roll(b, 8 - shift, 0), 0.0)
                b = b + a * b_after
                a = a * a_after
            adjoint = b + a * after_adjoint
            after_adjoint = adjoint[0:1]
            after_carried = own[0:1]
            found.append(adjoint)
        adjoint = jnp.concatenate(found[::-1], axis=0)
        state = state_ref[pl.ds(at, STEP), :]
        tail = state_ref[pl.ds(at_before + (STEP - 8), 8), :]
        earlier = jnp.concatenate([tail, state], axis=0)[7 : 7 + STEP]
        driven_part = adjoint * intake
        log_grad = adjoint * earlier * carried - driven_part * conv * link * square / root
        recur_grad = log_grad * soft * recur * (1.0 - recur)
        spread = driven_part * multiplier
        intake_grad = spread * conv * (1.0 - intake)
        pre_ref[0, pl.ds(here, STEP), :] = recur_grad.astype(bf16)
        pre_ref[1, pl.ds(here, STEP), :] = intake_grad.astype(bf16)
        conv_low[pl.ds(here, STEP), :] = conv.astype(bf16)
        conv_grad[pl.ds(here, STEP), :] = spread
        return (
            after_carried,
            after_adjoint,
            decay_sum + fold(log_grad * recur),
            recur_sum + fold(recur_grad),
            intake_sum + fold(intake_grad),
        )

    line = jnp.zeros((1, width), f32)
    eight = jnp.zeros((8, width), f32)
    kept = lax.fori_loop(0, steps, retreat, (line, line, eight, eight, eight), unroll=2)
    sums_ref[5:6, :] = jnp.sum(kept[3], axis=0, keepdims=True)
    sums_ref[6:7, :] = jnp.sum(kept[4], axis=0, keepdims=True)
    sums_ref[7:8, :] = jnp.sum(kept[2], axis=0, keepdims=True)

    conv_grad[length : length + 8, :] = eight
    for first, last in tiles(width):
        low, high = tile_span(first, last, head, width)
        span, cols = slice(low, high), slice(first, last)
        total = conv_grad[0:length, cols]
        for which in range(2):
            total = total + lax.dot_general(
                pre_ref[which, :, span], high_ref[which, cols, span], contract_cols, preferred_element_type=f32
            )
            gates_ref[which, span, cols] = lax.dot_general(
                conv_low[:, span], pre_ref[which, :, cols], contract_rows, preferred_element_type=f32
            )
        conv_grad[0:length, cols] = total

    def unwind(step, kept):
        at = offset(step)
        here = pl.multiple_of(step * STEP, STEP)
        ahead = conv_grad[pl.ds(here, STEP + 8), :]
        now = stream_ref[pl.ds(at, STEP), :]
        total = taps_ref[0:1, :] * ahead[0:STEP]
        sums = [kept[0] + fold(ahead[0:STEP] * now)]
        for k in range(1, 4):
            mask = widen(joined_ref[k - 1, pl.ds(here, STEP + 8), :], width)
            moved = (ahead * mask)[k : k + STEP]
            total = total + taps_ref[k : k + 1, :] * moved
            sums.append(kept[k] + fold(moved * now))
        stream_grad_ref[pl.ds(at, STEP), :] = total.astype(bf16)
        return (*sums, kept[4] + fold(ahead[0:STEP]))

    kept = lax.fori_loop(0, steps, unwind, (eight,) * 5, unroll=2)
    for k in range(5):
        sums_ref[k : k + 1, :] = jnp.sum(kept[k], axis=0, keepdims=True)
    count = width // head
    lanes = lax.broadcasted_iota(jnp.int32, (head, width), 1)
    for out_ref, which in ((mine_ref, spot_ref[1]), (theirs_ref, 1 - spot_ref[1])):
        blocks = gates_ref[which, 0:head, :]
        for h in range(1, count):
            blocks = jnp.where(lanes >= h * head, gates_ref[which, h * head : (h + 1) * head, :], blocks)
        out_ref[0:head, :] = blocks
        out_ref[head : head + 8, :] = sums_ref[...]
        out_ref[head + 8 :, :] = jnp.zeros((out_ref.shape[0] - head - 8, width), f32)

    step_cols = 512
    for first in range(0, branch_w.shape[0], step_cols):
        cols = slice(first, first + step_cols)
        value = lax.dot_general(
            branch_grad_ref[...], branch_w[cols, :], contract_cols, preferred_element_type=f32
        ) + lax.dot_general(
            stream_grad_ref[...], stream_w[cols, :], contract_cols, preferred_element_type=f32
        )
        half = normed_mine.shape[1]
        inside = slice(first % half, first % half + step_cols)
        mine = spot_ref[1] == first // half
        normed = jnp.where(mine, normed_mine[:, inside], normed_theirs[:, inside]).astype(f32)
        gains = jnp.sum(value * normed, axis=0, keepdims=True) / gain_ref[:, cols]
        for part in range(step_cols // 256):
            row = head + 8 + first // 256 + part
            below = row + branch_w.shape[0] // 256
            at = slice(part * 256, (part + 1) * 256)
            for out_ref in (mine_ref, theirs_ref):
                out_ref[row : row + 1, 0:256] = gains[:, at]
                out_ref[below : below + 1, 0:256] = other_gains[:, cols][:, at]
        emit(value, first, branch_w.shape[0], sends, plain, None if plain else spot_ref[0])


def rows_kernel(token_ref, grad_ref, gate_ref, up_ref, *rest):
    activ_ref, gate_out, up_out = rest[-3:]
    tokens = token_ref[...]
    hidden = gate_ref.shape[0]
    part = hidden // 3
    for n in range(3):
        rows = slice(n * part, (n + 1) * part)
        gate_pre = lax.dot_general(gate_ref[rows], tokens, contract_cols, preferred_element_type=f32)
        up_pre = lax.dot_general(up_ref[rows], tokens, contract_cols, preferred_element_type=f32)
        activ_grad = grad_ref[rows]
        value, slope = gelu_terms(gate_pre)
        activ_ref[rows] = (value * up_pre).astype(bf16)
        gate_out[rows] = (activ_grad * up_pre * slope).astype(bf16)
        up_out[rows] = (activ_grad * value).astype(bf16)


def mlp_rows(tokens, grads, gate, up, after):
    count, width = tokens.shape
    hidden = gate.shape[0]
    tile = 512
    tall = pl.BlockSpec((hidden, tile), lambda i: (0, i))
    weight = pl.BlockSpec((hidden, width), lambda i: (0, 0))
    return pl.pallas_call(
        rows_kernel,
        grid=(count // tile,),
        in_specs=[pl.BlockSpec((tile, width), lambda i: (i, 0)), tall, weight, weight]
        + [pl.BlockSpec(memory_space=pl.ANY)] * len(after),
        out_specs=[tall, tall, tall],
        out_shape=[jax.ShapeDtypeStruct((hidden, count), bf16)] * 3,
        cost_estimate=cost(34),
        compiler_params=large,
    )(tokens, grads, gate, up, *after)


def row_back_kernel(*refs, count):
    pieces, (weight_ref, out_ref, rows_ref) = refs[:count], refs[count:]

    @pl.when(pl.program_id(0) == 0)
    def _():
        half = pieces[0].shape[0] // 2
        at = 0
        for n in range(2):
            for piece in pieces:
                rows_ref[at : at + half, :] = piece[n * half : (n + 1) * half, :]
                at += half

    out_ref[...] = lax.dot_general(
        rows_ref[...], weight_ref[...], contract_cols, preferred_element_type=f32
    )


def row_back(pieces, down):
    hidden, width = down.shape
    length = sum(piece.shape[0] for piece in pieces)
    tile = min(512, hidden)
    return pl.pallas_call(
        functools.partial(row_back_kernel, count=len(pieces)),
        grid=(hidden // tile,),
        in_specs=[pl.BlockSpec(piece.shape, lambda i: (0, 0)) for piece in pieces]
        + [pl.BlockSpec((tile, width), lambda i: (i, 0))],
        out_specs=pl.BlockSpec((length, tile), lambda i: (0, i)),
        out_shape=jax.ShapeDtypeStruct((length, hidden), f32),
        scratch_shapes=[pltpu.VMEM((length, width), bf16)],
        cost_estimate=cost(6),
        compiler_params=large,
    )(*pieces, down)


def product(left, right, core, turn, after=()):
    rows, depth = left.shape
    cols = right.shape[1]
    tile = 256

    def body(core_ref, left_ref, right_ref, *rest):
        low_ref, whole_ref = rest[-2:]
        low = jnp.dot(left_ref[...], right_ref[...], preferred_element_type=f32).astype(bf16)
        low_ref[...] = low
        wide = low.astype(f32)
        whole_ref[...] = wide.T if turn else wide

    if turn:
        place = pl.BlockSpec((tile, rows), lambda n, core: (n, core[0]))
        shape = (cols, 2 * rows)
    else:
        place = pl.BlockSpec((rows, tile), lambda n, core: (core[0], n))
        shape = (2 * rows, cols)
    return pl.pallas_call(
        body,
        grid_spec=pltpu.PrefetchScalarGridSpec(
            num_scalar_prefetch=1,
            grid=(cols // tile,),
            in_specs=[
                pl.BlockSpec((rows, depth), lambda n, core: (0, 0)),
                pl.BlockSpec((depth, tile), lambda n, core: (0, n)),
            ]
            + [pl.BlockSpec(memory_space=pl.ANY)] * len(after),
            out_specs=[pl.BlockSpec((rows, tile), lambda n, core: (0, n)), place],
        ),
        out_shape=[jax.ShapeDtypeStruct((rows, cols), bf16), jax.ShapeDtypeStruct(shape, f32)],
        cost_estimate=cost(20),
        compiler_params=large,
    )(core, left, right, *after)


def filled(whole, other, core, turn, after=()):
    rows, cols = other.shape
    tile = cols // 2

    def body(core_ref, other_ref, *rest):
        wide = other_ref[...].astype(f32)
        rest[-1][...] = wide.T if turn else wide

    if turn:
        place = pl.BlockSpec((tile, rows), lambda n, core: (n, 1 - core[0]))
    else:
        place = pl.BlockSpec((rows, tile), lambda n, core: (1 - core[0], n))
    return pl.pallas_call(
        body,
        grid_spec=pltpu.PrefetchScalarGridSpec(
            num_scalar_prefetch=1,
            grid=(2,),
            in_specs=[
                pl.BlockSpec((rows, tile), lambda n, core: (0, n)),
            ]
            + [pl.BlockSpec(memory_space=pl.ANY)] * (1 + len(after)),
            out_specs=place,
        ),
        out_shape=jax.ShapeDtypeStruct(whole.shape, f32),
        input_output_aliases={2: 0},
        cost_estimate=cost(4.5),
        compiler_params=large,
    )(core, other, whole, *after)


def join_kernel(core_ref, own_ref, other_ref, *rest):
    mine = pl.program_id(0) == core_ref[0]
    rest[-1][...] = jnp.where(mine, own_ref[...], other_ref[...]).astype(f32)


def joined_halves(own, other, core, axis, after):
    rows, cols = own.shape
    part = pl.BlockSpec((rows, cols), lambda h, core: (0, 0))
    place = pl.BlockSpec((rows, cols), (lambda h, core: (h, 0)) if axis == 0 else (lambda h, core: (0, h)))
    shape = (2 * rows, cols) if axis == 0 else (rows, 2 * cols)
    return pl.pallas_call(
        join_kernel,
        grid_spec=pltpu.PrefetchScalarGridSpec(
            num_scalar_prefetch=1,
            grid=(2,),
            in_specs=[part, part] + [pl.BlockSpec(memory_space=pl.ANY)] * len(after),
            out_specs=place,
        ),
        out_shape=jax.ShapeDtypeStruct(shape, f32),
        cost_estimate=cost(4),
        compiler_params=large,
    )(core, own, other, *after)


def back_kernel(core_ref, weight_ref, cot_ref, *rest):
    rest[-1][...] = lax.dot_general(
        weight_ref[...], cot_ref[...], contract_cols, preferred_element_type=f32
    )


def down_back(core, cots, down, after):
    count, width = cots.shape
    hidden = down.shape[0] // 2
    tile = 512
    return pl.pallas_call(
        back_kernel,
        grid_spec=pltpu.PrefetchScalarGridSpec(
            num_scalar_prefetch=1,
            grid=(count // tile,),
            in_specs=[
                pl.BlockSpec((hidden, width), lambda i, core: (core[0], 0)),
                pl.BlockSpec((tile, width), lambda i, core: (i, 0)),
            ]
            + [pl.BlockSpec(memory_space=pl.ANY)] * len(after),
            out_specs=pl.BlockSpec((hidden, tile), lambda i, core: (0, i)),
        ),
        out_shape=jax.ShapeDtypeStruct((hidden, count), f32),
        cost_estimate=cost(20),
        compiler_params=large,
    )(core, down, cots, *after)


def flip_kernel(core_ref, one_ref, two_ref, *rest):
    rest[-2][...] = one_ref[...].astype(f32).T.astype(bf16)
    rest[-1][...] = two_ref[...].astype(f32).T.astype(bf16)


def flipped(one, two, core, after):
    width, hidden = one.shape[0], one.shape[1] // 2
    tile = 256
    source = pl.BlockSpec((tile, hidden), lambda n, core: (n, core[0]))
    result = pl.BlockSpec((hidden, tile), lambda n, core: (0, n))
    return pl.pallas_call(
        flip_kernel,
        grid_spec=pltpu.PrefetchScalarGridSpec(
            num_scalar_prefetch=1,
            grid=(width // tile,),
            in_specs=[source, source] + [pl.BlockSpec(memory_space=pl.ANY)] * len(after),
            out_specs=[result, result],
        ),
        out_shape=[jax.ShapeDtypeStruct((hidden, width), bf16)] * 2,
        cost_estimate=cost(8),
    )(core.astype(jnp.int32).reshape((1,)), one, two, *after)


def run(body, outs, args, scratch=(), after=(), scalar=False, micros=1):
    vmem = pl.BlockSpec(memory_space=pltpu.VMEM)
    specs = [vmem] * len(args)
    if scalar:
        specs[0] = pl.BlockSpec(memory_space=pltpu.SMEM)
    count = len(args)

    def whole(*refs):
        body(*refs[:count], *refs[count + len(after) :])

    return pl.pallas_call(
        whole,
        out_shape=outs,
        in_specs=specs + [pl.BlockSpec(memory_space=pl.ANY)] * len(after),
        out_specs=[vmem] * len(outs),
        scratch_shapes=scratch,
        cost_estimate=cost(micros),
        compiler_params=middle,
    )(*args, *after)


def run_rows(body, kind, args, count, after=()):
    rows, cols = args[0].shape
    block = pl.BlockSpec((count, cols), lambda n: (n, 0))
    row = pl.BlockSpec((1, cols), lambda n: (0, 0))

    def whole(*refs):
        body(*refs[: len(args)], refs[-1])

    return pl.pallas_call(
        whole,
        grid=(rows // count,),
        in_specs=[row if arg.shape[0] == 1 else block for arg in args]
        + [pl.BlockSpec(memory_space=pl.ANY)] * len(after),
        out_specs=block,
        out_shape=jax.ShapeDtypeStruct((rows, cols), kind),
        cost_estimate=brief,
        compiler_params=large,
    )(*args, *after)


def unpack_kernel(core_ref, flat_ref, other_ref, recur_ref, intake_ref, sums_ref, *, heads):
    head = recur_ref.shape[1]
    own, other = flat_ref[:head].astype(f32), other_ref[...].astype(f32)
    first = core_ref[0] == 0
    for ref, blocks in (
        (recur_ref, jnp.where(first, own, other)),
        (intake_ref, jnp.where(first, other, own)),
    ):
        for h in range(heads):
            ref[h] = blocks[:, h * head : (h + 1) * head]
    sums_ref[...] = flat_ref[head:].astype(f32)


def local(
    inputs,
    cotangent,
    segment_ids,
    norm_gain,
    branch_weight,
    stream_weight,
    conv_weight,
    conv_bias,
    recur_weight,
    recur_bias,
    intake_weight,
    intake_bias,
    decay_param,
    output_weight,
    mlp_gain,
    gate_weight,
    up_weight,
    down_weight,
    *,
    depth,
    square,
):
    line = square and depth == 4
    plain = not square
    core = lax.axis_index("core")
    core_id = core.astype(jnp.int32).reshape((1,))
    spot = jnp.zeros((1,), jnp.int32)
    if square:
        spot = spot + (2 * lax.axis_index("y") + lax.axis_index("x")).astype(jnp.int32)
    where = jnp.concatenate([spot, core_id])
    heads, head = recur_weight.shape[0], recur_weight.shape[1]
    width = heads * head
    length = segment_ids.shape[1]
    block, features = inputs.shape
    hidden_units = gate_weight.shape[1]
    shape = jax.ShapeDtypeStruct
    halves = [shape((block // 2, features), bf16)] * 2

    gain_one = norm_gain.astype(f32)[None, :]
    gain_two = mlp_gain.astype(f32)[None, :]
    normed_own = run(norm_kernel, halves, (inputs, gain_one))

    seg_row = segment_ids[0]
    masks = []
    for k in range(1, 4):
        earlier = jnp.concatenate([jnp.full((k,), -1, jnp.int32), seg_row[:-k]])
        masks.append((seg_row == earlier).astype(f32))
    joined = jnp.pad(jnp.stack(masks), ((0, 0), (0, 8)))
    joined = jnp.broadcast_to(joined[:, :, None], (3, length + 8, 128))
    square_low = shape((2, width, width), bf16)
    wide_high, wide_low = pl.pallas_call(
        prep_kernel, out_shape=[square_low, square_low], cost_estimate=brief
    )(recur_weight, intake_weight)
    gate_bias = jnp.stack([recur_bias, intake_bias])
    soft = (-decay_scale * jax.nn.softplus(-decay_param))[None, :]
    taps = conv_weight.astype(f32)

    if line:
        cots = lax.all_gather(cotangent, ALL, axis=0, tiled=True)

    normed_pieces = gather_row(normed_own, square, (wide_high,) if square else ())
    token = shape((length, width), f32)
    token_low = shape((length, width), bf16)
    row_low = shape((length, features), bf16)
    row_sends = send_shapes(length, features, plain)
    half_row = shape((length, features // 2), bf16)
    normed_mine, normed_theirs, branch_pre, stream_pre, gated, convolved, recur_gate, intake_gate, state, *sends = run(
        functools.partial(forward_kernel, count=len(normed_pieces), head=head, plain=plain),
        [half_row, half_row, token, token, token_low, token, token, token, token, *row_sends],
        (
            where,
            *normed_pieces,
            branch_weight,
            stream_weight,
            output_weight,
            joined,
            taps,
            conv_bias.astype(f32)[None, :],
            wide_high,
            wide_low,
            gate_bias,
            soft,
        ),
        [pltpu.VMEM((length, width), bf16)] * 2 + [pltpu.VMEM((length, features), bf16)],
        scalar=True,
        micros=20,
    )
    own_cots = cotangent
    if square:
        (own_cots,) = held((cotangent,), normed_pieces)
    own_cots = gather_blocks(own_cots, square)
    activ_grad = row_back(own_cots, down_weight)
    if square:
        sends[:2] = held(sends[:2], own_cots[1:])
    addends = scatter_row(sends, square, (activ_grad,) if square else ())

    hidden, one, two, normed_two = run(
        second_norm_kernel,
        [shape((block, features), f32), *halves, shape((block, features), bf16)],
        (inputs, gain_two, *addends),
    )
    if line:
        tokens = lax.all_gather(normed_two, ALL, axis=0, tiled=True)
        gate_turned, up_turned = flipped(gate_weight, up_weight, core, (gated,))
    mlp_pieces = gather_row((one, two), square, (gate_turned,) if line else ())
    tile = min(768, hidden_units)
    fixed = [pl.BlockSpec(piece.shape, lambda i: (0, 0)) for piece in mlp_pieces]
    column = pl.BlockSpec((length, tile), lambda i: (0, i))
    weight_column = pl.BlockSpec((features, tile), lambda i: (0, i))
    low_units = shape((length, hidden_units), bf16)
    kept = [] if line else [low_units, low_units]
    mlp_in, activ, *sends = pl.pallas_call(
        functools.partial(mlp_kernel, count=len(mlp_pieces), plain=plain, keep=not line),
        grid=(hidden_units // tile,),
        in_specs=[*fixed, column, weight_column, weight_column],
        out_specs=[pl.BlockSpec(row_low.shape, lambda i: (0, 0)), column]
        + [column] * len(kept)
        + [pl.BlockSpec(send.shape, lambda i: (0, 0)) for send in row_sends],
        out_shape=[row_low, low_units, *kept, *row_sends],
        scratch_shapes=[pltpu.VMEM((length, features), bf16), pltpu.VMEM((length, features), f32)],
        cost_estimate=cost(23),
        compiler_params=pltpu.CompilerParams(vmem_limit_bytes=56 * 1024 * 1024),
    )(*mlp_pieces, activ_grad, gate_weight, up_weight)
    kept, sends = sends[: len(kept)], sends[len(kept) :]
    beside = ()
    if line:
        grads = down_back(core_id, cots, down_weight, (sends[0],))
        beside = (grads,)
    addends = scatter_row(sends, square, beside)

    mlp_gain_part, resid_grad, one, two = run(
        functools.partial(norm_back_kernel, final=False),
        [shape((1, features), f32), shape((block, features), f32), *halves],
        (hidden, cotangent, gain_two, *addends),
    )
    (out_part,) = run(
        functools.partial(down_kernel, plain=plain), [row_low], (spot, activ, down_weight), after=(one,), scalar=True, micros=6
    )
    mlp_out = lax.psum_scatter(out_part, ("y", "x"), scatter_dimension=0, tiled=True)
    cot_pieces = gather_row((one, two), square, (out_part,) if square else ())

    cot_mine, cot_theirs, branch_low, state_grad = run(
        functools.partial(branch_back_kernel, count=len(cot_pieces)),
        [half_row, half_row, token_low, token],
        (where, *cot_pieces, output_weight, branch_pre, state),
        [pltpu.VMEM((length, features), bf16)],
        scalar=True,
        micros=6,
    )
    normed_other = sibling(normed_theirs)
    pairs = (
        gated,
        sibling(gated),
        cot_mine,
        sibling(cot_theirs),
        normed_mine,
        normed_other,
        branch_low,
        sibling(branch_low),
    )
    output_half, branch_half = run(
        pairs_kernel,
        [shape((width, features // 2), bf16), shape((features // 2, width), bf16)],
        pairs,
    )
    packed = shape((head + 32, width), f32)
    stream_low, flat_mine, flat_theirs, one_part = run(
        functools.partial(backward_kernel, head=head, plain=plain),
        [token_low, packed, packed, row_low],
        (
            where,
            state_grad,
            branch_low,
            branch_weight,
            stream_weight,
            stream_pre,
            joined,
            convolved,
            recur_gate,
            intake_gate,
            state,
            taps,
            wide_high,
            soft,
            normed_mine,
            normed_theirs,
            gain_one,
            mlp_gain_part,
        ),
        [
            pltpu.VMEM((2, width, width), f32),
            pltpu.VMEM((8, width), f32),
            pltpu.VMEM((2, length, width), bf16),
            pltpu.VMEM((length, width), bf16),
            pltpu.VMEM((length + 8, width), f32),
        ],
        after=(output_half, branch_half),
        scalar=True,
        micros=0,
    )
    if line:
        moved = line_move([(output_half, 0)])
    pairs = (normed_mine, normed_other, stream_low, sibling(stream_low))
    (stream_half,) = run(
        pairs_kernel, [shape((features // 2, width), bf16)], pairs, micros=0
    )
    last = ()
    if line:
        rows = branch_half.shape[0]
        (branch_half,) = run(
            below_kernel,
            [shape((rows + packed.shape[0], width), bf16)],
            (branch_half, flat_mine, sibling(flat_theirs)),
            after=(stream_half,),
            micros=0,
        )
        (output_sum,) = line_settle(moved, (branch_half, tokens))
        branch_half, stream_half, one_part = held((branch_half, stream_half, one_part), (output_sum,))
        moved = line_move([(output_sum, 1), (branch_half, 0)])
        activ_all, gate_all, up_all = mlp_rows(tokens, grads, gate_turned, up_turned, (output_sum,))
        output_sum, branch_sum = line_settle(moved, (activ_all,))
        gate_all, up_all, activ_all, stream_half = held(
            (gate_all, up_all, activ_all, stream_half), (branch_sum,)
        )
        moved = line_move([(output_sum, 2), (branch_sum, 1), (stream_half, 0)])
        gate_low, gate_w_grad = product(gate_all, tokens, core_id, True)
        up_low, up_w_grad = product(up_all, tokens, core_id, True, (gate_low,))
        output_sum, branch_sum, stream_sum = line_settle(moved, (up_low,))
        gate_low, up_low, activ_all = held((gate_low, up_low, activ_all), (stream_sum,))
        moved = line_move([(branch_sum, 2), (stream_sum, 1)])
        down_low, down_w_grad = product(activ_all, cots, core_id, False)
        gate_w_grad = filled(gate_w_grad, sibling(gate_low), core_id, True, (down_low,))
        up_w_grad = filled(up_w_grad, sibling(up_low), core_id, True, (gate_w_grad,))
        branch_sum, stream_sum = line_settle(moved, (up_w_grad,))
        branch_sum, flat_sum = branch_sum[:rows], branch_sum[rows:]
        (down_low,) = held((down_low,), (stream_sum,))
        moved = line_move([(stream_sum, 2)])
        last = (stream_sum,)
    else:
        (flat,) = run(sum_kernel, [packed], (flat_mine, sibling(flat_theirs)))

    one_grad = lax.psum_scatter(one_part, ("y", "x"), scatter_dimension=0, tiled=True)

    inputs_grad = run_rows(
        functools.partial(norm_back_kernel, final=True),
        bf16,
        (inputs, resid_grad, gain_one, one_grad),
        block // 4,
        last,
    )
    block_out = run_rows(add_kernel, bf16, (hidden, mlp_out), block // 4, last)

    def apart(flat_sum, beside):
        gates_other = sibling(flat_sum[:head])
        blocks = shape((heads, head, head), f32)
        found = run(
            functools.partial(unpack_kernel, heads=heads),
            [blocks, blocks, shape((8, width), f32)],
            (core_id, flat_sum[: head + 8], gates_other),
            after=beside[:1],
            scalar=True,
        )
        gains = flat_sum[head + 8 : head + 24, :256].astype(f32)
        if square:
            for axis, other in zip(("x", "y"), beside, strict=True):
                gains = gains + held((lax.ppermute(gains, axis, swap),), (other,))[0]
        else:
            gains = lax.psum(gains, ("y", "x"))
        return *found, gains

    def whole(own, axis, after=()):
        return joined_halves(own, sibling(own), core_id, axis, after)

    if line:
        output_w_grad = whole(output_sum, 1, (inputs_grad, block_out))
        branch_w_grad = whole(branch_sum, 0, (output_w_grad,))
        down_w_grad = filled(down_w_grad, sibling(down_low), core_id, False, (branch_w_grad,))
        recur_grad, intake_grad, sums, gains = apart(flat_sum, (output_w_grad, branch_w_grad))
        (stream_sum,) = line_settle(moved, (down_w_grad, recur_grad, gains))
        stream_w_grad = whole(stream_sum, 0)
    else:
        output_sum, branch_sum, stream_sum, flat_sum = (
            lax.psum(part, "z") for part in (output_half, branch_half, stream_half, flat)
        )
        recur_grad, intake_grad, sums, gains = apart(flat_sum, (inputs_grad, block_out))
        output_w_grad, branch_w_grad, stream_w_grad = (
            whole(output_sum, 1),
            whole(branch_sum, 0),
            whole(stream_sum, 0),
        )

        def over_rows(left, right):
            part = lax.dot_general(left, right, contract_rows, preferred_element_type=f32)
            return lax.psum(part.astype(bf16), ("z", "core")).astype(f32)

        gate_w_grad = over_rows(mlp_in, kept[0])
        up_w_grad = over_rows(mlp_in, kept[1])
        down_w_grad = over_rows(activ, jnp.concatenate(own_cots, axis=0))

    gains = gains.reshape(2, -1)
    return (
        block_out,
        inputs_grad,
        gains[0],
        branch_w_grad,
        stream_w_grad,
        sums[0:4],
        sums[4],
        recur_grad,
        sums[5],
        intake_grad,
        sums[6],
        sums[7] * decay_scale * jax.nn.sigmoid(-decay_param),
        output_w_grad,
        gains[1],
        gate_w_grad,
        up_w_grad,
        down_w_grad,
    )


def solution(mesh):
    depth = mesh.shape["dp"] // 2
    across = mesh.shape["mp"] // 2
    fine = Mesh(mesh.devices.reshape(depth, 2, 2, across), ALL)
    dp, mp = ("z", "core"), ("y", "x")
    cols, vec, blocks, rows = P(None, mp), P(mp), P(mp, None, None), P(mp, None)
    tokens = P(ALL, None)
    return jax.shard_map(
        functools.partial(local, depth=depth, square=across == 2),
        mesh=fine,
        in_specs=(
            tokens,
            tokens,
            P(dp, None),
            P(),
            cols,
            cols,
            cols,
            vec,
            blocks,
            vec,
            blocks,
            vec,
            vec,
            rows,
            P(),
            cols,
            cols,
            rows,
        ),
        out_specs=(
            tokens,
            tokens,
            P(),
            cols,
            cols,
            cols,
            vec,
            blocks,
            vec,
            blocks,
            vec,
            vec,
            rows,
            P(),
            cols,
            cols,
            rows,
        ),
        check_vma=False,
    )
```

```python
import functools

import jax
import jax.numpy as jnp
from jax import lax
from jax.experimental import pallas as pl
from jax.experimental.pallas import tpu as pltpu
from jax.sharding import Mesh
from jax.sharding import PartitionSpec as P

eps = 1e-06
decay_scale = 8.0
contract_rows = (((0,), (0,)), ((), ()))
contract_cols = (((1,), (1,)), ((), ()))
f32 = jnp.float32
bf16 = jnp.bfloat16
swap = [(0, 1), (1, 0)]


def cost(micros):
    return pl.CostEstimate(flops=0, bytes_accessed=int(micros * 3e6), transcendentals=0)


brief = cost(1)
large = pltpu.CompilerParams(vmem_limit_bytes=48 * 1024 * 1024)
middle = pltpu.CompilerParams(vmem_limit_bytes=32 * 1024 * 1024)
ALL = ("z", "core", "y", "x")
STEP = 16
root_two_over_pi = 0.7978845608028654


def pass_kernel(*refs):
    pass


def held(values, after):
    values, after = list(values), list(after)
    anywhere = pl.BlockSpec(memory_space=pl.ANY)
    return pl.pallas_call(
        pass_kernel,
        in_specs=[anywhere] * (len(values) + len(after)),
        out_specs=[anywhere] * len(values),
        out_shape=[jax.ShapeDtypeStruct(value.shape, value.dtype) for value in values],
        input_output_aliases={n: n for n in range(len(values))},
        cost_estimate=cost(0.1),
    )(*values, *after)


def gather_row(halves, square, beside=()):
    if not square:
        return [lax.all_gather(jnp.concatenate(halves, axis=0), ("y", "x"), axis=0, tiled=True)]
    one, two = halves
    one_x = lax.ppermute(one, "x", swap)
    two_y = lax.ppermute(two, "y", swap)
    two_x = lax.ppermute(two, "x", swap)
    one_y = lax.ppermute(one, "y", swap)
    if beside:
        one_x, two_y = held((one_x, two_y), beside)
    one_d = lax.ppermute(one_x, "y", swap)
    two_d = lax.ppermute(two_y, "x", swap)
    return [one, one_x, one_y, one_d, two, two_x, two_y, two_d]


def gather_blocks(block, square):
    if not square:
        return gather_row((block,), square)
    return [
        block,
        lax.ppermute(block, "x", swap),
        lax.ppermute(block, "y", swap),
        lax.ppermute(block, ("y", "x"), [(0, 3), (3, 0), (1, 2), (2, 1)]),
    ]


def scatter_row(sends, square, beside=()):
    if not square:
        return [lax.psum_scatter(sends[0], ("y", "x"), scatter_dimension=0, tiled=True)]
    to_x, to_y, keep_x, keep_y, own = sends
    got_x = lax.ppermute(to_x, "x", swap)
    got_y = lax.ppermute(to_y, "y", swap)
    if beside:
        got_x, got_y = held((got_x, got_y), beside)
    send_y, send_x = run(
        middle_kernel,
        [jax.ShapeDtypeStruct(keep_x.shape, bf16)] * 2,
        (got_x, got_y, keep_x, keep_y),
    )
    last_y = lax.ppermute(send_y, "y", swap)
    last_x = lax.ppermute(send_x, "x", swap)
    return [own, got_x, got_y, last_y, last_x]


def sibling(value):
    return lax.ppermute(value, "core", swap)


def line_move(pieces):
    pairs = [[(0, 1), (3, 2)], [(1, 2), (2, 1)], [(1, 0), (2, 3)]]
    return [(piece, stage, lax.ppermute(piece, "z", pairs[stage])) for piece, stage in pieces]


def settle_kernel(inner_ref, *refs, stages):
    count = len(stages)
    for n, stage in enumerate(stages):
        piece, other, out = refs[n], refs[count + n], refs[2 * count + n]
        if stage < 2:
            out[...] = (piece[...].astype(f32) + other[...].astype(f32)).astype(out.dtype)
        else:
            out[...] = jnp.where(inner_ref[0] == 1, piece[...], other[...])


def line_settle(moved, after):
    place = lax.axis_index("z")
    inner = ((place == 1) | (place == 2)).astype(jnp.int32).reshape((1,))
    pieces, stages, others = zip(*moved, strict=True)
    blocks = [
        pl.BlockSpec((piece.shape[0] // 4, piece.shape[1]), lambda n, inner: (n, 0)) for piece in pieces
    ]

    def body(inner_ref, *refs):
        settle_kernel(inner_ref, *refs[: 2 * len(pieces)], *refs[-len(pieces) :], stages=stages)

    return pl.pallas_call(
        body,
        grid_spec=pltpu.PrefetchScalarGridSpec(
            num_scalar_prefetch=1,
            grid=(4,),
            in_specs=[*blocks, *blocks] + [pl.BlockSpec(memory_space=pl.ANY)] * len(after),
            out_specs=blocks,
        ),
        out_shape=[pltpu.HBM(piece.shape, piece.dtype) for piece in pieces],
        cost_estimate=brief,
        compiler_params=large,
    )(inner, *pieces, *others, *after)


def assemble(pieces, out_ref):
    at = 0
    for piece in pieces:
        out_ref[at : at + piece.shape[0], :] = piece[...]
        at += piece.shape[0]


def split(whole_ref, core, mine_ref, theirs_ref):
    size = mine_ref.shape[1]
    for ref, which in ((mine_ref, core), (theirs_ref, 1 - core)):
        ref[...] = whole_ref[:, pl.ds(pl.multiple_of(which * size, 128), size)]


def pairs_kernel(*refs):
    count = len(refs) // 5
    for n in range(count):
        own_left, other_left, own_right, other_right = refs[4 * n : 4 * n + 4]
        out_ref = refs[4 * count + n]
        cols = out_ref.shape[1]
        for first in range(0, cols, 512):
            span = slice(first, min(first + 512, cols))
            out_ref[:, span] = (
                lax.dot_general(
                    own_left[...], own_right[:, span], contract_rows, preferred_element_type=f32
                )
                + lax.dot_general(
                    other_left[...], other_right[:, span], contract_rows, preferred_element_type=f32
                )
            ).astype(bf16)


def sum_kernel(one_ref, two_ref, out_ref):
    out_ref[...] = (one_ref[...] + two_ref[...]).astype(out_ref.dtype)


def below_kernel(top_ref, one_ref, two_ref, out_ref):
    rows = top_ref.shape[0]
    out_ref[:rows, :] = top_ref[...]
    out_ref[rows:, :] = (one_ref[...] + two_ref[...]).astype(out_ref.dtype)


def send_shapes(length, width, plain):
    if plain:
        return [jax.ShapeDtypeStruct((length, width), bf16)]
    block, cut = length // 4, width // 2
    return (
        [jax.ShapeDtypeStruct((2 * block, cut), bf16)] * 2
        + [jax.ShapeDtypeStruct((block, cut), bf16)] * 2
        + [jax.ShapeDtypeStruct((block, width), f32)]
    )


def emit(value, first, width, sends, plain, spot=None):
    last = first + value.shape[1]
    if spot is not None:
        half = value.shape[0] // 8
        for n in range(2):
            for k in range(4):
                start = pl.multiple_of((lax.bitwise_xor(k, spot) * 2 + n) * half, half)
                block = value[(n * 4 + k) * half : (n * 4 + k + 1) * half]
                sends[0][pl.ds(start, half), first:last] = block.astype(bf16)
        return
    if plain:
        sends[0][:, first:last] = value.astype(bf16)
        return
    to_x, to_y, keep_x, keep_y, own = sends
    cut = width // 2
    half = value.shape[0] // 8

    def put(ref, at, block, cols, kind):
        for n in range(2):
            rows = slice(n * 4 * half + block * half, n * 4 * half + (block + 1) * half)
            ref[at + n * half : at + (n + 1) * half, cols] = value[rows].astype(kind)

    put(own, 0, 0, slice(first, last), f32)
    if last <= cut:
        cols = slice(first, last)
        put(to_x, 0, 1, cols, bf16)
        put(to_x, 2 * half, 3, cols, bf16)
        put(keep_y, 0, 2, cols, bf16)
    else:
        cols = slice(first - cut, last - cut)
        put(to_y, 0, 2, cols, bf16)
        put(to_y, 2 * half, 3, cols, bf16)
        put(keep_x, 0, 1, cols, bf16)


def middle_kernel(got_x, got_y, keep_x, keep_y, send_y, send_x):
    block = keep_x.shape[0]
    send_y[...] = (keep_y[...].astype(f32) + got_x[block:].astype(f32)).astype(bf16)
    send_x[...] = (keep_x[...].astype(f32) + got_y[block:].astype(f32)).astype(bf16)


def finish(refs):
    if len(refs) == 1:
        return refs[0][...].astype(f32)
    own, got_x, got_y, last_y, last_x = refs
    block, cut = last_y.shape
    left = own[:, :cut] + got_x[:block].astype(f32) + last_y[...].astype(f32)
    right = own[:, cut:] + got_y[:block].astype(f32) + last_x[...].astype(f32)
    return jnp.concatenate([left, right], axis=1)


def mean_of(x):
    return jnp.mean(x, axis=-1, keepdims=True)


def norm_kernel(input_ref, gain_ref, one_ref, two_ref):
    values = input_ref[...].astype(f32)
    normed = (values * lax.rsqrt(mean_of(values * values) + eps) * gain_ref[...]).astype(bf16)
    half = normed.shape[0] // 2
    one_ref[...] = normed[:half]
    two_ref[...] = normed[half:]


def second_norm_kernel(input_ref, gain_ref, *refs):
    addends, (hidden_ref, one_ref, two_ref, all_ref) = refs[:-4], refs[-4:]
    hidden = input_ref[...].astype(f32) + finish(addends)
    hidden_ref[...] = hidden
    normed = (hidden * lax.rsqrt(mean_of(hidden * hidden) + eps) * gain_ref[...]).astype(bf16)
    half = normed.shape[0] // 2
    one_ref[...] = normed[:half]
    two_ref[...] = normed[half:]
    all_ref[...] = normed


def norm_back_kernel(value_ref, before_ref, gain_ref, *refs, final):
    outs = 1 if final else 4
    addends, outs = refs[:-outs], refs[-outs:]
    values = value_ref[...].astype(f32)
    scale = lax.rsqrt(mean_of(values * values) + eps)
    hat = values * scale
    grad = finish(addends)
    scaled = grad * gain_ref[...]
    total = before_ref[...].astype(f32) + scale * (scaled - hat * mean_of(scaled * hat))
    if final:
        outs[0][...] = total.astype(bf16)
        return
    outs[0][...] = jnp.sum(grad * hat, axis=0, keepdims=True)
    outs[1][...] = total
    low = total.astype(bf16)
    half = low.shape[0] // 2
    outs[2][...] = low[:half]
    outs[3][...] = low[half:]


def add_kernel(value_ref, *refs):
    refs[-1][...] = (value_ref[...] + finish(refs[:-1])).astype(bf16)


def mlp_kernel(*refs, count, plain, keep):
    pieces, (grad_ref, gate_w, up_w), refs = refs[:count], refs[count : count + 3], refs[count + 3 :]
    *outs, token_ref, total_ref = refs
    token_out, activ_ref, *outs = outs
    step = pl.program_id(0)

    @pl.when(step == 0)
    def _():
        assemble(pieces, token_ref)
        token_out[...] = token_ref[...]

    tokens = token_ref[...]
    gate_pre = jnp.dot(tokens, gate_w[...], preferred_element_type=f32)
    up_pre = jnp.dot(tokens, up_w[...], preferred_element_type=f32)
    activ_grad = grad_ref[...]
    value, slope = gelu_terms(gate_pre)
    activ_ref[...] = (value * up_pre).astype(bf16)
    gate_low = (activ_grad * up_pre * slope).astype(bf16)
    up_low = (activ_grad * value).astype(bf16)
    if keep:
        outs[0][...] = gate_low
        outs[1][...] = up_low
        outs = outs[2:]
    width = total_ref.shape[1]
    last = step == pl.num_programs(0) - 1
    for first in range(0, width, 512):
        cols = slice(first, first + 512)
        part = lax.dot_general(
            gate_low, gate_w[cols, :], contract_cols, preferred_element_type=f32
        ) + lax.dot_general(up_low, up_w[cols, :], contract_cols, preferred_element_type=f32)

        @pl.when(step == 0)
        def _(part=part, cols=cols):
            total_ref[:, cols] = part

        @pl.when(step > 0)
        def _(part=part, cols=cols):
            total_ref[:, cols] += part

    @pl.when(last)
    def _():
        for first in range(0, width, 512):
            emit(total_ref[:, first : first + 512], first, width, outs, plain)


def down_kernel(spot_ref, activ_ref, weight_ref, *sends, plain):
    spot = None if plain else spot_ref[0]
    width = weight_ref.shape[1]
    for first in range(0, width, 512):
        cols = slice(first, first + 512)
        value = jnp.dot(activ_ref[...], weight_ref[:, cols], preferred_element_type=f32)
        emit(value, first, width, sends, plain, spot)


def tile_span(first, last, head, width):
    low = (first // head) * head // 128 * 128
    high = min(width, -(-(((last - 1) // head + 1) * head) // 128) * 128)
    return low, high


def tiles(width):
    return [(n, min(n + 256, width)) for n in range(0, width, 256)]


def sigmoid(x):
    return 1.0 / (1.0 + jnp.exp(-x))


def decay_terms(gate, soft, link):
    log_decay = gate * soft
    decay = jnp.exp(log_decay)
    square = decay * decay
    x = 2.0 * log_decay
    series = 1.0 + x * (1.0 / 6.0) * (1.0 + x * (1.0 / 7.0))
    series = 1.0 + x * (1.0 / 4.0) * (1.0 + x * (1.0 / 5.0) * series)
    series = -x * (1.0 + x * (1.0 / 2.0) * (1.0 + x * (1.0 / 3.0) * series))
    gap = jnp.where(x > -0.3, series, 1.0 - square)
    root = jnp.sqrt(gap)
    return link * decay, square, root, link * root + (1.0 - link)


def gelu_terms(x):
    inner = jnp.tanh(root_two_over_pi * (x + 0.044715 * x * x * x))
    value = 0.5 * x * (1.0 + inner)
    slope = 0.5 * (1.0 + inner) + 0.5 * x * (1.0 - inner * inner) * root_two_over_pi * (
        1.0 + 3.0 * 0.044715 * x * x
    )
    return value, slope


def widen(mask, width):
    return jnp.concatenate([mask] * (-(-width // 128)), axis=1)[:, :width]


def token_place(length, spot, plain):
    block, half = length // 4, length // 8
    per_block = block // STEP
    per_half = half // STEP

    def offset(step):
        if plain:
            return pl.multiple_of(step * STEP, STEP)
        turn = lax.bitwise_xor(step // per_block, spot)
        inside = lax.rem(step, per_block)
        at = (inside // per_half) * (length // 2) + turn * half + lax.rem(inside, per_half) * STEP
        return pl.multiple_of(at, STEP)

    return offset


def prep_kernel(recur_ref, intake_ref, high_ref, low_ref):
    count, size, _ = recur_ref.shape
    for which, ref in ((0, recur_ref), (1, intake_ref)):
        for h in range(count):
            parts = [ref[h]]
            if h:
                parts.insert(0, jnp.zeros((size, h * size), f32))
            if h < count - 1:
                parts.append(jnp.zeros((size, (count - 1 - h) * size), f32))
            row = jnp.concatenate(parts, axis=1)
            high = row.astype(bf16)
            rows = slice(h * size, (h + 1) * size)
            high_ref[which, rows, :] = high
            low_ref[which, rows, :] = (row - high.astype(f32)).astype(bf16)


def forward_kernel(spot_ref, *refs, count, head, plain):
    pieces, refs = refs[:count], refs[count:]
    (branch_w, stream_w, output_w, joined_ref, taps_ref, bias_ref, high_ref, low_ref, gate_bias_ref, soft_ref), refs = (
        refs[:10],
        refs[10:],
    )
    (mine_ref, theirs_ref, branch_ref, stream_ref, gated_ref, conv_ref, recur_ref, intake_ref, state_ref), refs = (
        refs[:9],
        refs[9:],
    )
    *sends, part_high, part_low, normed_ref = refs
    assemble(pieces, normed_ref)
    split(normed_ref, spot_ref[1], mine_ref, theirs_ref)
    for first, last in tiles(branch_ref.shape[1]):
        cols = slice(first, last)
        branch_ref[:, cols] = jnp.dot(normed_ref[...], branch_w[:, cols], preferred_element_type=f32)
        stream_ref[:, cols] = jnp.dot(normed_ref[...], stream_w[:, cols], preferred_element_type=f32)
    length, width = branch_ref.shape
    steps = length // STEP
    offset = token_place(length, spot_ref[0], plain)

    def convolve(step, before):
        at = offset(step)
        here = pl.multiple_of(step * STEP, STEP)
        now = stream_ref[pl.ds(at, STEP), :]
        both = jnp.concatenate([before, now], axis=0)
        total = bias_ref[0:1, :] + taps_ref[0:1, :] * now
        for k in range(1, 4):
            mask = widen(joined_ref[k - 1, pl.ds(here, STEP), :], width)
            total = total + taps_ref[k : k + 1, :] * both[8 - k : 8 - k + STEP] * mask
        conv_ref[pl.ds(at, STEP), :] = total
        high = total.astype(bf16)
        part_high[pl.ds(here, STEP), :] = high
        part_low[pl.ds(here, STEP), :] = (total - high.astype(f32)).astype(bf16)
        return now[STEP - 8 :]

    lax.fori_loop(0, steps, convolve, jnp.zeros((8, width), f32), unroll=2)

    for which, out_ref in ((0, recur_ref), (1, intake_ref)):
        for first, last in tiles(width):
            low, high = tile_span(first, last, head, width)
            span, cols = slice(low, high), slice(first, last)
            high_part, low_part = high_ref[which, span, cols], low_ref[which, span, cols]
            pre = (
                jnp.dot(part_high[:, span], high_part, preferred_element_type=f32)
                + jnp.dot(part_low[:, span], high_part, preferred_element_type=f32)
                + jnp.dot(part_high[:, span], low_part, preferred_element_type=f32)
            )
            out_ref[:, cols] = pre + gate_bias_ref[which : which + 1, cols]

    rows = lax.broadcasted_iota(jnp.int32, (8, width), 0)
    soft = soft_ref[0:1, :]

    def advance(step, last_state):
        at = offset(step)
        here = pl.multiple_of(step * STEP, STEP)
        link = widen(joined_ref[0, pl.ds(here, STEP), :], width)
        conv = conv_ref[pl.ds(at, STEP), :]
        recur = sigmoid(recur_ref[pl.ds(here, STEP), :])
        intake = sigmoid(intake_ref[pl.ds(here, STEP), :])
        recur_ref[pl.ds(here, STEP), :] = recur
        intake_ref[pl.ds(here, STEP), :] = intake
        carried, square, root, multiplier = decay_terms(recur, soft, link)
        driven = multiplier * intake * conv
        found = []
        for part in range(STEP // 8):
            a = carried[8 * part : 8 * part + 8]
            b = driven[8 * part : 8 * part + 8]
            for shift in (1, 2, 4):
                a_before = jnp.where(rows >= shift, pltpu.roll(a, shift, 0), 1.0)
                b_before = jnp.where(rows >= shift, pltpu.roll(b, shift, 0), 0.0)
                b = b + a * b_before
                a = a * a_before
            state = b + a * last_state
            last_state = state[7:8]
            found.append(state)
        state = jnp.concatenate(found, axis=0)
        state_ref[pl.ds(at, STEP), :] = state
        value, slope = gelu_terms(branch_ref[pl.ds(at, STEP), :])
        gated_ref[pl.ds(at, STEP), :] = (value * state).astype(bf16)
        return last_state

    lax.fori_loop(0, steps, advance, jnp.zeros((1, width), f32), unroll=2)
    step_cols = 512
    for first in range(0, output_w.shape[1], step_cols):
        cols = slice(first, first + step_cols)
        value = jnp.dot(gated_ref[...], output_w[:, cols], preferred_element_type=f32)
        emit(value, first, output_w.shape[1], sends, plain)


def branch_back_kernel(spot_ref, *refs, count):
    pieces, (output_w, branch_ref, state_ref), refs = refs[:count], refs[count : count + 3], refs[count + 3 :]
    mine_ref, theirs_ref, branch_grad_ref, grad_ref, cot_ref = refs
    assemble(pieces, cot_ref)
    split(cot_ref, spot_ref[1], mine_ref, theirs_ref)
    length, width = branch_ref.shape
    for first, last in tiles(width):
        cols = slice(first, last)
        grad_ref[:, cols] = lax.dot_general(
            cot_ref[...], output_w[cols, :], contract_cols, preferred_element_type=f32
        )

    def rows(step, _):
        at = pl.ds(pl.multiple_of(step * STEP, STEP), STEP)
        value, slope = gelu_terms(branch_ref[at, :])
        grad = grad_ref[at, :]
        branch_grad_ref[at, :] = (grad * state_ref[at, :] * slope).astype(bf16)
        grad_ref[at, :] = grad * value
        return _

    lax.fori_loop(0, length // STEP, rows, 0)


def backward_kernel(
    spot_ref,
    grad_ref,
    branch_grad_ref,
    branch_w,
    stream_w,
    stream_ref,
    joined_ref,
    conv_ref,
    recur_ref,
    intake_ref,
    state_ref,
    taps_ref,
    high_ref,
    soft_ref,
    normed_mine,
    normed_theirs,
    gain_ref,
    other_gains,
    stream_grad_ref,
    mine_ref,
    theirs_ref,
    *refs,
    head,
    plain,
):
    *sends, gates_ref, sums_ref, pre_ref, conv_low, conv_grad = refs
    length, width = grad_ref.shape
    steps = length // STEP
    offset = token_place(length, spot_ref[0], plain)

    rows = lax.broadcasted_iota(jnp.int32, (8, width), 0)
    soft = soft_ref[0:1, :]
    count = STEP // 8

    def fold(value):
        total = value[0:8]
        for part in range(1, count):
            total = total + value[8 * part : 8 * part + 8]
        return total

    def retreat(turn, kept):
        after_carried, after_adjoint, decay_sum, recur_sum, intake_sum = kept
        step = steps - 1 - turn
        at = offset(step)
        at_before = offset(jnp.maximum(step - 1, 0))
        here = pl.multiple_of(step * STEP, STEP)
        link = widen(joined_ref[0, pl.ds(here, STEP), :], width)
        conv = conv_ref[pl.ds(at, STEP), :]
        recur = recur_ref[pl.ds(here, STEP), :]
        intake = intake_ref[pl.ds(here, STEP), :]
        carried, square, root, multiplier = decay_terms(recur, soft, link)
        grad = grad_ref[pl.ds(at, STEP), :]
        found = []
        for part in reversed(range(count)):
            own = carried[8 * part : 8 * part + 8]
            a = jnp.where(rows < 7, pltpu.roll(own, 7, 0), after_carried)
            b = grad[8 * part : 8 * part + 8]
            for shift in (1, 2, 4):
                a_after = jnp.where(rows < 8 - shift, pltpu.roll(a, 8 - shift, 0), 1.0)
                b_after = jnp.where(rows < 8 - shift, pltpu.roll(b, 8 - shift, 0), 0.0)
                b = b + a * b_after
                a = a * a_after
            adjoint = b + a * after_adjoint
            after_adjoint = adjoint[0:1]
            after_carried = own[0:1]
            found.append(adjoint)
        adjoint = jnp.concatenate(found[::-1], axis=0)
        state = state_ref[pl.ds(at, STEP), :]
        tail = state_ref[pl.ds(at_before + (STEP - 8), 8), :]
        earlier = jnp.concatenate([tail, state], axis=0)[7 : 7 + STEP]
        driven_part = adjoint * intake
        log_grad = adjoint * earlier * carried - driven_part * conv * link * square / root
        recur_grad = log_grad * soft * recur * (1.0 - recur)
        spread = driven_part * multiplier
        intake_grad = spread * conv * (1.0 - intake)
        pre_ref[0, pl.ds(here, STEP), :] = recur_grad.astype(bf16)
        pre_ref[1, pl.ds(here, STEP), :] = intake_grad.astype(bf16)
        conv_low[pl.ds(here, STEP), :] = conv.astype(bf16)
        conv_grad[pl.ds(here, STEP), :] = spread
        return (
            after_carried,
            after_adjoint,
            decay_sum + fold(log_grad * recur),
            recur_sum + fold(recur_grad),
            intake_sum + fold(intake_grad),
        )

    line = jnp.zeros((1, width), f32)
    eight = jnp.zeros((8, width), f32)
    kept = lax.fori_loop(0, steps, retreat, (line, line, eight, eight, eight), unroll=2)
    sums_ref[5:6, :] = jnp.sum(kept[3], axis=0, keepdims=True)
    sums_ref[6:7, :] = jnp.sum(kept[4], axis=0, keepdims=True)
    sums_ref[7:8, :] = jnp.sum(kept[2], axis=0, keepdims=True)

    conv_grad[length : length + 8, :] = eight
    for first, last in tiles(width):
        low, high = tile_span(first, last, head, width)
        span, cols = slice(low, high), slice(first, last)
        total = conv_grad[0:length, cols]
        for which in range(2):
            total = total + lax.dot_general(
                pre_ref[which, :, span], high_ref[which, cols, span], contract_cols, preferred_element_type=f32
            )
            gates_ref[which, span, cols] = lax.dot_general(
                conv_low[:, span], pre_ref[which, :, cols], contract_rows, preferred_element_type=f32
            )
        conv_grad[0:length, cols] = total

    def unwind(step, kept):
        at = offset(step)
        here = pl.multiple_of(step * STEP, STEP)
        ahead = conv_grad[pl.ds(here, STEP + 8), :]
        now = stream_ref[pl.ds(at, STEP), :]
        total = taps_ref[0:1, :] * ahead[0:STEP]
        sums = [kept[0] + fold(ahead[0:STEP] * now)]
        for k in range(1, 4):
            mask = widen(joined_ref[k - 1, pl.ds(here, STEP + 8), :], width)
            moved = (ahead * mask)[k : k + STEP]
            total = total + taps_ref[k : k + 1, :] * moved
            sums.append(kept[k] + fold(moved * now))
        stream_grad_ref[pl.ds(at, STEP), :] = total.astype(bf16)
        return (*sums, kept[4] + fold(ahead[0:STEP]))

    kept = lax.fori_loop(0, steps, unwind, (eight,) * 5, unroll=2)
    for k in range(5):
        sums_ref[k : k + 1, :] = jnp.sum(kept[k], axis=0, keepdims=True)
    count = width // head
    lanes = lax.broadcasted_iota(jnp.int32, (head, width), 1)
    for out_ref, which in ((mine_ref, spot_ref[1]), (theirs_ref, 1 - spot_ref[1])):
        blocks = gates_ref[which, 0:head, :]
        for h in range(1, count):
            blocks = jnp.where(lanes >= h * head, gates_ref[which, h * head : (h + 1) * head, :], blocks)
        out_ref[0:head, :] = blocks
        out_ref[head : head + 8, :] = sums_ref[...]
        out_ref[head + 8 :, :] = jnp.zeros((out_ref.shape[0] - head - 8, width), f32)

    step_cols = 512
    for first in range(0, branch_w.shape[0], step_cols):
        cols = slice(first, first + step_cols)
        value = lax.dot_general(
            branch_grad_ref[...], branch_w[cols, :], contract_cols, preferred_element_type=f32
        ) + lax.dot_general(
            stream_grad_ref[...], stream_w[cols, :], contract_cols, preferred_element_type=f32
        )
        half = normed_mine.shape[1]
        inside = slice(first % half, first % half + step_cols)
        mine = spot_ref[1] == first // half
        normed = jnp.where(mine, normed_mine[:, inside], normed_theirs[:, inside]).astype(f32)
        gains = jnp.sum(value * normed, axis=0, keepdims=True) / gain_ref[:, cols]
        for part in range(step_cols // 256):
            row = head + 8 + first // 256 + part
            below = row + branch_w.shape[0] // 256
            at = slice(part * 256, (part + 1) * 256)
            for out_ref in (mine_ref, theirs_ref):
                out_ref[row : row + 1, 0:256] = gains[:, at]
                out_ref[below : below + 1, 0:256] = other_gains[:, cols][:, at]
        emit(value, first, branch_w.shape[0], sends, plain, None if plain else spot_ref[0])


def rows_kernel(token_ref, grad_ref, gate_ref, up_ref, *rest):
    activ_ref, gate_out, up_out = rest[-3:]
    tokens = token_ref[...]
    hidden = gate_ref.shape[0]
    part = hidden // 3
    for n in range(3):
        rows = slice(n * part, (n + 1) * part)
        gate_pre = lax.dot_general(gate_ref[rows], tokens, contract_cols, preferred_element_type=f32)
        up_pre = lax.dot_general(up_ref[rows], tokens, contract_cols, preferred_element_type=f32)
        activ_grad = grad_ref[rows]
        value, slope = gelu_terms(gate_pre)
        activ_ref[rows] = (value * up_pre).astype(bf16)
        gate_out[rows] = (activ_grad * up_pre * slope).astype(bf16)
        up_out[rows] = (activ_grad * value).astype(bf16)


def mlp_rows(tokens, grads, gate, up, after):
    count, width = tokens.shape
    hidden = gate.shape[0]
    tile = 512
    tall = pl.BlockSpec((hidden, tile), lambda i: (0, i))
    weight = pl.BlockSpec((hidden, width), lambda i: (0, 0))
    return pl.pallas_call(
        rows_kernel,
        grid=(count // tile,),
        in_specs=[pl.BlockSpec((tile, width), lambda i: (i, 0)), tall, weight, weight]
        + [pl.BlockSpec(memory_space=pl.ANY)] * len(after),
        out_specs=[tall, tall, tall],
        out_shape=[jax.ShapeDtypeStruct((hidden, count), bf16)] * 3,
        cost_estimate=cost(34),
        compiler_params=large,
    )(tokens, grads, gate, up, *after)


def row_back_kernel(*refs, count):
    pieces, (weight_ref, out_ref, rows_ref) = refs[:count], refs[count:]

    @pl.when(pl.program_id(0) == 0)
    def _():
        half = pieces[0].shape[0] // 2
        at = 0
        for n in range(2):
            for piece in pieces:
                rows_ref[at : at + half, :] = piece[n * half : (n + 1) * half, :]
                at += half

    out_ref[...] = lax.dot_general(
        rows_ref[...], weight_ref[...], contract_cols, preferred_element_type=f32
    )


def row_back(pieces, down):
    hidden, width = down.shape
    length = sum(piece.shape[0] for piece in pieces)
    tile = min(512, hidden)
    return pl.pallas_call(
        functools.partial(row_back_kernel, count=len(pieces)),
        grid=(hidden // tile,),
        in_specs=[pl.BlockSpec(piece.shape, lambda i: (0, 0)) for piece in pieces]
        + [pl.BlockSpec((tile, width), lambda i: (i, 0))],
        out_specs=pl.BlockSpec((length, tile), lambda i: (0, i)),
        out_shape=jax.ShapeDtypeStruct((length, hidden), f32),
        scratch_shapes=[pltpu.VMEM((length, width), bf16)],
        cost_estimate=cost(6),
        compiler_params=large,
    )(*pieces, down)


def product(left, right, core, turn, after=()):
    rows, depth = left.shape
    cols = right.shape[1]
    tile = 256

    def body(core_ref, left_ref, right_ref, *rest):
        low_ref, whole_ref = rest[-2:]
        low = jnp.dot(left_ref[...], right_ref[...], preferred_element_type=f32).astype(bf16)
        low_ref[...] = low
        wide = low.astype(f32)
        whole_ref[...] = wide.T if turn else wide

    if turn:
        place = pl.BlockSpec((tile, rows), lambda n, core: (n, core[0]))
        shape = (cols, 2 * rows)
    else:
        place = pl.BlockSpec((rows, tile), lambda n, core: (core[0], n))
        shape = (2 * rows, cols)
    return pl.pallas_call(
        body,
        grid_spec=pltpu.PrefetchScalarGridSpec(
            num_scalar_prefetch=1,
            grid=(cols // tile,),
            in_specs=[
                pl.BlockSpec((rows, depth), lambda n, core: (0, 0)),
                pl.BlockSpec((depth, tile), lambda n, core: (0, n)),
            ]
            + [pl.BlockSpec(memory_space=pl.ANY)] * len(after),
            out_specs=[pl.BlockSpec((rows, tile), lambda n, core: (0, n)), place],
        ),
        out_shape=[pltpu.HBM((rows, cols), bf16), pltpu.HBM(shape, f32)],
        cost_estimate=cost(20),
        compiler_params=large,
    )(core, left, right, *after)


def filled(whole, other, core, turn, after=()):
    rows, cols = other.shape
    tile = cols // 2

    def body(core_ref, other_ref, *rest):
        wide = other_ref[...].astype(f32)
        rest[-1][...] = wide.T if turn else wide

    if turn:
        place = pl.BlockSpec((tile, rows), lambda n, core: (n, 1 - core[0]))
    else:
        place = pl.BlockSpec((rows, tile), lambda n, core: (1 - core[0], n))
    return pl.pallas_call(
        body,
        grid_spec=pltpu.PrefetchScalarGridSpec(
            num_scalar_prefetch=1,
            grid=(2,),
            in_specs=[
                pl.BlockSpec((rows, tile), lambda n, core: (0, n)),
            ]
            + [pl.BlockSpec(memory_space=pl.ANY)] * (1 + len(after)),
            out_specs=place,
        ),
        out_shape=pltpu.HBM(whole.shape, f32),
        input_output_aliases={2: 0},
        cost_estimate=cost(4.5),
        compiler_params=large,
    )(core, other, whole, *after)


def join_kernel(core_ref, own_ref, other_ref, *rest):
    mine = pl.program_id(0) == core_ref[0]
    rest[-1][...] = jnp.where(mine, own_ref[...], other_ref[...]).astype(f32)


def joined_halves(own, other, core, axis, after):
    rows, cols = own.shape
    part = pl.BlockSpec((rows, cols), lambda h, core: (0, 0))
    place = pl.BlockSpec((rows, cols), (lambda h, core: (h, 0)) if axis == 0 else (lambda h, core: (0, h)))
    shape = (2 * rows, cols) if axis == 0 else (rows, 2 * cols)
    return pl.pallas_call(
        join_kernel,
        grid_spec=pltpu.PrefetchScalarGridSpec(
            num_scalar_prefetch=1,
            grid=(2,),
            in_specs=[part, part] + [pl.BlockSpec(memory_space=pl.ANY)] * len(after),
            out_specs=place,
        ),
        out_shape=pltpu.HBM(shape, f32),
        cost_estimate=cost(4),
        compiler_params=large,
    )(core, own, other, *after)


def back_kernel(core_ref, weight_ref, cot_ref, *rest):
    rest[-1][...] = lax.dot_general(
        weight_ref[...], cot_ref[...], contract_cols, preferred_element_type=f32
    )


def down_back(core, cots, down, after):
    count, width = cots.shape
    hidden = down.shape[0] // 2
    tile = 512
    return pl.pallas_call(
        back_kernel,
        grid_spec=pltpu.PrefetchScalarGridSpec(
            num_scalar_prefetch=1,
            grid=(count // tile,),
            in_specs=[
                pl.BlockSpec((hidden, width), lambda i, core: (core[0], 0)),
                pl.BlockSpec((tile, width), lambda i, core: (i, 0)),
            ]
            + [pl.BlockSpec(memory_space=pl.ANY)] * len(after),
            out_specs=pl.BlockSpec((hidden, tile), lambda i, core: (0, i)),
        ),
        out_shape=jax.ShapeDtypeStruct((hidden, count), f32),
        cost_estimate=cost(20),
        compiler_params=large,
    )(core, down, cots, *after)


def flip_kernel(core_ref, one_ref, two_ref, *rest):
    rest[-2][...] = one_ref[...].astype(f32).T.astype(bf16)
    rest[-1][...] = two_ref[...].astype(f32).T.astype(bf16)


def flipped(one, two, core, after):
    width, hidden = one.shape[0], one.shape[1] // 2
    tile = 256
    source = pl.BlockSpec((tile, hidden), lambda n, core: (n, core[0]))
    result = pl.BlockSpec((hidden, tile), lambda n, core: (0, n))
    return pl.pallas_call(
        flip_kernel,
        grid_spec=pltpu.PrefetchScalarGridSpec(
            num_scalar_prefetch=1,
            grid=(width // tile,),
            in_specs=[source, source] + [pl.BlockSpec(memory_space=pl.ANY)] * len(after),
            out_specs=[result, result],
        ),
        out_shape=[jax.ShapeDtypeStruct((hidden, width), bf16)] * 2,
        cost_estimate=cost(8),
    )(core.astype(jnp.int32).reshape((1,)), one, two, *after)


def run(body, outs, args, scratch=(), after=(), scalar=False, micros=1):
    vmem = pl.BlockSpec(memory_space=pltpu.VMEM)
    specs = [vmem] * len(args)
    if scalar:
        specs[0] = pl.BlockSpec(memory_space=pltpu.SMEM)
    count = len(args)

    def whole(*refs):
        body(*refs[:count], *refs[count + len(after) :])

    return pl.pallas_call(
        whole,
        out_shape=outs,
        in_specs=specs + [pl.BlockSpec(memory_space=pl.ANY)] * len(after),
        out_specs=[vmem] * len(outs),
        scratch_shapes=scratch,
        cost_estimate=cost(micros),
        compiler_params=middle,
    )(*args, *after)


def run_rows(body, kind, args, count, after=()):
    rows, cols = args[0].shape
    block = pl.BlockSpec((count, cols), lambda n: (n, 0))
    row = pl.BlockSpec((1, cols), lambda n: (0, 0))

    def whole(*refs):
        body(*refs[: len(args)], refs[-1])

    return pl.pallas_call(
        whole,
        grid=(rows // count,),
        in_specs=[row if arg.shape[0] == 1 else block for arg in args]
        + [pl.BlockSpec(memory_space=pl.ANY)] * len(after),
        out_specs=block,
        out_shape=jax.ShapeDtypeStruct((rows, cols), kind),
        cost_estimate=brief,
        compiler_params=large,
    )(*args, *after)


def unpack_kernel(core_ref, flat_ref, other_ref, recur_ref, intake_ref, sums_ref, *, heads):
    head = recur_ref.shape[1]
    own, other = flat_ref[:head].astype(f32), other_ref[...].astype(f32)
    first = core_ref[0] == 0
    for ref, blocks in (
        (recur_ref, jnp.where(first, own, other)),
        (intake_ref, jnp.where(first, other, own)),
    ):
        for h in range(heads):
            ref[h] = blocks[:, h * head : (h + 1) * head]
    sums_ref[...] = flat_ref[head:].astype(f32)


def local(
    inputs,
    cotangent,
    segment_ids,
    norm_gain,
    branch_weight,
    stream_weight,
    conv_weight,
    conv_bias,
    recur_weight,
    recur_bias,
    intake_weight,
    intake_bias,
    decay_param,
    output_weight,
    mlp_gain,
    gate_weight,
    up_weight,
    down_weight,
    *,
    depth,
    square,
):
    line = square and depth == 4
    plain = not square
    core = lax.axis_index("core")
    core_id = core.astype(jnp.int32).reshape((1,))
    spot = jnp.zeros((1,), jnp.int32)
    if square:
        spot = spot + (2 * lax.axis_index("y") + lax.axis_index("x")).astype(jnp.int32)
    where = jnp.concatenate([spot, core_id])
    heads, head = recur_weight.shape[0], recur_weight.shape[1]
    width = heads * head
    length = segment_ids.shape[1]
    block, features = inputs.shape
    hidden_units = gate_weight.shape[1]
    shape = jax.ShapeDtypeStruct
    halves = [shape((block // 2, features), bf16)] * 2

    gain_one = norm_gain.astype(f32)[None, :]
    gain_two = mlp_gain.astype(f32)[None, :]
    normed_own = run(norm_kernel, halves, (inputs, gain_one))

    seg_row = segment_ids[0]
    masks = []
    for k in range(1, 4):
        earlier = jnp.concatenate([jnp.full((k,), -1, jnp.int32), seg_row[:-k]])
        masks.append((seg_row == earlier).astype(f32))
    joined = jnp.pad(jnp.stack(masks), ((0, 0), (0, 8)))
    joined = jnp.broadcast_to(joined[:, :, None], (3, length + 8, 128))
    square_low = shape((2, width, width), bf16)
    wide_high, wide_low = pl.pallas_call(
        prep_kernel, out_shape=[square_low, square_low], cost_estimate=brief
    )(recur_weight, intake_weight)
    gate_bias = jnp.stack([recur_bias, intake_bias])
    soft = (-decay_scale * jax.nn.softplus(-decay_param))[None, :]
    taps = conv_weight.astype(f32)

    if line:
        cots = lax.all_gather(cotangent, ALL, axis=0, tiled=True)

    normed_pieces = gather_row(normed_own, square, (wide_high,) if square else ())
    token = shape((length, width), f32)
    token_low = shape((length, width), bf16)
    row_low = shape((length, features), bf16)
    row_sends = send_shapes(length, features, plain)
    half_row = shape((length, features // 2), bf16)
    normed_mine, normed_theirs, branch_pre, stream_pre, gated, convolved, recur_gate, intake_gate, state, *sends = run(
        functools.partial(forward_kernel, count=len(normed_pieces), head=head, plain=plain),
        [half_row, half_row, token, token, token_low, token, token, token, token, *row_sends],
        (
            where,
            *normed_pieces,
            branch_weight,
            stream_weight,
            output_weight,
            joined,
            taps,
            conv_bias.astype(f32)[None, :],
            wide_high,
            wide_low,
            gate_bias,
            soft,
        ),
        [pltpu.VMEM((length, width), bf16)] * 2 + [pltpu.VMEM((length, features), bf16)],
        scalar=True,
        micros=20,
    )
    own_cots = cotangent
    if square:
        (own_cots,) = held((cotangent,), normed_pieces)
    own_cots = gather_blocks(own_cots, square)
    activ_grad = row_back(own_cots, down_weight)
    if square:
        sends[:2] = held(sends[:2], own_cots[1:])
    addends = scatter_row(sends, square, (activ_grad,) if square else ())

    hidden, one, two, normed_two = run(
        second_norm_kernel,
        [shape((block, features), f32), *halves, shape((block, features), bf16)],
        (inputs, gain_two, *addends),
    )
    if line:
        tokens = lax.all_gather(normed_two, ALL, axis=0, tiled=True)
        gate_turned, up_turned = flipped(gate_weight, up_weight, core, (gated,))
    mlp_pieces = gather_row((one, two), square, (gate_turned,) if line else ())
    tile = min(768, hidden_units)
    fixed = [pl.BlockSpec(piece.shape, lambda i: (0, 0)) for piece in mlp_pieces]
    column = pl.BlockSpec((length, tile), lambda i: (0, i))
    weight_column = pl.BlockSpec((features, tile), lambda i: (0, i))
    low_units = shape((length, hidden_units), bf16)
    kept = [] if line else [low_units, low_units]
    mlp_in, activ, *sends = pl.pallas_call(
        functools.partial(mlp_kernel, count=len(mlp_pieces), plain=plain, keep=not line),
        grid=(hidden_units // tile,),
        in_specs=[*fixed, column, weight_column, weight_column],
        out_specs=[pl.BlockSpec(row_low.shape, lambda i: (0, 0)), column]
        + [column] * len(kept)
        + [pl.BlockSpec(send.shape, lambda i: (0, 0)) for send in row_sends],
        out_shape=[row_low, low_units, *kept, *row_sends],
        scratch_shapes=[pltpu.VMEM((length, features), bf16), pltpu.VMEM((length, features), f32)],
        cost_estimate=cost(23),
        compiler_params=pltpu.CompilerParams(vmem_limit_bytes=56 * 1024 * 1024),
    )(*mlp_pieces, activ_grad, gate_weight, up_weight)
    kept, sends = sends[: len(kept)], sends[len(kept) :]
    beside = ()
    if line:
        grads = down_back(core_id, cots, down_weight, (sends[0],))
        beside = (grads,)
    addends = scatter_row(sends, square, beside)

    mlp_gain_part, resid_grad, one, two = run(
        functools.partial(norm_back_kernel, final=False),
        [shape((1, features), f32), shape((block, features), f32), *halves],
        (hidden, cotangent, gain_two, *addends),
    )
    (out_part,) = run(
        functools.partial(down_kernel, plain=plain), [row_low], (spot, activ, down_weight), after=(one,), scalar=True, micros=6
    )
    mlp_out = lax.psum_scatter(out_part, ("y", "x"), scatter_dimension=0, tiled=True)
    cot_pieces = gather_row((one, two), square, (out_part,) if square else ())

    cot_mine, cot_theirs, branch_low, state_grad = run(
        functools.partial(branch_back_kernel, count=len(cot_pieces)),
        [half_row, half_row, token_low, token],
        (where, *cot_pieces, output_weight, branch_pre, state),
        [pltpu.VMEM((length, features), bf16)],
        scalar=True,
        micros=6,
    )
    normed_other = sibling(normed_theirs)
    pairs = (
        gated,
        sibling(gated),
        cot_mine,
        sibling(cot_theirs),
        normed_mine,
        normed_other,
        branch_low,
        sibling(branch_low),
    )
    output_half, branch_half = run(
        pairs_kernel,
        [shape((width, features // 2), bf16), shape((features // 2, width), bf16)],
        pairs,
    )
    packed = shape((head + 32, width), f32)
    stream_low, flat_mine, flat_theirs, one_part = run(
        functools.partial(backward_kernel, head=head, plain=plain),
        [token_low, packed, packed, row_low],
        (
            where,
            state_grad,
            branch_low,
            branch_weight,
            stream_weight,
            stream_pre,
            joined,
            convolved,
            recur_gate,
            intake_gate,
            state,
            taps,
            wide_high,
            soft,
            normed_mine,
            normed_theirs,
            gain_one,
            mlp_gain_part,
        ),
        [
            pltpu.VMEM((2, width, width), f32),
            pltpu.VMEM((8, width), f32),
            pltpu.VMEM((2, length, width), bf16),
            pltpu.VMEM((length, width), bf16),
            pltpu.VMEM((length + 8, width), f32),
        ],
        after=(output_half, branch_half),
        scalar=True,
        micros=0,
    )
    if line:
        moved = line_move([(output_half, 0)])
    pairs = (normed_mine, normed_other, stream_low, sibling(stream_low))
    (stream_half,) = run(
        pairs_kernel, [shape((features // 2, width), bf16)], pairs, micros=0
    )
    last = ()
    if line:
        rows = branch_half.shape[0]
        (branch_half,) = run(
            below_kernel,
            [shape((rows + packed.shape[0], width), bf16)],
            (branch_half, flat_mine, sibling(flat_theirs)),
            after=(stream_half,),
            micros=0,
        )
        (output_sum,) = line_settle(moved, (branch_half, tokens))
        branch_half, stream_half, one_part = held((branch_half, stream_half, one_part), (output_sum,))
        moved = line_move([(output_sum, 1), (branch_half, 0)])
        activ_all, gate_all, up_all = mlp_rows(tokens, grads, gate_turned, up_turned, (output_sum,))
        output_sum, branch_sum = line_settle(moved, (activ_all,))
        gate_all, up_all, activ_all, stream_half = held(
            (gate_all, up_all, activ_all, stream_half), (branch_sum,)
        )
        moved = line_move([(output_sum, 2), (branch_sum, 1), (stream_half, 0)])
        gate_low, gate_w_grad = product(gate_all, tokens, core_id, True)
        up_low, up_w_grad = product(up_all, tokens, core_id, True, (gate_low,))
        output_sum, branch_sum, stream_sum = line_settle(moved, (up_low,))
        gate_low, up_low, activ_all = held((gate_low, up_low, activ_all), (stream_sum,))
        moved = line_move([(branch_sum, 2), (stream_sum, 1)])
        down_low, down_w_grad = product(activ_all, cots, core_id, False)
        gate_w_grad = filled(gate_w_grad, sibling(gate_low), core_id, True, (down_low,))
        up_w_grad = filled(up_w_grad, sibling(up_low), core_id, True, (gate_w_grad,))
        branch_sum, stream_sum = line_settle(moved, (up_w_grad,))
        branch_sum, flat_sum = branch_sum[:rows], branch_sum[rows:]
        (down_low,) = held((down_low,), (stream_sum,))
        moved = line_move([(stream_sum, 2)])
        last = (stream_sum,)
    else:
        (flat,) = run(sum_kernel, [packed], (flat_mine, sibling(flat_theirs)))

    one_grad = lax.psum_scatter(one_part, ("y", "x"), scatter_dimension=0, tiled=True)

    inputs_grad = run_rows(
        functools.partial(norm_back_kernel, final=True),
        bf16,
        (inputs, resid_grad, gain_one, one_grad),
        block // 4,
        last,
    )
    block_out = run_rows(add_kernel, bf16, (hidden, mlp_out), block // 4, last)

    def apart(flat_sum, beside):
        gates_other = sibling(flat_sum[:head])
        blocks = shape((heads, head, head), f32)
        found = run(
            functools.partial(unpack_kernel, heads=heads),
            [blocks, blocks, shape((8, width), f32)],
            (core_id, flat_sum[: head + 8], gates_other),
            after=beside[:1],
            scalar=True,
        )
        gains = flat_sum[head + 8 : head + 24, :256].astype(f32)
        if square:
            for axis, other in zip(("x", "y"), beside, strict=True):
                gains = gains + held((lax.ppermute(gains, axis, swap),), (other,))[0]
        else:
            gains = lax.psum(gains, ("y", "x"))
        return *found, gains

    def whole(own, axis, after=()):
        return joined_halves(own, sibling(own), core_id, axis, after)

    if line:
        output_w_grad = whole(output_sum, 1, (inputs_grad, block_out))
        branch_w_grad = whole(branch_sum, 0, (output_w_grad,))
        down_w_grad = filled(down_w_grad, sibling(down_low), core_id, False, (branch_w_grad,))
        recur_grad, intake_grad, sums, gains = apart(flat_sum, (output_w_grad, branch_w_grad))
        (stream_sum,) = line_settle(moved, (down_w_grad, recur_grad, gains))
        stream_w_grad = whole(stream_sum, 0)
    else:
        output_sum, branch_sum, stream_sum, flat_sum = (
            lax.psum(part, "z") for part in (output_half, branch_half, stream_half, flat)
        )
        recur_grad, intake_grad, sums, gains = apart(flat_sum, (inputs_grad, block_out))
        output_w_grad, branch_w_grad, stream_w_grad = (
            whole(output_sum, 1),
            whole(branch_sum, 0),
            whole(stream_sum, 0),
        )

        def over_rows(left, right):
            part = lax.dot_general(left, right, contract_rows, preferred_element_type=f32)
            return lax.psum(part.astype(bf16), ("z", "core")).astype(f32)

        gate_w_grad = over_rows(mlp_in, kept[0])
        up_w_grad = over_rows(mlp_in, kept[1])
        down_w_grad = over_rows(activ, jnp.concatenate(own_cots, axis=0))

    gains = gains.reshape(2, -1)
    return (
        block_out,
        inputs_grad,
        gains[0],
        branch_w_grad,
        stream_w_grad,
        sums[0:4],
        sums[4],
        recur_grad,
        sums[5],
        intake_grad,
        sums[6],
        sums[7] * decay_scale * jax.nn.sigmoid(-decay_param),
        output_w_grad,
        gains[1],
        gate_w_grad,
        up_w_grad,
        down_w_grad,
    )


def solution(mesh):
    depth = mesh.shape["dp"] // 2
    across = mesh.shape["mp"] // 2
    fine = Mesh(mesh.devices.reshape(depth, 2, 2, across), ALL)
    dp, mp = ("z", "core"), ("y", "x")
    cols, vec, blocks, rows = P(None, mp), P(mp), P(mp, None, None), P(mp, None)
    tokens = P(ALL, None)
    return jax.shard_map(
        functools.partial(local, depth=depth, square=across == 2),
        mesh=fine,
        in_specs=(
            tokens,
            tokens,
            P(dp, None),
            P(),
            cols,
            cols,
            cols,
            vec,
            blocks,
            vec,
            blocks,
            vec,
            vec,
            rows,
            P(),
            cols,
            cols,
            rows,
        ),
        out_specs=(
            tokens,
            tokens,
            P(),
            cols,
            cols,
            cols,
            vec,
            blocks,
            vec,
            blocks,
            vec,
            vec,
            rows,
            P(),
            cols,
            cols,
            rows,
        ),
        check_vma=False,
    )
```

```python
import functools

import jax
import jax.numpy as jnp
from jax import lax
from jax.experimental import pallas as pl
from jax.experimental.pallas import tpu as pltpu
from jax.sharding import Mesh
from jax.sharding import PartitionSpec as P

eps = 1e-06
decay_scale = 8.0
contract_rows = (((0,), (0,)), ((), ()))
contract_cols = (((1,), (1,)), ((), ()))
f32 = jnp.float32
bf16 = jnp.bfloat16
swap = [(0, 1), (1, 0)]


def cost(micros):
    return pl.CostEstimate(flops=0, bytes_accessed=int(micros * 3e6), transcendentals=0)


brief = cost(1)
large = pltpu.CompilerParams(vmem_limit_bytes=48 * 1024 * 1024)
middle = pltpu.CompilerParams(vmem_limit_bytes=32 * 1024 * 1024)
ALL = ("z", "core", "y", "x")
STEP = 16
root_two_over_pi = 0.7978845608028654


def pass_kernel(*refs):
    pass


def held(values, after):
    values, after = list(values), list(after)
    anywhere = pl.BlockSpec(memory_space=pl.ANY)
    return pl.pallas_call(
        pass_kernel,
        in_specs=[anywhere] * (len(values) + len(after)),
        out_specs=[anywhere] * len(values),
        out_shape=[jax.ShapeDtypeStruct(value.shape, value.dtype) for value in values],
        input_output_aliases={n: n for n in range(len(values))},
        cost_estimate=cost(0.1),
    )(*values, *after)


def gather_row(halves, square, beside=()):
    if not square:
        return [lax.all_gather(jnp.concatenate(halves, axis=0), ("y", "x"), axis=0, tiled=True)]
    one, two = halves
    one_x = lax.ppermute(one, "x", swap)
    two_y = lax.ppermute(two, "y", swap)
    two_x = lax.ppermute(two, "x", swap)
    one_y = lax.ppermute(one, "y", swap)
    if beside:
        one_x, two_y = held((one_x, two_y), beside)
    one_d = lax.ppermute(one_x, "y", swap)
    two_d = lax.ppermute(two_y, "x", swap)
    return [one, one_x, one_y, one_d, two, two_x, two_y, two_d]


def gather_blocks(block, square):
    if not square:
        return gather_row((block,), square)
    return [
        block,
        lax.ppermute(block, "x", swap),
        lax.ppermute(block, "y", swap),
        lax.ppermute(block, ("y", "x"), [(0, 3), (3, 0), (1, 2), (2, 1)]),
    ]


def scatter_row(sends, square, beside=()):
    if not square:
        return [lax.psum_scatter(sends[0], ("y", "x"), scatter_dimension=0, tiled=True)]
    to_x, to_y, keep_x, keep_y, own = sends
    got_x = lax.ppermute(to_x, "x", swap)
    got_y = lax.ppermute(to_y, "y", swap)
    if beside:
        got_x, got_y = held((got_x, got_y), beside)
    send_y, send_x = run(
        middle_kernel,
        [jax.ShapeDtypeStruct(keep_x.shape, bf16)] * 2,
        (got_x, got_y, keep_x, keep_y),
    )
    last_y = lax.ppermute(send_y, "y", swap)
    last_x = lax.ppermute(send_x, "x", swap)
    return [own, got_x, got_y, last_y, last_x]


def sibling(value):
    return lax.ppermute(value, "core", swap)


def line_move(pieces):
    pairs = [[(0, 1), (3, 2)], [(1, 2), (2, 1)], [(1, 0), (2, 3)]]
    return [(piece, stage, lax.ppermute(piece, "z", pairs[stage])) for piece, stage in pieces]


def settle_kernel(inner_ref, *refs, stages):
    count = len(stages)
    for n, stage in enumerate(stages):
        piece, other, out = refs[n], refs[count + n], refs[2 * count + n]
        if stage < 2:
            out[...] = (piece[...].astype(f32) + other[...].astype(f32)).astype(out.dtype)
        else:
            out[...] = jnp.where(inner_ref[0] == 1, piece[...], other[...])


def line_settle(moved, after):
    place = lax.axis_index("z")
    inner = ((place == 1) | (place == 2)).astype(jnp.int32).reshape((1,))
    pieces, stages, others = zip(*moved, strict=True)
    blocks = [
        pl.BlockSpec((piece.shape[0] // 4, piece.shape[1]), lambda n, inner: (n, 0)) for piece in pieces
    ]

    def body(inner_ref, *refs):
        settle_kernel(inner_ref, *refs[: 2 * len(pieces)], *refs[-len(pieces) :], stages=stages)

    return pl.pallas_call(
        body,
        grid_spec=pltpu.PrefetchScalarGridSpec(
            num_scalar_prefetch=1,
            grid=(4,),
            in_specs=[*blocks, *blocks] + [pl.BlockSpec(memory_space=pl.ANY)] * len(after),
            out_specs=blocks,
        ),
        out_shape=[pltpu.HBM(piece.shape, piece.dtype) for piece in pieces],
        cost_estimate=brief,
        compiler_params=large,
    )(inner, *pieces, *others, *after)


def assemble(pieces, out_ref):
    at = 0
    for piece in pieces:
        out_ref[at : at + piece.shape[0], :] = piece[...]
        at += piece.shape[0]


def split(whole_ref, core, mine_ref, theirs_ref):
    size = mine_ref.shape[1]
    for ref, which in ((mine_ref, core), (theirs_ref, 1 - core)):
        ref[...] = whole_ref[:, pl.ds(pl.multiple_of(which * size, 128), size)]


def pairs_kernel(*refs):
    count = len(refs) // 5
    for n in range(count):
        own_left, other_left, own_right, other_right = refs[4 * n : 4 * n + 4]
        out_ref = refs[4 * count + n]
        cols = out_ref.shape[1]
        for first in range(0, cols, 512):
            span = slice(first, min(first + 512, cols))
            out_ref[:, span] = (
                lax.dot_general(
                    own_left[...], own_right[:, span], contract_rows, preferred_element_type=f32
                )
                + lax.dot_general(
                    other_left[...], other_right[:, span], contract_rows, preferred_element_type=f32
                )
            ).astype(bf16)


def sum_kernel(one_ref, two_ref, out_ref):
    out_ref[...] = (one_ref[...] + two_ref[...]).astype(out_ref.dtype)


def below_kernel(top_ref, one_ref, two_ref, out_ref):
    rows = top_ref.shape[0]
    out_ref[:rows, :] = top_ref[...]
    out_ref[rows:, :] = (one_ref[...] + two_ref[...]).astype(out_ref.dtype)


def send_shapes(length, width, plain):
    if plain:
        return [jax.ShapeDtypeStruct((length, width), bf16)]
    block, cut = length // 4, width // 2
    return (
        [jax.ShapeDtypeStruct((2 * block, cut), bf16)] * 2
        + [jax.ShapeDtypeStruct((block, cut), bf16)] * 2
        + [jax.ShapeDtypeStruct((block, width), f32)]
    )


def emit(value, first, width, sends, plain, spot=None):
    last = first + value.shape[1]
    if spot is not None:
        half = value.shape[0] // 8
        for n in range(2):
            for k in range(4):
                start = pl.multiple_of((lax.bitwise_xor(k, spot) * 2 + n) * half, half)
                block = value[(n * 4 + k) * half : (n * 4 + k + 1) * half]
                sends[0][pl.ds(start, half), first:last] = block.astype(bf16)
        return
    if plain:
        sends[0][:, first:last] = value.astype(bf16)
        return
    to_x, to_y, keep_x, keep_y, own = sends
    cut = width // 2
    half = value.shape[0] // 8

    def put(ref, at, block, cols, kind):
        for n in range(2):
            rows = slice(n * 4 * half + block * half, n * 4 * half + (block + 1) * half)
            ref[at + n * half : at + (n + 1) * half, cols] = value[rows].astype(kind)

    put(own, 0, 0, slice(first, last), f32)
    if last <= cut:
        cols = slice(first, last)
        put(to_x, 0, 1, cols, bf16)
        put(to_x, 2 * half, 3, cols, bf16)
        put(keep_y, 0, 2, cols, bf16)
    else:
        cols = slice(first - cut, last - cut)
        put(to_y, 0, 2, cols, bf16)
        put(to_y, 2 * half, 3, cols, bf16)
        put(keep_x, 0, 1, cols, bf16)


def middle_kernel(got_x, got_y, keep_x, keep_y, send_y, send_x):
    block = keep_x.shape[0]
    send_y[...] = (keep_y[...].astype(f32) + got_x[block:].astype(f32)).astype(bf16)
    send_x[...] = (keep_x[...].astype(f32) + got_y[block:].astype(f32)).astype(bf16)


def finish(refs):
    if len(refs) == 1:
        return refs[0][...].astype(f32)
    own, got_x, got_y, last_y, last_x = refs
    block, cut = last_y.shape
    left = own[:, :cut] + got_x[:block].astype(f32) + last_y[...].astype(f32)
    right = own[:, cut:] + got_y[:block].astype(f32) + last_x[...].astype(f32)
    return jnp.concatenate([left, right], axis=1)


def mean_of(x):
    return jnp.mean(x, axis=-1, keepdims=True)


def norm_kernel(input_ref, gain_ref, one_ref, two_ref):
    values = input_ref[...].astype(f32)
    normed = (values * lax.rsqrt(mean_of(values * values) + eps) * gain_ref[...]).astype(bf16)
    half = normed.shape[0] // 2
    one_ref[...] = normed[:half]
    two_ref[...] = normed[half:]


def second_norm_kernel(input_ref, gain_ref, *refs):
    addends, (hidden_ref, one_ref, two_ref, all_ref) = refs[:-4], refs[-4:]
    hidden = input_ref[...].astype(f32) + finish(addends)
    hidden_ref[...] = hidden
    normed = (hidden * lax.rsqrt(mean_of(hidden * hidden) + eps) * gain_ref[...]).astype(bf16)
    half = normed.shape[0] // 2
    one_ref[...] = normed[:half]
    two_ref[...] = normed[half:]
    all_ref[...] = normed


def norm_back_kernel(value_ref, before_ref, gain_ref, *refs, final):
    outs = 1 if final else 4
    addends, outs = refs[:-outs], refs[-outs:]
    values = value_ref[...].astype(f32)
    scale = lax.rsqrt(mean_of(values * values) + eps)
    hat = values * scale
    grad = finish(addends)
    scaled = grad * gain_ref[...]
    total = before_ref[...].astype(f32) + scale * (scaled - hat * mean_of(scaled * hat))
    if final:
        outs[0][...] = total.astype(bf16)
        return
    outs[0][...] = jnp.sum(grad * hat, axis=0, keepdims=True)
    outs[1][...] = total
    low = total.astype(bf16)
    half = low.shape[0] // 2
    outs[2][...] = low[:half]
    outs[3][...] = low[half:]


def add_kernel(value_ref, *refs):
    refs[-1][...] = (value_ref[...] + finish(refs[:-1])).astype(bf16)


def mlp_kernel(*refs, count, plain, keep):
    pieces, (grad_ref, gate_w, up_w), refs = refs[:count], refs[count : count + 3], refs[count + 3 :]
    *outs, token_ref, total_ref = refs
    token_out, activ_ref, *outs = outs
    step = pl.program_id(0)

    @pl.when(step == 0)
    def _():
        assemble(pieces, token_ref)
        token_out[...] = token_ref[...]

    tokens = token_ref[...]
    gate_pre = jnp.dot(tokens, gate_w[...], preferred_element_type=f32)
    up_pre = jnp.dot(tokens, up_w[...], preferred_element_type=f32)
    activ_grad = grad_ref[...]
    value, slope = gelu_terms(gate_pre)
    activ_ref[...] = (value * up_pre).astype(bf16)
    gate_low = (activ_grad * up_pre * slope).astype(bf16)
    up_low = (activ_grad * value).astype(bf16)
    if keep:
        outs[0][...] = gate_low
        outs[1][...] = up_low
        outs = outs[2:]
    width = total_ref.shape[1]
    last = step == pl.num_programs(0) - 1
    for first in range(0, width, 512):
        cols = slice(first, first + 512)
        part = lax.dot_general(
            gate_low, gate_w[cols, :], contract_cols, preferred_element_type=f32
        ) + lax.dot_general(up_low, up_w[cols, :], contract_cols, preferred_element_type=f32)

        @pl.when(step == 0)
        def _(part=part, cols=cols):
            total_ref[:, cols] = part

        @pl.when(step > 0)
        def _(part=part, cols=cols):
            total_ref[:, cols] += part

    @pl.when(last)
    def _():
        for first in range(0, width, 512):
            emit(total_ref[:, first : first + 512], first, width, outs, plain)


def down_kernel(spot_ref, activ_ref, weight_ref, *sends, plain):
    spot = None if plain else spot_ref[0]
    width = weight_ref.shape[1]
    for first in range(0, width, 512):
        cols = slice(first, first + 512)
        value = jnp.dot(activ_ref[...], weight_ref[:, cols], preferred_element_type=f32)
        emit(value, first, width, sends, plain, spot)


def tile_span(first, last, head, width):
    low = (first // head) * head // 128 * 128
    high = min(width, -(-(((last - 1) // head + 1) * head) // 128) * 128)
    return low, high


def tiles(width):
    return [(n, min(n + 256, width)) for n in range(0, width, 256)]


def sigmoid(x):
    return 1.0 / (1.0 + jnp.exp(-x))


def decay_terms(gate, soft, link):
    log_decay = gate * soft
    decay = jnp.exp(log_decay)
    square = decay * decay
    x = 2.0 * log_decay
    series = 1.0 + x * (1.0 / 6.0) * (1.0 + x * (1.0 / 7.0))
    series = 1.0 + x * (1.0 / 4.0) * (1.0 + x * (1.0 / 5.0) * series)
    series = -x * (1.0 + x * (1.0 / 2.0) * (1.0 + x * (1.0 / 3.0) * series))
    gap = jnp.where(x > -0.3, series, 1.0 - square)
    root = jnp.sqrt(gap)
    return link * decay, square, root, link * root + (1.0 - link)


def gelu_terms(x):
    inner = jnp.tanh(root_two_over_pi * (x + 0.044715 * x * x * x))
    value = 0.5 * x * (1.0 + inner)
    slope = 0.5 * (1.0 + inner) + 0.5 * x * (1.0 - inner * inner) * root_two_over_pi * (
        1.0 + 3.0 * 0.044715 * x * x
    )
    return value, slope


def widen(mask, width):
    return jnp.concatenate([mask] * (-(-width // 128)), axis=1)[:, :width]


def token_place(length, spot, plain):
    block, half = length // 4, length // 8
    per_block = block // STEP
    per_half = half // STEP

    def offset(step):
        if plain:
            return pl.multiple_of(step * STEP, STEP)
        turn = lax.bitwise_xor(step // per_block, spot)
        inside = lax.rem(step, per_block)
        at = (inside // per_half) * (length // 2) + turn * half + lax.rem(inside, per_half) * STEP
        return pl.multiple_of(at, STEP)

    return offset


def prep_kernel(recur_ref, intake_ref, high_ref, low_ref):
    count, size, _ = recur_ref.shape
    for which, ref in ((0, recur_ref), (1, intake_ref)):
        for h in range(count):
            parts = [ref[h]]
            if h:
                parts.insert(0, jnp.zeros((size, h * size), f32))
            if h < count - 1:
                parts.append(jnp.zeros((size, (count - 1 - h) * size), f32))
            row = jnp.concatenate(parts, axis=1)
            high = row.astype(bf16)
            rows = slice(h * size, (h + 1) * size)
            high_ref[which, rows, :] = high
            low_ref[which, rows, :] = (row - high.astype(f32)).astype(bf16)


def forward_kernel(spot_ref, *refs, count, head, plain):
    pieces, refs = refs[:count], refs[count:]
    (branch_w, stream_w, output_w, joined_ref, taps_ref, bias_ref, high_ref, low_ref, gate_bias_ref, soft_ref), refs = (
        refs[:10],
        refs[10:],
    )
    (mine_ref, theirs_ref, branch_ref, stream_ref, gated_ref, conv_ref, recur_ref, intake_ref, state_ref), refs = (
        refs[:9],
        refs[9:],
    )
    *sends, part_high, part_low, normed_ref = refs
    assemble(pieces, normed_ref)
    split(normed_ref, spot_ref[1], mine_ref, theirs_ref)
    for first, last in tiles(branch_ref.shape[1]):
        cols = slice(first, last)
        branch_ref[:, cols] = jnp.dot(normed_ref[...], branch_w[:, cols], preferred_element_type=f32)
        stream_ref[:, cols] = jnp.dot(normed_ref[...], stream_w[:, cols], preferred_element_type=f32)
    length, width = branch_ref.shape
    steps = length // STEP
    offset = token_place(length, spot_ref[0], plain)

    def convolve(step, before):
        at = offset(step)
        here = pl.multiple_of(step * STEP, STEP)
        now = stream_ref[pl.ds(at, STEP), :]
        both = jnp.concatenate([before, now], axis=0)
        total = bias_ref[0:1, :] + taps_ref[0:1, :] * now
        for k in range(1, 4):
            mask = widen(joined_ref[k - 1, pl.ds(here, STEP), :], width)
            total = total + taps_ref[k : k + 1, :] * both[8 - k : 8 - k + STEP] * mask
        conv_ref[pl.ds(at, STEP), :] = total
        high = total.astype(bf16)
        part_high[pl.ds(here, STEP), :] = high
        part_low[pl.ds(here, STEP), :] = (total - high.astype(f32)).astype(bf16)
        return now[STEP - 8 :]

    lax.fori_loop(0, steps, convolve, jnp.zeros((8, width), f32), unroll=2)

    for which, out_ref in ((0, recur_ref), (1, intake_ref)):
        for first, last in tiles(width):
            low, high = tile_span(first, last, head, width)
            span, cols = slice(low, high), slice(first, last)
            high_part, low_part = high_ref[which, span, cols], low_ref[which, span, cols]
            pre = (
                jnp.dot(part_high[:, span], high_part, preferred_element_type=f32)
                + jnp.dot(part_low[:, span], high_part, preferred_element_type=f32)
                + jnp.dot(part_high[:, span], low_part, preferred_element_type=f32)
            )
            out_ref[:, cols] = pre + gate_bias_ref[which : which + 1, cols]

    rows = lax.broadcasted_iota(jnp.int32, (8, width), 0)
    soft = soft_ref[0:1, :]

    def advance(step, last_state):
        at = offset(step)
        here = pl.multiple_of(step * STEP, STEP)
        link = widen(joined_ref[0, pl.ds(here, STEP), :], width)
        conv = conv_ref[pl.ds(at, STEP), :]
        recur = sigmoid(recur_ref[pl.ds(here, STEP), :])
        intake = sigmoid(intake_ref[pl.ds(here, STEP), :])
        recur_ref[pl.ds(here, STEP), :] = recur
        intake_ref[pl.ds(here, STEP), :] = intake
        carried, square, root, multiplier = decay_terms(recur, soft, link)
        driven = multiplier * intake * conv
        found = []
        for part in range(STEP // 8):
            a = carried[8 * part : 8 * part + 8]
            b = driven[8 * part : 8 * part + 8]
            for shift in (1, 2, 4):
                a_before = jnp.where(rows >= shift, pltpu.roll(a, shift, 0), 1.0)
                b_before = jnp.where(rows >= shift, pltpu.roll(b, shift, 0), 0.0)
                b = b + a * b_before
                a = a * a_before
            state = b + a * last_state
            last_state = state[7:8]
            found.append(state)
        state = jnp.concatenate(found, axis=0)
        state_ref[pl.ds(at, STEP), :] = state
        value, slope = gelu_terms(branch_ref[pl.ds(at, STEP), :])
        gated_ref[pl.ds(at, STEP), :] = (value * state).astype(bf16)
        return last_state

    lax.fori_loop(0, steps, advance, jnp.zeros((1, width), f32), unroll=2)
    step_cols = 512
    for first in range(0, output_w.shape[1], step_cols):
        cols = slice(first, first + step_cols)
        value = jnp.dot(gated_ref[...], output_w[:, cols], preferred_element_type=f32)
        emit(value, first, output_w.shape[1], sends, plain)


def branch_back_kernel(spot_ref, *refs, count):
    pieces, (output_w, branch_ref, state_ref), refs = refs[:count], refs[count : count + 3], refs[count + 3 :]
    mine_ref, theirs_ref, branch_grad_ref, grad_ref, cot_ref = refs
    assemble(pieces, cot_ref)
    split(cot_ref, spot_ref[1], mine_ref, theirs_ref)
    length, width = branch_ref.shape
    for first, last in tiles(width):
        cols = slice(first, last)
        grad_ref[:, cols] = lax.dot_general(
            cot_ref[...], output_w[cols, :], contract_cols, preferred_element_type=f32
        )

    def rows(step, _):
        at = pl.ds(pl.multiple_of(step * STEP, STEP), STEP)
        value, slope = gelu_terms(branch_ref[at, :])
        grad = grad_ref[at, :]
        branch_grad_ref[at, :] = (grad * state_ref[at, :] * slope).astype(bf16)
        grad_ref[at, :] = grad * value
        return _

    lax.fori_loop(0, length // STEP, rows, 0)


def backward_kernel(
    spot_ref,
    grad_ref,
    branch_grad_ref,
    branch_w,
    stream_w,
    stream_ref,
    joined_ref,
    conv_ref,
    recur_ref,
    intake_ref,
    state_ref,
    taps_ref,
    high_ref,
    soft_ref,
    normed_mine,
    normed_theirs,
    gain_ref,
    other_gains,
    stream_grad_ref,
    mine_ref,
    theirs_ref,
    *refs,
    head,
    plain,
):
    *sends, gates_ref, sums_ref, pre_ref, conv_low, conv_grad = refs
    length, width = grad_ref.shape
    steps = length // STEP
    offset = token_place(length, spot_ref[0], plain)

    rows = lax.broadcasted_iota(jnp.int32, (8, width), 0)
    soft = soft_ref[0:1, :]
    count = STEP // 8

    def fold(value):
        total = value[0:8]
        for part in range(1, count):
            total = total + value[8 * part : 8 * part + 8]
        return total

    def retreat(turn, kept):
        after_carried, after_adjoint, decay_sum, recur_sum, intake_sum = kept
        step = steps - 1 - turn
        at = offset(step)
        at_before = offset(jnp.maximum(step - 1, 0))
        here = pl.multiple_of(step * STEP, STEP)
        link = widen(joined_ref[0, pl.ds(here, STEP), :], width)
        conv = conv_ref[pl.ds(at, STEP), :]
        recur = recur_ref[pl.ds(here, STEP), :]
        intake = intake_ref[pl.ds(here, STEP), :]
        carried, square, root, multiplier = decay_terms(recur, soft, link)
        grad = grad_ref[pl.ds(at, STEP), :]
        found = []
        for part in reversed(range(count)):
            own = carried[8 * part : 8 * part + 8]
            a = jnp.where(rows < 7, pltpu.roll(own, 7, 0), after_carried)
            b = grad[8 * part : 8 * part + 8]
            for shift in (1, 2, 4):
                a_after = jnp.where(rows < 8 - shift, pltpu.roll(a, 8 - shift, 0), 1.0)
                b_after = jnp.where(rows < 8 - shift, pltpu.roll(b, 8 - shift, 0), 0.0)
                b = b + a * b_after
                a = a * a_after
            adjoint = b + a * after_adjoint
            after_adjoint = adjoint[0:1]
            after_carried = own[0:1]
            found.append(adjoint)
        adjoint = jnp.concatenate(found[::-1], axis=0)
        state = state_ref[pl.ds(at, STEP), :]
        tail = state_ref[pl.ds(at_before + (STEP - 8), 8), :]
        earlier = jnp.concatenate([tail, state], axis=0)[7 : 7 + STEP]
        driven_part = adjoint * intake
        log_grad = adjoint * earlier * carried - driven_part * conv * link * square / root
        recur_grad = log_grad * soft * recur * (1.0 - recur)
        spread = driven_part * multiplier
        intake_grad = spread * conv * (1.0 - intake)
        pre_ref[0, pl.ds(here, STEP), :] = recur_grad.astype(bf16)
        pre_ref[1, pl.ds(here, STEP), :] = intake_grad.astype(bf16)
        conv_low[pl.ds(here, STEP), :] = conv.astype(bf16)
        conv_grad[pl.ds(here, STEP), :] = spread
        return (
            after_carried,
            after_adjoint,
            decay_sum + fold(log_grad * recur),
            recur_sum + fold(recur_grad),
            intake_sum + fold(intake_grad),
        )

    line = jnp.zeros((1, width), f32)
    eight = jnp.zeros((8, width), f32)
    kept = lax.fori_loop(0, steps, retreat, (line, line, eight, eight, eight), unroll=2)
    sums_ref[5:6, :] = jnp.sum(kept[3], axis=0, keepdims=True)
    sums_ref[6:7, :] = jnp.sum(kept[4], axis=0, keepdims=True)
    sums_ref[7:8, :] = jnp.sum(kept[2], axis=0, keepdims=True)

    conv_grad[length : length + 8, :] = eight
    for first, last in tiles(width):
        low, high = tile_span(first, last, head, width)
        span, cols = slice(low, high), slice(first, last)
        total = conv_grad[0:length, cols]
        for which in range(2):
            total = total + lax.dot_general(
                pre_ref[which, :, span], high_ref[which, cols, span], contract_cols, preferred_element_type=f32
            )
            gates_ref[which, span, cols] = lax.dot_general(
                conv_low[:, span], pre_ref[which, :, cols], contract_rows, preferred_element_type=f32
            )
        conv_grad[0:length, cols] = total

    def unwind(step, kept):
        at = offset(step)
        here = pl.multiple_of(step * STEP, STEP)
        ahead = conv_grad[pl.ds(here, STEP + 8), :]
        now = stream_ref[pl.ds(at, STEP), :]
        total = taps_ref[0:1, :] * ahead[0:STEP]
        sums = [kept[0] + fold(ahead[0:STEP] * now)]
        for k in range(1, 4):
            mask = widen(joined_ref[k - 1, pl.ds(here, STEP + 8), :], width)
            moved = (ahead * mask)[k : k + STEP]
            total = total + taps_ref[k : k + 1, :] * moved
            sums.append(kept[k] + fold(moved * now))
        stream_grad_ref[pl.ds(at, STEP), :] = total.astype(bf16)
        return (*sums, kept[4] + fold(ahead[0:STEP]))

    kept = lax.fori_loop(0, steps, unwind, (eight,) * 5, unroll=2)
    for k in range(5):
        sums_ref[k : k + 1, :] = jnp.sum(kept[k], axis=0, keepdims=True)
    count = width // head
    lanes = lax.broadcasted_iota(jnp.int32, (head, width), 1)
    for out_ref, which in ((mine_ref, spot_ref[1]), (theirs_ref, 1 - spot_ref[1])):
        blocks = gates_ref[which, 0:head, :]
        for h in range(1, count):
            blocks = jnp.where(lanes >= h * head, gates_ref[which, h * head : (h + 1) * head, :], blocks)
        out_ref[0:head, :] = blocks
        out_ref[head : head + 8, :] = sums_ref[...]
        out_ref[head + 8 :, :] = jnp.zeros((out_ref.shape[0] - head - 8, width), f32)

    step_cols = 512
    for first in range(0, branch_w.shape[0], step_cols):
        cols = slice(first, first + step_cols)
        value = lax.dot_general(
            branch_grad_ref[...], branch_w[cols, :], contract_cols, preferred_element_type=f32
        ) + lax.dot_general(
            stream_grad_ref[...], stream_w[cols, :], contract_cols, preferred_element_type=f32
        )
        half = normed_mine.shape[1]
        inside = slice(first % half, first % half + step_cols)
        mine = spot_ref[1] == first // half
        normed = jnp.where(mine, normed_mine[:, inside], normed_theirs[:, inside]).astype(f32)
        gains = jnp.sum(value * normed, axis=0, keepdims=True) / gain_ref[:, cols]
        for part in range(step_cols // 256):
            row = head + 8 + first // 256 + part
            below = row + branch_w.shape[0] // 256
            at = slice(part * 256, (part + 1) * 256)
            for out_ref in (mine_ref, theirs_ref):
                out_ref[row : row + 1, 0:256] = gains[:, at]
                out_ref[below : below + 1, 0:256] = other_gains[:, cols][:, at]
        emit(value, first, branch_w.shape[0], sends, plain, None if plain else spot_ref[0])


def rows_kernel(token_ref, grad_ref, gate_ref, up_ref, *rest):
    activ_ref, gate_out, up_out = rest[-3:]
    tokens = token_ref[...]
    hidden = gate_ref.shape[0]
    part = hidden // 3
    for n in range(3):
        rows = slice(n * part, (n + 1) * part)
        gate_pre = lax.dot_general(gate_ref[rows], tokens, contract_cols, preferred_element_type=f32)
        up_pre = lax.dot_general(up_ref[rows], tokens, contract_cols, preferred_element_type=f32)
        activ_grad = grad_ref[rows]
        value, slope = gelu_terms(gate_pre)
        activ_ref[rows] = (value * up_pre).astype(bf16)
        gate_out[rows] = (activ_grad * up_pre * slope).astype(bf16)
        up_out[rows] = (activ_grad * value).astype(bf16)


def mlp_rows(tokens, grads, gate, up, after):
    count, width = tokens.shape
    hidden = gate.shape[0]
    tile = 512
    tall = pl.BlockSpec((hidden, tile), lambda i: (0, i))
    weight = pl.BlockSpec((hidden, width), lambda i: (0, 0))
    return pl.pallas_call(
        rows_kernel,
        grid=(count // tile,),
        in_specs=[pl.BlockSpec((tile, width), lambda i: (i, 0)), tall, weight, weight]
        + [pl.BlockSpec(memory_space=pl.ANY)] * len(after),
        out_specs=[tall, tall, tall],
        out_shape=[jax.ShapeDtypeStruct((hidden, count), bf16)] * 3,
        cost_estimate=cost(34),
        compiler_params=large,
    )(tokens, grads, gate, up, *after)


def row_back_kernel(*refs, count):
    pieces, (weight_ref, out_ref, rows_ref) = refs[:count], refs[count:]

    @pl.when(pl.program_id(0) == 0)
    def _():
        half = pieces[0].shape[0] // 2
        at = 0
        for n in range(2):
            for piece in pieces:
                rows_ref[at : at + half, :] = piece[n * half : (n + 1) * half, :]
                at += half

    out_ref[...] = lax.dot_general(
        rows_ref[...], weight_ref[...], contract_cols, preferred_element_type=f32
    )


def row_back(pieces, down):
    hidden, width = down.shape
    length = sum(piece.shape[0] for piece in pieces)
    tile = min(512, hidden)
    return pl.pallas_call(
        functools.partial(row_back_kernel, count=len(pieces)),
        grid=(hidden // tile,),
        in_specs=[pl.BlockSpec(piece.shape, lambda i: (0, 0)) for piece in pieces]
        + [pl.BlockSpec((tile, width), lambda i: (i, 0))],
        out_specs=pl.BlockSpec((length, tile), lambda i: (0, i)),
        out_shape=jax.ShapeDtypeStruct((length, hidden), f32),
        scratch_shapes=[pltpu.VMEM((length, width), bf16)],
        cost_estimate=cost(6),
        compiler_params=large,
    )(*pieces, down)


def product(left, right, core, turn, after=()):
    rows, depth = left.shape
    cols = right.shape[1]
    tile = 256

    def body(core_ref, left_ref, right_ref, *rest):
        low_ref, whole_ref = rest[-2:]
        low = jnp.dot(left_ref[...], right_ref[...], preferred_element_type=f32).astype(bf16)
        low_ref[...] = low
        wide = low.astype(f32)
        whole_ref[...] = wide.T if turn else wide

    if turn:
        place = pl.BlockSpec((tile, rows), lambda n, core: (n, core[0]))
        shape = (cols, 2 * rows)
    else:
        place = pl.BlockSpec((rows, tile), lambda n, core: (core[0], n))
        shape = (2 * rows, cols)
    return pl.pallas_call(
        body,
        grid_spec=pltpu.PrefetchScalarGridSpec(
            num_scalar_prefetch=1,
            grid=(cols // tile,),
            in_specs=[
                pl.BlockSpec((rows, depth), lambda n, core: (0, 0)),
                pl.BlockSpec((depth, tile), lambda n, core: (0, n)),
            ]
            + [pl.BlockSpec(memory_space=pl.ANY)] * len(after),
            out_specs=[pl.BlockSpec((rows, tile), lambda n, core: (0, n)), place],
        ),
        out_shape=[pltpu.HBM((rows, cols), bf16), pltpu.HBM(shape, f32)],
        cost_estimate=cost(20),
        compiler_params=large,
    )(core, left, right, *after)


def filled(whole, other, core, turn, after=()):
    rows, cols = other.shape
    tile = cols // 2

    def body(core_ref, other_ref, *rest):
        wide = other_ref[...].astype(f32)
        rest[-1][...] = wide.T if turn else wide

    if turn:
        place = pl.BlockSpec((tile, rows), lambda n, core: (n, 1 - core[0]))
    else:
        place = pl.BlockSpec((rows, tile), lambda n, core: (1 - core[0], n))
    return pl.pallas_call(
        body,
        grid_spec=pltpu.PrefetchScalarGridSpec(
            num_scalar_prefetch=1,
            grid=(2,),
            in_specs=[
                pl.BlockSpec((rows, tile), lambda n, core: (0, n)),
            ]
            + [pl.BlockSpec(memory_space=pl.ANY)] * (1 + len(after)),
            out_specs=place,
        ),
        out_shape=pltpu.HBM(whole.shape, f32),
        input_output_aliases={2: 0},
        cost_estimate=cost(4.5),
        compiler_params=large,
    )(core, other, whole, *after)


def join_kernel(core_ref, own_ref, other_ref, *rest):
    mine = pl.program_id(0) == core_ref[0]
    rest[-1][...] = jnp.where(mine, own_ref[...], other_ref[...]).astype(f32)


def joined_halves(own, other, core, axis, after):
    rows, cols = own.shape
    part = pl.BlockSpec((rows, cols), lambda h, core: (0, 0))
    place = pl.BlockSpec((rows, cols), (lambda h, core: (h, 0)) if axis == 0 else (lambda h, core: (0, h)))
    shape = (2 * rows, cols) if axis == 0 else (rows, 2 * cols)
    return pl.pallas_call(
        join_kernel,
        grid_spec=pltpu.PrefetchScalarGridSpec(
            num_scalar_prefetch=1,
            grid=(2,),
            in_specs=[part, part] + [pl.BlockSpec(memory_space=pl.ANY)] * len(after),
            out_specs=place,
        ),
        out_shape=pltpu.HBM(shape, f32),
        cost_estimate=cost(4),
        compiler_params=large,
    )(core, own, other, *after)


def back_kernel(core_ref, weight_ref, cot_ref, *rest):
    rest[-1][...] = lax.dot_general(
        weight_ref[...], cot_ref[...], contract_cols, preferred_element_type=f32
    )


def down_back(core, cots, down, after):
    count, width = cots.shape
    hidden = down.shape[0] // 2
    tile = 512
    return pl.pallas_call(
        back_kernel,
        grid_spec=pltpu.PrefetchScalarGridSpec(
            num_scalar_prefetch=1,
            grid=(count // tile,),
            in_specs=[
                pl.BlockSpec((hidden, width), lambda i, core: (core[0], 0)),
                pl.BlockSpec((tile, width), lambda i, core: (i, 0)),
            ]
            + [pl.BlockSpec(memory_space=pl.ANY)] * len(after),
            out_specs=pl.BlockSpec((hidden, tile), lambda i, core: (0, i)),
        ),
        out_shape=jax.ShapeDtypeStruct((hidden, count), f32),
        cost_estimate=cost(20),
        compiler_params=large,
    )(core, down, cots, *after)


def flip_kernel(core_ref, one_ref, two_ref, *rest):
    rest[-2][...] = one_ref[...].astype(f32).T.astype(bf16)
    rest[-1][...] = two_ref[...].astype(f32).T.astype(bf16)


def flipped(one, two, core, after):
    width, hidden = one.shape[0], one.shape[1] // 2
    tile = 256
    source = pl.BlockSpec((tile, hidden), lambda n, core: (n, core[0]))
    result = pl.BlockSpec((hidden, tile), lambda n, core: (0, n))
    return pl.pallas_call(
        flip_kernel,
        grid_spec=pltpu.PrefetchScalarGridSpec(
            num_scalar_prefetch=1,
            grid=(width // tile,),
            in_specs=[source, source] + [pl.BlockSpec(memory_space=pl.ANY)] * len(after),
            out_specs=[result, result],
        ),
        out_shape=[jax.ShapeDtypeStruct((hidden, width), bf16)] * 2,
        cost_estimate=cost(8),
    )(core.astype(jnp.int32).reshape((1,)), one, two, *after)


def run(body, outs, args, scratch=(), after=(), scalar=False, micros=1):
    vmem = pl.BlockSpec(memory_space=pltpu.VMEM)
    specs = [vmem] * len(args)
    if scalar:
        specs[0] = pl.BlockSpec(memory_space=pltpu.SMEM)
    count = len(args)

    def whole(*refs):
        body(*refs[:count], *refs[count + len(after) :])

    return pl.pallas_call(
        whole,
        out_shape=outs,
        in_specs=specs + [pl.BlockSpec(memory_space=pl.ANY)] * len(after),
        out_specs=[vmem] * len(outs),
        scratch_shapes=scratch,
        cost_estimate=cost(micros),
        compiler_params=middle,
    )(*args, *after)


def run_rows(body, kind, args, count, after=()):
    rows, cols = args[0].shape
    block = pl.BlockSpec((count, cols), lambda n: (n, 0))
    row = pl.BlockSpec((1, cols), lambda n: (0, 0))

    def whole(*refs):
        body(*refs[: len(args)], refs[-1])

    return pl.pallas_call(
        whole,
        grid=(rows // count,),
        in_specs=[row if arg.shape[0] == 1 else block for arg in args]
        + [pl.BlockSpec(memory_space=pl.ANY)] * len(after),
        out_specs=block,
        out_shape=jax.ShapeDtypeStruct((rows, cols), kind),
        cost_estimate=brief,
        compiler_params=large,
    )(*args, *after)


def unpack_kernel(core_ref, flat_ref, other_ref, recur_ref, intake_ref, sums_ref, *, heads):
    head = recur_ref.shape[1]
    own, other = flat_ref[:head].astype(f32), other_ref[...].astype(f32)
    first = core_ref[0] == 0
    for ref, blocks in (
        (recur_ref, jnp.where(first, own, other)),
        (intake_ref, jnp.where(first, other, own)),
    ):
        for h in range(heads):
            ref[h] = blocks[:, h * head : (h + 1) * head]
    sums_ref[...] = flat_ref[head : head + 16].astype(f32)[:8]


def local(
    inputs,
    cotangent,
    segment_ids,
    norm_gain,
    branch_weight,
    stream_weight,
    conv_weight,
    conv_bias,
    recur_weight,
    recur_bias,
    intake_weight,
    intake_bias,
    decay_param,
    output_weight,
    mlp_gain,
    gate_weight,
    up_weight,
    down_weight,
    *,
    depth,
    square,
):
    line = square and depth == 4
    plain = not square
    core = lax.axis_index("core")
    core_id = core.astype(jnp.int32).reshape((1,))
    spot = jnp.zeros((1,), jnp.int32)
    if square:
        spot = spot + (2 * lax.axis_index("y") + lax.axis_index("x")).astype(jnp.int32)
    where = jnp.concatenate([spot, core_id])
    heads, head = recur_weight.shape[0], recur_weight.shape[1]
    width = heads * head
    length = segment_ids.shape[1]
    block, features = inputs.shape
    hidden_units = gate_weight.shape[1]
    shape = jax.ShapeDtypeStruct
    halves = [shape((block // 2, features), bf16)] * 2

    gain_one = norm_gain.astype(f32)[None, :]
    gain_two = mlp_gain.astype(f32)[None, :]
    normed_own = run(norm_kernel, halves, (inputs, gain_one))

    seg_row = segment_ids[0]
    masks = []
    for k in range(1, 4):
        earlier = jnp.concatenate([jnp.full((k,), -1, jnp.int32), seg_row[:-k]])
        masks.append((seg_row == earlier).astype(f32))
    joined = jnp.pad(jnp.stack(masks), ((0, 0), (0, 8)))
    joined = jnp.broadcast_to(joined[:, :, None], (3, length + 8, 128))
    square_low = shape((2, width, width), bf16)
    wide_high, wide_low = pl.pallas_call(
        prep_kernel, out_shape=[square_low, square_low], cost_estimate=brief
    )(recur_weight, intake_weight)
    gate_bias = jnp.stack([recur_bias, intake_bias])
    soft = (-decay_scale * jax.nn.softplus(-decay_param))[None, :]
    taps = conv_weight.astype(f32)

    if line:
        cots = lax.all_gather(cotangent, ALL, axis=0, tiled=True)

    normed_pieces = gather_row(normed_own, square, (wide_high,) if square else ())
    token = shape((length, width), f32)
    token_low = shape((length, width), bf16)
    row_low = shape((length, features), bf16)
    row_sends = send_shapes(length, features, plain)
    half_row = shape((length, features // 2), bf16)
    normed_mine, normed_theirs, branch_pre, stream_pre, gated, convolved, recur_gate, intake_gate, state, *sends = run(
        functools.partial(forward_kernel, count=len(normed_pieces), head=head, plain=plain),
        [half_row, half_row, token, token, token_low, token, token, token, token, *row_sends],
        (
            where,
            *normed_pieces,
            branch_weight,
            stream_weight,
            output_weight,
            joined,
            taps,
            conv_bias.astype(f32)[None, :],
            wide_high,
            wide_low,
            gate_bias,
            soft,
        ),
        [pltpu.VMEM((length, width), bf16)] * 2 + [pltpu.VMEM((length, features), bf16)],
        scalar=True,
        micros=20,
    )
    own_cots = cotangent
    if square:
        (own_cots,) = held((cotangent,), normed_pieces)
    own_cots = gather_blocks(own_cots, square)
    activ_grad = row_back(own_cots, down_weight)
    if square:
        sends[:2] = held(sends[:2], own_cots[1:])
    addends = scatter_row(sends, square, (activ_grad,) if square else ())

    hidden, one, two, normed_two = run(
        second_norm_kernel,
        [shape((block, features), f32), *halves, shape((block, features), bf16)],
        (inputs, gain_two, *addends),
    )
    if line:
        tokens = lax.all_gather(normed_two, ALL, axis=0, tiled=True)
        gate_turned, up_turned = flipped(gate_weight, up_weight, core, (gated,))
    mlp_pieces = gather_row((one, two), square, (gate_turned,) if line else ())
    tile = min(768, hidden_units)
    fixed = [pl.BlockSpec(piece.shape, lambda i: (0, 0)) for piece in mlp_pieces]
    column = pl.BlockSpec((length, tile), lambda i: (0, i))
    weight_column = pl.BlockSpec((features, tile), lambda i: (0, i))
    low_units = shape((length, hidden_units), bf16)
    kept = [] if line else [low_units, low_units]
    mlp_in, activ, *sends = pl.pallas_call(
        functools.partial(mlp_kernel, count=len(mlp_pieces), plain=plain, keep=not line),
        grid=(hidden_units // tile,),
        in_specs=[*fixed, column, weight_column, weight_column],
        out_specs=[pl.BlockSpec(row_low.shape, lambda i: (0, 0)), column]
        + [column] * len(kept)
        + [pl.BlockSpec(send.shape, lambda i: (0, 0)) for send in row_sends],
        out_shape=[row_low, low_units, *kept, *row_sends],
        scratch_shapes=[pltpu.VMEM((length, features), bf16), pltpu.VMEM((length, features), f32)],
        cost_estimate=cost(23),
        compiler_params=pltpu.CompilerParams(vmem_limit_bytes=56 * 1024 * 1024),
    )(*mlp_pieces, activ_grad, gate_weight, up_weight)
    kept, sends = sends[: len(kept)], sends[len(kept) :]
    beside = ()
    if line:
        grads = down_back(core_id, cots, down_weight, (sends[0],))
        beside = (grads,)
    addends = scatter_row(sends, square, beside)

    mlp_gain_part, resid_grad, one, two = run(
        functools.partial(norm_back_kernel, final=False),
        [shape((1, features), f32), shape((block, features), f32), *halves],
        (hidden, cotangent, gain_two, *addends),
    )
    (out_part,) = run(
        functools.partial(down_kernel, plain=plain), [row_low], (spot, activ, down_weight), after=(one,), scalar=True, micros=6
    )
    mlp_out = lax.psum_scatter(out_part, ("y", "x"), scatter_dimension=0, tiled=True)
    cot_pieces = gather_row((one, two), square, (out_part,) if square else ())

    cot_mine, cot_theirs, branch_low, state_grad = run(
        functools.partial(branch_back_kernel, count=len(cot_pieces)),
        [half_row, half_row, token_low, token],
        (where, *cot_pieces, output_weight, branch_pre, state),
        [pltpu.VMEM((length, features), bf16)],
        scalar=True,
        micros=6,
    )
    normed_other = sibling(normed_theirs)
    pairs = (
        gated,
        sibling(gated),
        cot_mine,
        sibling(cot_theirs),
        normed_mine,
        normed_other,
        branch_low,
        sibling(branch_low),
    )
    output_half, branch_half = run(
        pairs_kernel,
        [shape((width, features // 2), bf16), shape((features // 2, width), bf16)],
        pairs,
    )
    packed = shape((head + 32, width), f32)
    stream_low, flat_mine, flat_theirs, one_part = run(
        functools.partial(backward_kernel, head=head, plain=plain),
        [token_low, packed, packed, row_low],
        (
            where,
            state_grad,
            branch_low,
            branch_weight,
            stream_weight,
            stream_pre,
            joined,
            convolved,
            recur_gate,
            intake_gate,
            state,
            taps,
            wide_high,
            soft,
            normed_mine,
            normed_theirs,
            gain_one,
            mlp_gain_part,
        ),
        [
            pltpu.VMEM((2, width, width), f32),
            pltpu.VMEM((8, width), f32),
            pltpu.VMEM((2, length, width), bf16),
            pltpu.VMEM((length, width), bf16),
            pltpu.VMEM((length + 8, width), f32),
        ],
        after=(output_half, branch_half),
        scalar=True,
        micros=0,
    )
    if line:
        moved = line_move([(output_half, 0)])
    pairs = (normed_mine, normed_other, stream_low, sibling(stream_low))
    (stream_half,) = run(
        pairs_kernel, [shape((features // 2, width), bf16)], pairs, micros=0
    )
    last = ()
    if line:
        rows = branch_half.shape[0]
        (branch_half,) = run(
            below_kernel,
            [shape((rows + packed.shape[0], width), bf16)],
            (branch_half, flat_mine, sibling(flat_theirs)),
            after=(stream_half,),
            micros=0,
        )
        (output_sum,) = line_settle(moved, (branch_half, tokens))
        branch_half, stream_half, one_part = held((branch_half, stream_half, one_part), (output_sum,))
        moved = line_move([(output_sum, 1), (branch_half, 0)])
        activ_all, gate_all, up_all = mlp_rows(tokens, grads, gate_turned, up_turned, (output_sum,))
        output_sum, branch_sum = line_settle(moved, (activ_all,))
        gate_all, up_all, activ_all, stream_half = held(
            (gate_all, up_all, activ_all, stream_half), (branch_sum,)
        )
        moved = line_move([(output_sum, 2), (branch_sum, 1), (stream_half, 0)])
        gate_low, gate_w_grad = product(gate_all, tokens, core_id, True)
        up_low, up_w_grad = product(up_all, tokens, core_id, True, (gate_low,))
        output_sum, branch_sum, stream_sum = line_settle(moved, (up_low,))
        gate_low, up_low, activ_all = held((gate_low, up_low, activ_all), (stream_sum,))
        moved = line_move([(branch_sum, 2), (stream_sum, 1)])
        down_low, down_w_grad = product(activ_all, cots, core_id, False)
        gate_w_grad = filled(gate_w_grad, sibling(gate_low), core_id, True, (down_low,))
        up_w_grad = filled(up_w_grad, sibling(up_low), core_id, True, (gate_w_grad,))
        branch_sum, stream_sum = line_settle(moved, (up_w_grad,))
        branch_sum, flat_sum = branch_sum[:rows], branch_sum[rows:]
        (down_low,) = held((down_low,), (stream_sum,))
        moved = line_move([(stream_sum, 2)])
        last = (stream_sum,)
    else:
        (flat,) = run(sum_kernel, [packed], (flat_mine, sibling(flat_theirs)))

    one_grad = lax.psum_scatter(one_part, ("y", "x"), scatter_dimension=0, tiled=True)

    inputs_grad = run_rows(
        functools.partial(norm_back_kernel, final=True),
        bf16,
        (inputs, resid_grad, gain_one, one_grad),
        block // 4,
        last,
    )
    block_out = run_rows(add_kernel, bf16, (hidden, mlp_out), block // 4, last)

    def apart(flat_sum, beside):
        gates_other = sibling(flat_sum[:head])
        blocks = shape((heads, head, head), f32)
        found = run(
            functools.partial(unpack_kernel, heads=heads),
            [blocks, blocks, shape((8, width), f32)],
            (core_id, flat_sum[: head + 16], gates_other),
            after=beside[:1],
            scalar=True,
        )
        gains = flat_sum[head + 8 : head + 24, :256].astype(f32)
        if square:
            for axis, other in zip(("x", "y"), beside, strict=True):
                gains = gains + held((lax.ppermute(gains, axis, swap),), (other,))[0]
        else:
            gains = lax.psum(gains, ("y", "x"))
        return *found, gains

    def whole(own, axis, after=()):
        return joined_halves(own, sibling(own), core_id, axis, after)

    if line:
        output_w_grad = whole(output_sum, 1, (inputs_grad, block_out))
        branch_w_grad = whole(branch_sum, 0, (output_w_grad,))
        down_w_grad = filled(down_w_grad, sibling(down_low), core_id, False, (branch_w_grad,))
        recur_grad, intake_grad, sums, gains = apart(flat_sum, (output_w_grad, branch_w_grad))
        (stream_sum,) = line_settle(moved, (down_w_grad, recur_grad, gains))
        stream_w_grad = whole(stream_sum, 0)
    else:
        output_sum, branch_sum, stream_sum, flat_sum = (
            lax.psum(part, "z") for part in (output_half, branch_half, stream_half, flat)
        )
        recur_grad, intake_grad, sums, gains = apart(flat_sum, (inputs_grad, block_out))
        output_w_grad, branch_w_grad, stream_w_grad = (
            whole(output_sum, 1),
            whole(branch_sum, 0),
            whole(stream_sum, 0),
        )

        def over_rows(left, right):
            part = lax.dot_general(left, right, contract_rows, preferred_element_type=f32)
            return lax.psum(part.astype(bf16), ("z", "core")).astype(f32)

        gate_w_grad = over_rows(mlp_in, kept[0])
        up_w_grad = over_rows(mlp_in, kept[1])
        down_w_grad = over_rows(activ, jnp.concatenate(own_cots, axis=0))

    gains = gains.reshape(2, -1)
    return (
        block_out,
        inputs_grad,
        gains[0],
        branch_w_grad,
        stream_w_grad,
        sums[0:4],
        sums[4],
        recur_grad,
        sums[5],
        intake_grad,
        sums[6],
        sums[7] * decay_scale * jax.nn.sigmoid(-decay_param),
        output_w_grad,
        gains[1],
        gate_w_grad,
        up_w_grad,
        down_w_grad,
    )


def solution(mesh):
    depth = mesh.shape["dp"] // 2
    across = mesh.shape["mp"] // 2
    fine = Mesh(mesh.devices.reshape(depth, 2, 2, across), ALL)
    dp, mp = ("z", "core"), ("y", "x")
    cols, vec, blocks, rows = P(None, mp), P(mp), P(mp, None, None), P(mp, None)
    tokens = P(ALL, None)
    return jax.shard_map(
        functools.partial(local, depth=depth, square=across == 2),
        mesh=fine,
        in_specs=(
            tokens,
            tokens,
            P(dp, None),
            P(),
            cols,
            cols,
            cols,
            vec,
            blocks,
            vec,
            blocks,
            vec,
            vec,
            rows,
            P(),
            cols,
            cols,
            rows,
        ),
        out_specs=(
            tokens,
            tokens,
            P(),
            cols,
            cols,
            cols,
            vec,
            blocks,
            vec,
            blocks,
            vec,
            vec,
            rows,
            P(),
            cols,
            cols,
            rows,
        ),
        check_vma=False,
    )
```
